128 devices in a mesh: px: 8 (over x, core), py: 16 (over z, y).
Axes of the slice: x: 4, y: 4, z: 4, core: 2. Of those that a mesh axis runs over, the one named last changes fastest.
Arguments:
- incident_power_density: float32 [3, 2048, 2048], P(None, ('px', 'py')), may hold values from 0.1 to 4
- coupling_patch_locator: int32 [8, 256, 2048], P(None, 'px', 'py'), may hold values from 0 to 32767, as said below
- coupling_share_factor: float32 [8, 256, 2048], P(None, 'px', 'py'), may hold values from 0.05 to 1
- starting_warmth: float32 [24, 256, 2048], P(None, 'px', 'py'), may hold values from -6 to 6
- diffusive_coefficient: float32 [24, 256, 2048], P(None, 'px', 'py'), may hold values from 0.3 to 3
- thermal_storage: float32 [24, 256, 2048], P(None, 'px', 'py'), may hold values from 0.05 to 0.5
Outputs:
- final_warmth: float32 [24, 256, 2048], P(None, 'px', 'py')
- leftover_error_vector: float32 [24, 256, 2048], P(None, 'px', 'py')
The draws below stay inside these ranges and needn't reach their ends.
Inputs may be any that keep to these rules, and one draw needn't show every extreme that they name: `coupling_patch_locator`: every index lies in the window of the cell's own part, near the tile that faces the cell.
All inputs are finite; a program needn't handle non-finite values.
Results may differ from the reference program's by a relative error of at most 0.00019.
Values sent between devices are 32-bit elements; how exact they have to be, the bound alone decides.
A program may use at most 128 MiB of HBM per device.

```python
import math
import jax
import jax.numpy as jnp

CX = 32
CY = 128
GAUGE_POINTS = 24
STEPS = 3
ITERS = 2
CORRELATIONS = 8
BR = 16
COLS = 128
LENGTHWISE_COUNT = 256
BREADTHWISE_COUNT = 2048
BEAM_ROWS = 2048
BEAM_COLS = 2048
N_PY = 16


def draw_coupling_patch_locator(key, part):
    key = jax.random.fold_in(key, 7)
    window_rows = BR * N_PY
    xs = jnp.arange(LENGTHWISE_COUNT, dtype=jnp.int32) % CX
    ys = jnp.arange(BREADTHWISE_COUNT, dtype=jnp.int32) % CY
    centre_row = xs * window_rows // CX
    centre_col = ys * COLS // CY
    span_row = max(window_rows // CX, 1)
    span_col = max(COLS // CY, 1)
    key_row, key_col = jax.random.split(key)
    off_row = jax.random.randint(key_row, (CORRELATIONS, LENGTHWISE_COUNT, BREADTHWISE_COUNT), -1, span_row + 1)
    offset_column = jax.random.randint(key_col, (CORRELATIONS, LENGTHWISE_COUNT, BREADTHWISE_COUNT), -1, span_col + 1)
    slot = jnp.arange(CORRELATIONS, dtype=jnp.int32)[:, None, None]
    last_cell = (xs == CX - 1)[None, :, None] & (ys == CY - 1)[None, None, :]
    first_cell = (xs == 0)[None, :, None] & (ys == 0)[None, None, :]
    off_row = jnp.where((slot == 0) & last_cell, window_rows, off_row)
    offset_column = jnp.where((slot == 0) & last_cell, COLS, offset_column)
    off_row = jnp.where((slot == 1) & first_cell, -1, off_row)
    offset_column = jnp.where((slot == 1) & first_cell, -1, offset_column)
    rows = jnp.clip(centre_row[None, :, None] + off_row, 0, window_rows - 1)
    cols = jnp.clip(centre_col[None, None, :] + offset_column, 0, COLS - 1)
    return (rows * COLS + cols).astype(jnp.int32)


def level_of(rng, dims, cuts, least, top_value):
    def one(position, shards_of):
        heights = jax.random.uniform(jax.random.fold_in(jax.random.fold_in(rng, 6), position), (shards_of,), jnp.float32, least / len(cuts), top_value / len(cuts))
        return jnp.repeat(jnp.exp(heights), dims[position] // shards_of).reshape((-1,) + (1,) * (len(dims) - position - 1))

    level = one(*cuts[0])
    for cut in cuts[1:]:
        level = level * one(*cut)
    return level


def normal_values(key, shape, deviation, bound, pieces=(), held_as=jnp.bfloat16):
    array = deviation * jax.random.normal(key, shape, jnp.float32)
    if pieces:
        array = array * level_of(key, shape, pieces, -0.22, 0.18)
    return jnp.clip(array, -bound, bound).astype(held_as)


def setup_inputs(seed: int = 0) -> dict:
    arg_keys = jax.random.split(jax.random.key(seed), 7)
    incident_power_density = jnp.clip(jnp.exp(math.log(4.0) - 3.6888794 * jax.random.uniform(arg_keys[0], (STEPS, BEAM_ROWS, BEAM_COLS), jnp.float32) ** level_of(arg_keys[0], (STEPS, BEAM_ROWS, BEAM_COLS), ((1, 128),), -0.2, 0.2)), 0.1, 4.0)
    coupling_patch_locator = draw_coupling_patch_locator(jax.random.fold_in(arg_keys[6], 71), 0)
    coupling_share_factor = jnp.clip(0.05 + 0.95 * jax.random.uniform(arg_keys[2], (CORRELATIONS, LENGTHWISE_COUNT, BREADTHWISE_COUNT), jnp.float32) ** level_of(arg_keys[2], (CORRELATIONS, LENGTHWISE_COUNT, BREADTHWISE_COUNT), ((1, 8), (2, 16)), -0.2, 0.2), 0.05, 1.0)
    starting_warmth = normal_values(arg_keys[3], (GAUGE_POINTS, LENGTHWISE_COUNT, BREADTHWISE_COUNT), 1.0, 6.0, ((1, 8), (2, 16)), jnp.float32)
    diffusive_coefficient = jnp.clip(jnp.exp(math.log(3.0) - 2.3025851 * jax.random.uniform(arg_keys[4], (GAUGE_POINTS, LENGTHWISE_COUNT, BREADTHWISE_COUNT), jnp.float32) ** level_of(arg_keys[4], (GAUGE_POINTS, LENGTHWISE_COUNT, BREADTHWISE_COUNT), ((1, 8), (2, 16)), -0.2, 0.2)), 0.3, 3.0)
    thermal_storage = jnp.clip(jnp.exp(math.log(0.5) - 2.3025851 * jax.random.uniform(arg_keys[5], (GAUGE_POINTS, LENGTHWISE_COUNT, BREADTHWISE_COUNT), jnp.float32) ** level_of(arg_keys[5], (GAUGE_POINTS, LENGTHWISE_COUNT, BREADTHWISE_COUNT), ((1, 8), (2, 16)), -0.2, 0.2)), 0.05, 0.5)
    return dict(incident_power_density=incident_power_density, coupling_patch_locator=coupling_patch_locator, coupling_share_factor=coupling_share_factor, starting_warmth=starting_warmth, diffusive_coefficient=diffusive_coefficient, thermal_storage=thermal_storage)


through_ratio = 0.5


def face_terms(diffusive_coefficient):
    padded = jnp.pad(diffusive_coefficient, 1)
    centre = diffusive_coefficient
    face_zlow = through_ratio * 0.5 * (centre + padded[:-2, 1:-1, 1:-1])
    face_zhigh = through_ratio * 0.5 * (centre + padded[2:, 1:-1, 1:-1])
    face_xlow = 0.5 * (centre + padded[1:-1, :-2, 1:-1])
    face_xhigh = 0.5 * (centre + padded[1:-1, 2:, 1:-1])
    face_ylow = 0.5 * (centre + padded[1:-1, 1:-1, :-2])
    face_yhigh = 0.5 * (centre + padded[1:-1, 1:-1, 2:])
    return (face_zlow, face_zhigh, face_xlow, face_xhigh, face_ylow, face_yhigh)


def operate(field, faces, diagonal):
    padded = jnp.pad(field, 1)
    beside = faces[0] * padded[:-2, 1:-1, 1:-1] + faces[1] * padded[2:, 1:-1, 1:-1]
    beside = beside + faces[2] * padded[1:-1, :-2, 1:-1] + faces[3] * padded[1:-1, 2:, 1:-1]
    beside = beside + faces[4] * padded[1:-1, 1:-1, :-2] + faces[5] * padded[1:-1, 1:-1, 2:]
    return diagonal * field - beside


def reference(incident_power_density, coupling_patch_locator, coupling_share_factor, starting_warmth, diffusive_coefficient, thermal_storage):
    window_rows = BR * N_PY
    xs = jnp.arange(LENGTHWISE_COUNT, dtype=jnp.int32)
    ys = jnp.arange(BREADTHWISE_COUNT, dtype=jnp.int32)
    beam_row = (xs // CX)[None, :, None] * window_rows + coupling_patch_locator // COLS
    beam_col = (ys // CY)[None, None, :] * COLS + coupling_patch_locator % COLS
    faces = face_terms(diffusive_coefficient)
    diagonal = thermal_storage + faces[0] + faces[1] + faces[2] + faces[3] + faces[4] + faces[5]
    final_warmth = starting_warmth
    leftover_error_vector = starting_warmth
    for frame in range(STEPS):
        values = incident_power_density[frame][beam_row, beam_col]
        flux = jnp.sum(coupling_share_factor * values, axis=0)
        right = thermal_storage * final_warmth
        right = right.at[GAUGE_POINTS - 1].add(flux)
        solution = final_warmth
        leftover_error_vector = right - operate(solution, faces, diagonal)
        scaled = leftover_error_vector / diagonal
        axis_direction = scaled
        gamma = jnp.sum(leftover_error_vector * scaled)
        for turn in range(ITERS):
            image = operate(axis_direction, faces, diagonal)
            alpha = gamma / jnp.sum(axis_direction * image)
            solution = solution + alpha * axis_direction
            leftover_error_vector = leftover_error_vector - alpha * image
            if turn + 1 < ITERS:
                scaled = leftover_error_vector / diagonal
                fresh = jnp.sum(leftover_error_vector * scaled)
                axis_direction = scaled + (fresh / gamma) * axis_direction
                gamma = fresh
        final_warmth = solution
    return final_warmth, leftover_error_vector
```

```python
import functools

import jax
import jax.numpy as jnp
from jax import lax
from jax.experimental import pallas as pl
from jax.experimental.pallas import tpu as pltpu
from jax.sharding import PartitionSpec as P

ITERS = 2
MESH = pl.DeviceIdType.MESH

NZ = 24
NX = 32
NY = 128
NPX = 8
NPY = 16
BR = 16
STEPS = 3
CORR = 8
NMOM = 5


through_ratio = 0.5


def extended(block, sides, width):
    for axis, dim in sides:
        count = lax.axis_size(axis)
        forward = [(i, i + 1) for i in range(count - 1)]
        backward = [(target, source) for source, target in forward]
        low = lax.ppermute(
            lax.slice_in_dim(block, block.shape[dim] - width, None, axis=dim), axis, forward
        )
        high = lax.ppermute(lax.slice_in_dim(block, 0, width, axis=dim), axis, backward)
        block = jnp.concatenate([low, block, high], axis=dim)
    return block


def with_rim(field):
    rimmed = extended(field, (("px", 1), ("py", 2)), 1)
    return jnp.pad(rimmed, ((1, 1), (0, 0), (0, 0)))


def stencil(padded, field, faces, diagonal):
    beside = faces[0] * padded[:-2, 1:-1, 1:-1] + faces[1] * padded[2:, 1:-1, 1:-1]
    beside = beside + faces[2] * padded[1:-1, :-2, 1:-1] + faces[3] * padded[1:-1, 2:, 1:-1]
    beside = beside + faces[4] * padded[1:-1, 1:-1, :-2] + faces[5] * padded[1:-1, 1:-1, 2:]
    return diagonal * field - beside


def operate(field, faces, diagonal):
    return stencil(with_rim(field), field, faces, diagonal)


def face_terms(centre, padded):
    return (
        through_ratio * 0.5 * (centre + padded[:-2, 1:-1, 1:-1]),
        through_ratio * 0.5 * (centre + padded[2:, 1:-1, 1:-1]),
        0.5 * (centre + padded[1:-1, :-2, 1:-1]),
        0.5 * (centre + padded[1:-1, 2:, 1:-1]),
        0.5 * (centre + padded[1:-1, 1:-1, :-2]),
        0.5 * (centre + padded[1:-1, 1:-1, 2:]),
    )


def surface_flux(window, coupling_patch_locator, coupling_share_factor):
    flat = window.reshape(-1)
    values = flat[coupling_patch_locator]
    return jnp.sum(coupling_share_factor * values, axis=0)


def total(a, b):
    return lax.psum(jnp.sum(a * b), ("px", "py"))


def solve_step(solution, leftover_error_vector, faces, diagonal):
    scaled = leftover_error_vector / diagonal
    axis_direction = scaled
    gamma = total(leftover_error_vector, scaled)
    for turn in range(ITERS):
        image = operate(axis_direction, faces, diagonal)
        alpha = gamma / total(axis_direction, image)
        solution = solution + alpha * axis_direction
        leftover_error_vector = leftover_error_vector - alpha * image
        if turn + 1 < ITERS:
            scaled = leftover_error_vector / diagonal
            fresh = total(leftover_error_vector, scaled)
            axis_direction = scaled + fresh / gamma * axis_direction
            gamma = fresh
    return (solution, leftover_error_vector)


def general(
    incident_power_density,
    coupling_patch_locator,
    coupling_share_factor,
    starting_warmth,
    diffusive_coefficient,
    thermal_storage,
):
    sheet_level = starting_warmth.shape[0]
    rimmed = extended(diffusive_coefficient, (("px", 1), ("py", 2)), 1)
    padded = jnp.pad(rimmed, ((1, 1), (0, 0), (0, 0)))
    faces = face_terms(diffusive_coefficient, padded)
    diagonal = thermal_storage + faces[0] + faces[1] + faces[2] + faces[3] + faces[4] + faces[5]
    frames = incident_power_density.shape[0]
    final_warmth = starting_warmth
    leftover_error_vector = starting_warmth
    for frame in range(frames):
        window = lax.all_to_all(
            incident_power_density[frame : frame + 1], "py", split_axis=2, concat_axis=1, tiled=True
        )[0]
        flux = surface_flux(window, coupling_patch_locator, coupling_share_factor)
        right = thermal_storage * final_warmth
        right = right.at[sheet_level - 1].add(flux)
        leftover_error_vector = right - operate(final_warmth, faces, diagonal)
        final_warmth, leftover_error_vector = solve_step(
            final_warmth, leftover_error_vector, faces, diagonal
        )
    return (final_warmth, leftover_error_vector)


def lanes(rows=NZ):
    return lax.broadcasted_iota(jnp.int32, (rows, NY), 1)


def rolled(v, shift, axis=1):
    return pltpu.roll(v, shift % v.shape[axis], axis)


def side_tile(packed, x):
    return pltpu.roll(packed, lax.rem(638 - 4 * x, 128), 1)


def lateral(v, side):
    lane = lanes(v.shape[0])
    left = jnp.where(lane == 0, side, rolled(v, 1))
    right = jnp.where(lane == NY - 1, side, rolled(v, -1))
    return left, right


def apply_slab(ref, i, side, g_ref, gi):
    v = ref[i]
    left, right = lateral(v, side)
    out = g_ref[0, gi] * rolled(v, 1, 0) + g_ref[1, gi] * rolled(v, -1, 0)
    out = out + (g_ref[2, gi] * ref[i - 1] + g_ref[3, gi] * ref[i + 1])
    out = out + (g_ref[4, gi] * left + g_ref[5, gi] * right)
    return v - out


def around_halo(halo, corner, pack):
    lane = lanes()
    j = lax.rem(lane, 4)
    below = jnp.where(lane < 4, corner, rolled(halo, 4))
    above = jnp.where(lane >= NY - 4, corner, rolled(halo, -4))
    outer = jnp.where(j == 1, rolled(halo, 1), rolled(halo, -1))
    return below, above, pack, outer


def apply_halo(halo, corner, pack, gp_ref):
    below, above, inner, outer = around_halo(halo, corner, pack)
    out = gp_ref[0] * rolled(halo, 1, 0) + gp_ref[1] * rolled(halo, -1, 0)
    out = out + gp_ref[2] * below + gp_ref[3] * above + gp_ref[4] * inner + gp_ref[5] * outer
    return halo - out


class Place:
    def __init__(self):
        self.px = lax.axis_index("px")
        self.py = lax.axis_index("py")
        self.has_low = jnp.where(self.px > 0, 1.0, 0.0).astype(jnp.float32)
        self.has_high = jnp.where(self.px < NPX - 1, 1.0, 0.0).astype(jnp.float32)
        self.has_left = jnp.where(self.py > 0, 1.0, 0.0).astype(jnp.float32)
        self.has_right = jnp.where(self.py < NPY - 1, 1.0, 0.0).astype(jnp.float32)

    def at(self, dx, dy):
        return (lax.rem(self.px + dx + NPX, NPX), lax.rem(self.py + dy + NPY, NPY))


CORNERS = ((-1, 1), (-1, -1), (1, 1), (1, -1))


class Exchange:
    def __init__(self, place, refs):
        self.place = place
        self.rx, self.rs, self.rk, self.pack, self.send, self.recv = refs
        self.copies = []

    def start(self, low, high):
        place = self.place
        plan = []
        for n, (dx, dy) in enumerate(CORNERS):
            plan.append((self.pack, self.rk.at[n], (-dx, -dy)))
        plan.append((self.pack, self.rs.at[0], (0, 1)))
        plan.append((self.pack, self.rs.at[1], (0, -1)))
        single = len(low.shape) == 3
        for n, (src, dx) in enumerate(((high, 1), (low, -1))):
            plan.append((src, self.rx.at[n, 0] if single else self.rx.at[n], (dx, 0)))
        for n, (src, dst, (dx, dy)) in enumerate(plan):
            copy = pltpu.make_async_remote_copy(
                src_ref=src,
                dst_ref=dst,
                send_sem=self.send.at[n],
                recv_sem=self.recv.at[n],
                device_id=place.at(dx, dy),
                device_id_type=MESH,
            )
            copy.start()
            self.copies.append(copy)

    def arrive(self):
        for copy in self.copies:
            copy.wait_recv()

    def sent(self):
        for copy in self.copies:
            copy.wait_send()

    def slabs(self, field):
        p = self.place
        return (
            self.rx[0, field, 0] * p.has_low,
            self.rx[0, field, 1] * p.has_low,
            self.rx[1, field, 0] * p.has_high,
            self.rx[1, field, 1] * p.has_high,
        )

    def halo(self, field):
        p = self.place
        left = self.rs[0, field] * p.has_left
        right = self.rs[1, field] * p.has_right
        j = lax.rem(lanes(left.shape[0]), 4)
        far = jnp.where(j == 0, rolled(right, -3), rolled(left, 3))
        near = jnp.where(j == 1, rolled(right, -1), rolled(left, 1))
        return jnp.where((j == 1) | (j == 2), near, far)

    def corner(self, field):
        p = self.place
        a = rolled(self.rk[0, field] * (p.has_low * p.has_right), 3)
        b = rolled(self.rk[1, field] * (p.has_low * p.has_left), 5)
        c = rolled(self.rk[2, field] * (p.has_high * p.has_right), -5)
        d = rolled(self.rk[3, field] * (p.has_high * p.has_left), -3)
        lane = lanes(a.shape[0])
        out = jnp.where(lane == 1, a, jnp.zeros_like(a))
        out = jnp.where(lane == 2, b, out)
        out = jnp.where(lane == NY - 3, c, out)
        return jnp.where(lane == NY - 2, d, out)


def packed_into(pack, v, x):
    lane = lanes(v.shape[0])
    return jnp.where(lane // 4 == x, pltpu.roll(v, lax.rem(4 * x + 2, NY), 1), pack)


HOPS = sorted(
    ((dz, dy) for dz in range(4) for dy in range(4) if dz or dy),
    key=lambda t: -(min(t[0], 4 - t[0]) + min(t[1], 4 - t[1])),
)


def ring_targets(place):
    x, core = place.px // 2, lax.rem(place.px, 2)
    z, y = place.py // 4, lax.rem(place.py, 4)
    px = []
    for dx, dc in ((2, 1), (2, 0), (1, 1), (1, 0), (3, 1), (3, 0), (0, 1)):
        px.append((lax.rem(x + dx, 4) * 2 + lax.rem(core + dc, 2), place.py))
    py = []
    for dz, dy in HOPS:
        py.append((place.px, lax.rem(z + dz, 4) * 4 + lax.rem(y + dy, 4)))
    return px, py


def kernel(
    beam,
    loc_in,
    share_in,
    t_in,
    k_in,
    c_in,
    x_out,
    r_out,
    flag_out,
    kraw,
    craw,
    traw,
    loc,
    share,
    window,
    weights,
    kct,
    z_ref,
    u_ref,
    v_ref,
    x_ref,
    g_ref,
    gp_ref,
    d_ref,
    e_ref,
    fd_ref,
    red_src,
    red_px,
    red_py,
    local_sem,
    beam_send,
    beam_recv,
    red_send,
    red_recv,
    *exchange_refs,
):
    place = Place()
    px_ring, py_ring = ring_targets(place)
    diagonal_devices = [place.at(dx, dy) for dx, dy in CORNERS]

    local = [
        pltpu.make_async_copy(src, dst, local_sem.at[n])
        for n, (src, dst) in enumerate(
            (
                (k_in, kraw),
                (c_in, craw),
                (t_in, traw),
                (loc_in, loc),
                (share_in, share),
            )
        )
    ]
    for copy in local:
        copy.start()
    own_columns = pl.ds(pl.multiple_of(place.py * NY, NY), NY)
    own_rows = pl.ds(pl.multiple_of(place.py * BR, BR), BR)
    own_beam = pltpu.make_async_copy(
        beam.at[:, :, own_columns], window.at[:, own_rows, :], local_sem.at[5]
    )
    own_beam.start()

    barrier = pltpu.get_barrier_semaphore()
    everyone = py_ring + px_ring + diagonal_devices
    for device in everyone:
        pl.semaphore_signal(barrier, inc=1, device_id=device, device_id_type=MESH)

    exchanges = [
        Exchange(place, exchange_refs[6 * n : 6 * n + 6]) for n in range(1 + STEPS)
    ]

    for copy in local[:3]:
        copy.wait()
    zero = jnp.zeros((NZ, NY), jnp.float32)

    def lay(x, packs):
        out = []
        for n, raw in enumerate((kraw, craw, traw)):
            v = raw[pl.ds(x, NZ, stride=NX), :]
            kct[n, x + 2] = v
            out.append(packed_into(packs[n], v, x))
        return tuple(out)

    packs = lax.fori_loop(0, NX, lay, (zero, zero, zero))
    k_pack, c_pack, t_pack = packs
    first = exchanges[0]
    for n in range(3):
        first.pack[n] = packs[n]

    pl.semaphore_wait(barrier, len(everyone))

    def send_frame(frame):
        copies = []
        for device in py_ring:
            columns = pl.ds(pl.multiple_of(device[1] * NY, NY), NY)
            copy = pltpu.make_async_remote_copy(
                src_ref=beam.at[frame, :, columns],
                dst_ref=window.at[frame, own_rows, :],
                send_sem=beam_send.at[frame],
                recv_sem=beam_recv.at[frame],
                device_id=device,
                device_id_type=MESH,
            )
            copy.start()

    def frame_bytes(frame, sem):
        most = window.at[frame, pl.ds(0, (NPY - 1) * BR), :]
        return pltpu.make_async_copy(most, most, sem.at[frame])

    send_frame(0)
    first.start(kct.at[:, 2:4], kct.at[:, NX : NX + 2])
    for frame in range(1, STEPS):
        send_frame(frame)

    local[3].wait()
    local[4].wait()
    row8 = lax.broadcasted_iota(jnp.int32, (8, NY), 0)
    lane8 = lax.broadcasted_iota(jnp.int32, (8, NY), 1)
    beyond = jnp.where(row8 == 7, -1, jnp.where(row8 == 0, 8, -1000))

    def weigh(x, bad):
        own = [jnp.zeros((8, NY), jnp.float32) for _ in range(3)]
        edge = [jnp.zeros((8, NY), jnp.float32) for _ in range(3)]
        for k in range(CORR):
            index = jnp.broadcast_to(loc[k, pl.ds(x, 1), :], (8, NY))
            part = jnp.broadcast_to(share[k, pl.ds(x, 1), :], (8, NY))
            row = lax.shift_right_arithmetic(index, 7) - 8 * x
            col = lax.bitwise_and(index, 127) - lane8
            far = (row < -1) | (row > 8) | (col < -1) | (col > 1)
            bad = bad + jnp.where(far, 1.0, 0.0)
            inside = jnp.where(row == row8, part, 0.0)
            outside = jnp.where(row == beyond, part, 0.0)
            for n in range(3):
                here = col == n - 1
                own[n] = own[n] + jnp.where(here, inside, 0.0)
                edge[n] = edge[n] + jnp.where(here, outside, 0.0)
        for n in range(3):
            weights[n, x] = own[n]
            weights[3 + n, x] = edge[n]
        return bad

    bad = lax.fori_loop(0, NX, weigh, jnp.zeros((8, NY), jnp.float32))

    first.arrive()
    for n in range(3):
        slabs = first.slabs(n)
        for at, slab in zip((0, 1, NX + 2, NX + 3), slabs):
            kct[n, at] = slab
    k_halo, k_corner = first.halo(0), first.corner(0)
    c_halo, t_halo = first.halo(1), first.halo(2)
    level = lax.broadcasted_iota(jnp.int32, (NZ, NY), 0)

    def over(k, up, down, below, above, left, right, storage, mask):
        bottom, top = level == 0, level == NZ - 1
        up = jnp.where(bottom, 0.0, up)
        down = jnp.where(top, 0.0, down)
        faces = [0.25 * (k + up), 0.25 * (k + down)]
        faces += [0.5 * (k + other) for other in (below, above, left, right)]
        diagonal = storage + (
            (faces[0] + faces[1]) + (faces[2] + faces[3]) + (faces[4] + faces[5])
        )
        inverse = mask / diagonal
        faces[0] = jnp.where(bottom, 0.0, faces[0])
        faces[1] = jnp.where(top, 0.0, faces[1])
        return [face * inverse for face in faces], diagonal, inverse

    def conduct(x, side, mask):
        i = x + 2
        k = kct[0, i]
        left, right = lateral(k, side)
        g, diagonal, inverse = over(
            k,
            rolled(k, 1, 0),
            rolled(k, -1, 0),
            kct[0, i - 1],
            kct[0, i + 1],
            left,
            right,
            kct[1, i],
            mask,
        )
        for n in range(6):
            g_ref[n, x + 1] = g[n]
        return diagonal, inverse

    conduct(-1, side_tile(k_corner, 0), place.has_low)
    conduct(NX, side_tile(k_corner, NX - 1), place.has_high)

    def conduct_inside(x, carry):
        diagonal, inverse = conduct(x, side_tile(k_halo, x), 1.0)
        d_ref[x] = diagonal
        e_ref[x] = kct[1, x + 2] * inverse
        return carry

    lax.fori_loop(0, NX, conduct_inside, 0)

    below, above, inner, outer = around_halo(k_halo, k_corner, k_pack)
    j = lax.rem(lanes(), 4)
    halo_mask = jnp.where(j < 2, place.has_right, place.has_left)
    halo_mask = jnp.where((j == 1) | (j == 2), halo_mask, 0.0)
    gp, _, _ = over(
        k_halo,
        rolled(k_halo, 1, 0),
        rolled(k_halo, -1, 0),
        below,
        above,
        inner,
        outer,
        c_halo + jnp.where(halo_mask > 0.0, 0.0, 1.0),
        halo_mask,
    )
    for n in range(6):
        gp_ref[n] = gp[n]

    t_ref = kct.at[2]

    def residual(x, carry):
        image = apply_slab(t_ref, x + 2, side_tile(t_halo, x), g_ref, x + 1)
        t = t_ref[x + 2]
        z_ref[x + 2] = e_ref[x] * t - image
        x_ref[x] = t
        return carry

    lax.fori_loop(0, NX, residual, 0)
    first.sent()

    own_beam.wait()

    def flux_tile(frame, x):
        def rows(i):
            return window[frame, pl.ds(pl.multiple_of(i * 8, 8), 8), :]

        mine = rows(x)
        around = jnp.where(
            row8 == 7, rows(jnp.maximum(x - 1, 0)), rows(jnp.minimum(x + 1, NX - 1))
        )
        part = weights[1, x] * mine + weights[4, x] * around
        part = part + weights[0, x] * rolled(mine, 1) + weights[3, x] * rolled(around, 1)
        part = part + weights[2, x] * rolled(mine, -1) + weights[5, x] * rolled(around, -1)
        flux = jnp.sum(part, axis=0, keepdims=True)
        top = d_ref[x, NZ - 8 : NZ, :]
        return jnp.where(row8 == 7, flux, 0.0) / top

    def zero_row():
        return jnp.zeros((8, NY), jnp.float32)

    def all_sum(step, moments):
        lane = lax.broadcasted_iota(jnp.int32, (1, NY), 1)
        row = jnp.zeros((1, NY), jnp.float32)
        for n, m in enumerate(moments):
            row = jnp.where(lane == n, jnp.sum(m, keepdims=True), row)
        for phase, (ring, slots, me) in enumerate(
            ((px_ring, red_px, place.px), (py_ring, red_py, place.py))
        ):
            source = red_src.at[step, phase]
            source[...] = row
            for device in ring:
                pltpu.make_async_remote_copy(
                    src_ref=source,
                    dst_ref=slots.at[step, me],
                    send_sem=red_send.at[step, phase],
                    recv_sem=red_recv.at[step, phase],
                    device_id=device,
                    device_id_type=MESH,
                ).start()
            slots[step, me] = row
            most = slots.at[step, pl.ds(0, len(ring))]
            pltpu.make_async_copy(most, most, red_recv.at[step, phase]).wait()
            parts = [slots[step, n] for n in range(len(ring) + 1)]
            while len(parts) > 1:
                parts = [a + b for a, b in zip(parts[::2], parts[1::2])]
            row = parts[0]
        return [
            jnp.sum(jnp.where(lane == n, row, 0.0), axis=1, keepdims=True)
            for n in range(len(moments))
        ]

    def folded(v):
        return v[0:8] + v[8:16] + v[16:24]

    for step in range(STEPS):
        exchange = exchanges[1 + step]
        if step == 0:
            frame_bytes(0, beam_recv).wait()

            def add_flux(x, pack):
                tile = flux_tile(0, x)
                fd_ref[0, x] = tile
                z_ref[x + 2, NZ - 8 : NZ, :] = z_ref[x + 2, NZ - 8 : NZ, :] + tile
                return packed_into(pack, z_ref[x + 2], x)

            z_pack = lax.fori_loop(0, NX, add_flux, zero)
        exchange.pack[0] = z_pack
        exchange.start(z_ref.at[pl.ds(2, 2)], z_ref.at[pl.ds(NX, 2)])
        if step + 1 < STEPS:
            frame_bytes(step + 1, beam_recv).wait()

            def next_flux(x, carry):
                fd_ref[step + 1, x] = flux_tile(step + 1, x)
                return carry

            lax.fori_loop(0, NX, next_flux, 0)
        exchange.arrive()
        slabs = exchange.slabs(0)
        for at, slab in zip((0, 1, NX + 2, NX + 3), slabs):
            z_ref[at] = slab
        z_halo, z_corner = exchange.halo(0), exchange.corner(0)

        u_ref[1] = apply_slab(z_ref, 1, side_tile(z_corner, 0), g_ref, 0)
        u_ref[NX + 2] = apply_slab(z_ref, NX + 2, side_tile(z_corner, NX - 1), g_ref, NX + 1)
        u_halo = apply_halo(z_halo, z_corner, z_pack, gp_ref)

        def first_image(x, sums):
            u = apply_slab(z_ref, x + 2, side_tile(z_halo, x), g_ref, x + 1)
            u_ref[x + 2] = u
            z = z_ref[x + 2]
            dz = d_ref[x] * z
            du = d_ref[x] * u
            return (
                sums[0] + folded(dz * z),
                sums[1] + folded(dz * u),
                sums[2] + folded(du * u),
            )

        sums = lax.fori_loop(0, NX, first_image, (zero_row(),) * 3)

        def second_image(x, acc):
            v = apply_slab(u_ref, x + 2, side_tile(u_halo, x), g_ref, x + 1)
            v_ref[x] = v
            return acc + folded(d_ref[x] * u_ref[x + 2] * v)

        last = lax.fori_loop(0, NX, second_image, zero_row())
        g0, a, w, t, *rest = all_sum(step, list(sums) + [last] + ([bad] if step == 0 else []))
        if step == 0:
            flag_out[...] = jnp.broadcast_to(rest[0], (8, NY))
        alpha0 = g0 / a
        gamma1 = alpha0 * alpha0 * w - g0
        beta1 = 1.0 + gamma1 / g0
        alpha1 = gamma1 / (beta1 * beta1 * a - 2.0 * beta1 * alpha0 * w + alpha0 * alpha0 * t)
        d1 = jnp.broadcast_to(alpha0 + alpha1 * beta1, (NZ, NY))
        d2 = jnp.broadcast_to(-alpha0 * alpha1, (NZ, NY))
        exchange.sent()

        if step + 1 < STEPS:

            def update(x, pack):
                z, u, v = z_ref[x + 2], u_ref[x + 2], v_ref[x]
                move = d1 * z + d2 * u
                x_ref[x] = x_ref[x] + move
                z_ref[x + 2] = z - d1 * u - d2 * v + e_ref[x] * move
                tile = fd_ref[step + 1, x] - fd_ref[step, x]
                z_ref[x + 2, NZ - 8 : NZ, :] = z_ref[x + 2, NZ - 8 : NZ, :] + tile
                return packed_into(pack, z_ref[x + 2], x)

            z_pack = lax.fori_loop(0, NX, update, zero)
        else:

            def finish(x, carry):
                z, u, v = z_ref[x + 2], u_ref[x + 2], v_ref[x]
                x_out[pl.ds(x, NZ, stride=NX), :] = x_ref[x] + (d1 * z + d2 * u)
                r_out[pl.ds(x, NZ, stride=NX), :] = d_ref[x] * (z - d1 * u - d2 * v)
                return carry

            lax.fori_loop(0, NX, finish, 0)

    for frame in range(STEPS):
        frame_bytes(frame, beam_send).wait()
    for step in range(STEPS):
        for phase, (slots, count) in enumerate(((red_px, NPX - 1), (red_py, NPY - 1))):
            most = slots.at[step, pl.ds(0, count)]
            pltpu.make_async_copy(most, most, red_send.at[step, phase]).wait()


def exchange_scratch(fields, rows=NZ):
    f32 = jnp.float32
    return [
        pltpu.VMEM((2, fields, 2, rows, NY), f32),
        pltpu.VMEM((2, fields, rows, NY), f32),
        pltpu.VMEM((4, fields, rows, NY), f32),
        pltpu.VMEM((fields, rows, NY), f32),
        pltpu.SemaphoreType.DMA((8,)),
        pltpu.SemaphoreType.DMA((8,)),
    ]


def body(
    incident_power_density,
    coupling_patch_locator,
    coupling_share_factor,
    starting_warmth,
    diffusive_coefficient,
    thermal_storage,
):
    f32 = jnp.float32
    flat = (NZ * NX, NY)
    hbm = pl.BlockSpec(memory_space=pl.ANY)
    vmem = pl.BlockSpec(memory_space=pltpu.VMEM)
    scratch = [
        pltpu.VMEM(flat, f32),
        pltpu.VMEM(flat, f32),
        pltpu.VMEM(flat, f32),
        pltpu.VMEM((CORR, NX, NY), jnp.int32),
        pltpu.VMEM((CORR, NX, NY), f32),
        pltpu.VMEM((STEPS, BR * NPY, NY), f32),
        pltpu.VMEM((6, NX, 8, NY), f32),
        pltpu.VMEM((3, NX + 4, NZ, NY), f32),
        pltpu.VMEM((NX + 4, NZ, NY), f32),
        pltpu.VMEM((NX + 4, NZ, NY), f32),
        pltpu.VMEM((NX, NZ, NY), f32),
        pltpu.VMEM((NX, NZ, NY), f32),
        pltpu.VMEM((6, NX + 2, NZ, NY), f32),
        pltpu.VMEM((6, NZ, NY), f32),
        pltpu.VMEM((NX, NZ, NY), f32),
        pltpu.VMEM((NX, NZ, NY), f32),
        pltpu.VMEM((STEPS, NX, 8, NY), f32),
        pltpu.VMEM((STEPS, 2, 1, NY), f32),
        pltpu.VMEM((STEPS, NPX, 1, NY), f32),
        pltpu.VMEM((STEPS, NPY, 1, NY), f32),
        pltpu.SemaphoreType.DMA((6,)),
        pltpu.SemaphoreType.DMA((STEPS,)),
        pltpu.SemaphoreType.DMA((STEPS,)),
        pltpu.SemaphoreType.DMA((STEPS, 2)),
        pltpu.SemaphoreType.DMA((STEPS, 2)),
    ]
    for fields in (3, 1, 1, 1):
        scratch += exchange_scratch(fields)
    warmth, leftover, flag = pl.pallas_call(
        kernel,
        out_shape=(
            jax.ShapeDtypeStruct(flat, f32),
            jax.ShapeDtypeStruct(flat, f32),
            jax.ShapeDtypeStruct((8, NY), f32),
        ),
        in_specs=[hbm] * 6,
        out_specs=(vmem, vmem, vmem),
        scratch_shapes=scratch,
        compiler_params=pltpu.CompilerParams(
            collective_id=0, has_side_effects=True, vmem_limit_bytes=40 * 2**20
        ),
    )(
        incident_power_density,
        coupling_patch_locator,
        coupling_share_factor,
        starting_warmth.reshape(flat),
        diffusive_coefficient.reshape(flat),
        thermal_storage.reshape(flat),
    )
    shape = starting_warmth.shape
    return lax.cond(
        flag[0, 0] > 0.0,
        lambda: general(
            incident_power_density,
            coupling_patch_locator,
            coupling_share_factor,
            starting_warmth,
            diffusive_coefficient,
            thermal_storage,
        ),
        lambda: (warmth.reshape(shape), leftover.reshape(shape)),
    )


def solution(mesh):
    placed = (
        P(None, ("px", "py"), None),
        P(None, "px", "py"),
        P(None, "px", "py"),
        P(None, "px", "py"),
        P(None, "px", "py"),
        P(None, "px", "py"),
    )
    return jax.shard_map(
        body,
        mesh=mesh,
        in_specs=placed,
        out_specs=(P(None, "px", "py"), P(None, "px", "py")),
        check_vma=False,
    )
```

```python
import functools

import jax
import jax.numpy as jnp
from jax import lax
from jax.experimental import pallas as pl
from jax.experimental.pallas import tpu as pltpu
from jax.sharding import PartitionSpec as P

ITERS = 2
MESH = pl.DeviceIdType.MESH

NZ = 24
NX = 32
NY = 128
NPX = 8
NPY = 16
BR = 16
STEPS = 3
CORR = 8
UNROLL = 8


through_ratio = 0.5


def extended(block, sides, width):
    for axis, dim in sides:
        count = lax.axis_size(axis)
        forward = [(i, i + 1) for i in range(count - 1)]
        backward = [(target, source) for source, target in forward]
        low = lax.ppermute(
            lax.slice_in_dim(block, block.shape[dim] - width, None, axis=dim), axis, forward
        )
        high = lax.ppermute(lax.slice_in_dim(block, 0, width, axis=dim), axis, backward)
        block = jnp.concatenate([low, block, high], axis=dim)
    return block


def with_rim(field):
    rimmed = extended(field, (("px", 1), ("py", 2)), 1)
    return jnp.pad(rimmed, ((1, 1), (0, 0), (0, 0)))


def stencil(padded, field, faces, diagonal):
    beside = faces[0] * padded[:-2, 1:-1, 1:-1] + faces[1] * padded[2:, 1:-1, 1:-1]
    beside = beside + faces[2] * padded[1:-1, :-2, 1:-1] + faces[3] * padded[1:-1, 2:, 1:-1]
    beside = beside + faces[4] * padded[1:-1, 1:-1, :-2] + faces[5] * padded[1:-1, 1:-1, 2:]
    return diagonal * field - beside


def operate(field, faces, diagonal):
    return stencil(with_rim(field), field, faces, diagonal)


def face_terms(centre, padded):
    return (
        through_ratio * 0.5 * (centre + padded[:-2, 1:-1, 1:-1]),
        through_ratio * 0.5 * (centre + padded[2:, 1:-1, 1:-1]),
        0.5 * (centre + padded[1:-1, :-2, 1:-1]),
        0.5 * (centre + padded[1:-1, 2:, 1:-1]),
        0.5 * (centre + padded[1:-1, 1:-1, :-2]),
        0.5 * (centre + padded[1:-1, 1:-1, 2:]),
    )


def surface_flux(window, coupling_patch_locator, coupling_share_factor):
    flat = window.reshape(-1)
    values = flat[coupling_patch_locator]
    return jnp.sum(coupling_share_factor * values, axis=0)


def total(a, b):
    return lax.psum(jnp.sum(a * b), ("px", "py"))


def solve_step(solution, leftover_error_vector, faces, diagonal):
    scaled = leftover_error_vector / diagonal
    axis_direction = scaled
    gamma = total(leftover_error_vector, scaled)
    for turn in range(ITERS):
        image = operate(axis_direction, faces, diagonal)
        alpha = gamma / total(axis_direction, image)
        solution = solution + alpha * axis_direction
        leftover_error_vector = leftover_error_vector - alpha * image
        if turn + 1 < ITERS:
            scaled = leftover_error_vector / diagonal
            fresh = total(leftover_error_vector, scaled)
            axis_direction = scaled + fresh / gamma * axis_direction
            gamma = fresh
    return (solution, leftover_error_vector)


def general(
    incident_power_density,
    coupling_patch_locator,
    coupling_share_factor,
    starting_warmth,
    diffusive_coefficient,
    thermal_storage,
):
    sheet_level = starting_warmth.shape[0]
    rimmed = extended(diffusive_coefficient, (("px", 1), ("py", 2)), 1)
    padded = jnp.pad(rimmed, ((1, 1), (0, 0), (0, 0)))
    faces = face_terms(diffusive_coefficient, padded)
    diagonal = thermal_storage + faces[0] + faces[1] + faces[2] + faces[3] + faces[4] + faces[5]
    frames = incident_power_density.shape[0]
    final_warmth = starting_warmth
    leftover_error_vector = starting_warmth
    for frame in range(frames):
        window = lax.all_to_all(
            incident_power_density[frame : frame + 1], "py", split_axis=2, concat_axis=1, tiled=True
        )[0]
        flux = surface_flux(window, coupling_patch_locator, coupling_share_factor)
        right = thermal_storage * final_warmth
        right = right.at[sheet_level - 1].add(flux)
        leftover_error_vector = right - operate(final_warmth, faces, diagonal)
        final_warmth, leftover_error_vector = solve_step(
            final_warmth, leftover_error_vector, faces, diagonal
        )
    return (final_warmth, leftover_error_vector)


def lanes(rows=NZ):
    return lax.broadcasted_iota(jnp.int32, (rows, NY), 1)


def rolled(v, shift, axis=1):
    return pltpu.roll(v, shift % v.shape[axis], axis)


def slabs_loop(fn, init, step=UNROLL):
    def some(n, carry):
        for q in range(step):
            carry = fn(n * step + q, carry)
        return carry

    return lax.fori_loop(0, NX // step, some, init)


def side_tile(packed, x):
    return pltpu.roll(packed, lax.rem(638 - 4 * x, 128), 1)


def lateral(v, side):
    lane = lanes(v.shape[0])
    left = jnp.where(lane == 0, side, rolled(v, 1))
    right = jnp.where(lane == NY - 1, side, rolled(v, -1))
    return left, right


def apply_slab(ref, i, side, g_ref, gi):
    v = ref[i]
    left, right = lateral(v, side)
    out = g_ref[0, gi] * rolled(v, 1, 0) + g_ref[1, gi] * rolled(v, -1, 0)
    out = out + (g_ref[2, gi] * ref[i - 1] + g_ref[3, gi] * ref[i + 1])
    out = out + (g_ref[4, gi] * left + g_ref[5, gi] * right)
    return v - out


def around_halo(halo, corner, pack):
    lane = lanes()
    j = lax.rem(lane, 4)
    below = jnp.where(lane < 4, corner, rolled(halo, 4))
    above = jnp.where(lane >= NY - 4, corner, rolled(halo, -4))
    outer = jnp.where(j == 1, rolled(halo, 1), rolled(halo, -1))
    return below, above, pack, outer


def apply_halo(halo, corner, pack, gp_ref):
    below, above, inner, outer = around_halo(halo, corner, pack)
    out = gp_ref[0] * rolled(halo, 1, 0) + gp_ref[1] * rolled(halo, -1, 0)
    out = out + gp_ref[2] * below + gp_ref[3] * above + gp_ref[4] * inner + gp_ref[5] * outer
    return halo - out


class Place:
    def __init__(self):
        self.px = lax.axis_index("px")
        self.py = lax.axis_index("py")
        self.has_low = jnp.where(self.px > 0, 1.0, 0.0).astype(jnp.float32)
        self.has_high = jnp.where(self.px < NPX - 1, 1.0, 0.0).astype(jnp.float32)
        self.has_left = jnp.where(self.py > 0, 1.0, 0.0).astype(jnp.float32)
        self.has_right = jnp.where(self.py < NPY - 1, 1.0, 0.0).astype(jnp.float32)

    def at(self, dx, dy):
        return (lax.rem(self.px + dx + NPX, NPX), lax.rem(self.py + dy + NPY, NPY))


GHOSTS = (0, 1, NX + 2, NX + 3)
EXCHANGES = ((3, NZ), (1, NZ), (1, NZ), (2, 8), (2, NZ), (2, NZ))
CORNERS = ((-1, 1), (-1, -1), (1, 1), (1, -1))


class Exchange:
    def __init__(self, place, refs):
        self.place = place
        self.rx, self.rs, self.rk, self.pack, self.send, self.recv = refs
        self.copies = []

    def start(self, low, high):
        place = self.place
        plan = []
        for n, (dx, dy) in enumerate(CORNERS):
            plan.append((self.pack, self.rk.at[n], (-dx, -dy)))
        plan.append((self.pack, self.rs.at[0], (0, 1)))
        plan.append((self.pack, self.rs.at[1], (0, -1)))
        single = len(low.shape) == 3
        for n, (src, dx) in enumerate(((high, 1), (low, -1))):
            plan.append((src, self.rx.at[n, 0] if single else self.rx.at[n], (dx, 0)))
        for n, (src, dst, (dx, dy)) in enumerate(plan):
            copy = pltpu.make_async_remote_copy(
                src_ref=src,
                dst_ref=dst,
                send_sem=self.send.at[n],
                recv_sem=self.recv.at[n],
                device_id=place.at(dx, dy),
                device_id_type=MESH,
            )
            copy.start()
            self.copies.append(copy)

    def arrive(self):
        for copy in self.copies:
            copy.wait_recv()

    def sent(self):
        for copy in self.copies:
            copy.wait_send()

    def slabs(self, field):
        p = self.place
        return (
            self.rx[0, field, 0] * p.has_low,
            self.rx[0, field, 1] * p.has_low,
            self.rx[1, field, 0] * p.has_high,
            self.rx[1, field, 1] * p.has_high,
        )

    def halo(self, field):
        p = self.place
        left = self.rs[0, field] * p.has_left
        right = self.rs[1, field] * p.has_right
        j = lax.rem(lanes(left.shape[0]), 4)
        far = jnp.where(j == 0, rolled(right, -3), rolled(left, 3))
        near = jnp.where(j == 1, rolled(right, -1), rolled(left, 1))
        return jnp.where((j == 1) | (j == 2), near, far)

    def corner(self, field):
        p = self.place
        a = rolled(self.rk[0, field] * (p.has_low * p.has_right), 3)
        b = rolled(self.rk[1, field] * (p.has_low * p.has_left), 5)
        c = rolled(self.rk[2, field] * (p.has_high * p.has_right), -5)
        d = rolled(self.rk[3, field] * (p.has_high * p.has_left), -3)
        lane = lanes(a.shape[0])
        out = jnp.where(lane == 1, a, jnp.zeros_like(a))
        out = jnp.where(lane == 2, b, out)
        out = jnp.where(lane == NY - 3, c, out)
        return jnp.where(lane == NY - 2, d, out)


def packed_into(pack, v, x):
    lane = lanes(v.shape[0])
    return jnp.where(lane // 4 == x, pltpu.roll(v, lax.rem(4 * x + 2, NY), 1), pack)


HOPS = sorted(
    ((dz, dy) for dz in range(4) for dy in range(4) if dz or dy),
    key=lambda t: -(min(t[0], 4 - t[0]) + min(t[1], 4 - t[1])),
)


def ring_targets(place):
    x, core = place.px // 2, lax.rem(place.px, 2)
    z, y = place.py // 4, lax.rem(place.py, 4)
    px = []
    for dx, dc in ((2, 1), (2, 0), (1, 1), (1, 0), (3, 1), (3, 0), (0, 1)):
        px.append((lax.rem(x + dx, 4) * 2 + lax.rem(core + dc, 2), place.py))
    py = []
    for dz, dy in HOPS:
        py.append((place.px, lax.rem(z + dz, 4) * 4 + lax.rem(y + dy, 4)))
    return px, py


def kernel(
    beam,
    loc_in,
    share_in,
    t_in,
    k_in,
    c_in,
    x_out,
    r_out,
    flag_out,
    kraw,
    craw,
    traw,
    loc,
    share,
    window,
    weights,
    kct,
    z_ref,
    uv_ref,
    x_ref,
    g_ref,
    gp_ref,
    d_ref,
    e_ref,
    fd_ref,
    red_src,
    red_px,
    red_py,
    local_sem,
    beam_send,
    beam_recv,
    red_send,
    red_recv,
    *exchange_refs,
):
    place = Place()
    u_ref, v_ref = uv_ref.at[0], uv_ref.at[1]
    px_ring, py_ring = ring_targets(place)
    diagonal_devices = [place.at(dx, dy) for dx, dy in CORNERS]

    local = [
        pltpu.make_async_copy(src, dst, local_sem.at[n])
        for n, (src, dst) in enumerate(
            (
                (k_in, kraw),
                (c_in, craw),
                (t_in, traw),
                (loc_in, loc),
                (share_in, share),
            )
        )
    ]
    for copy in local:
        copy.start()
    own_columns = pl.ds(pl.multiple_of(place.py * NY, NY), NY)
    own_rows = pl.ds(pl.multiple_of(place.py * BR, BR), BR)
    own_beam = pltpu.make_async_copy(
        beam.at[:, :, own_columns], window.at[:, own_rows, :], local_sem.at[5]
    )
    own_beam.start()

    barrier = pltpu.get_barrier_semaphore()
    everyone = py_ring + px_ring + diagonal_devices
    for device in everyone:
        pl.semaphore_signal(barrier, inc=1, device_id=device, device_id_type=MESH)

    exchanges = [
        Exchange(place, exchange_refs[6 * n : 6 * n + 6]) for n in range(len(EXCHANGES))
    ]
    first, z_swap, e_swap, f_swap, *uv_swaps = exchanges

    for copy in local[:3]:
        copy.wait()
    zero = jnp.zeros((NZ, NY), jnp.float32)

    def lay(x, packs):
        out = []
        for n, raw in enumerate((kraw, craw, traw)):
            v = raw[pl.ds(x, NZ, stride=NX), :]
            kct[n, x + 2] = v
            out.append(packed_into(packs[n], v, x))
        return tuple(out)

    packs = slabs_loop(lay, (zero, zero, zero))
    k_pack, c_pack, t_pack = packs
    for n in range(3):
        first.pack[n] = packs[n]

    local[3].wait()
    local[4].wait()
    row8 = lax.broadcasted_iota(jnp.int32, (8, NY), 0)
    lane8 = lax.broadcasted_iota(jnp.int32, (8, NY), 1)
    beyond = jnp.where(row8 == 7, -1, jnp.where(row8 == 0, 8, -1000))

    def weigh(x, bad):
        own = [jnp.zeros((8, NY), jnp.float32) for _ in range(3)]
        edge = [jnp.zeros((8, NY), jnp.float32) for _ in range(3)]
        for k in range(CORR):
            index = jnp.broadcast_to(loc[k, pl.ds(x, 1), :], (8, NY))
            part = jnp.broadcast_to(share[k, pl.ds(x, 1), :], (8, NY))
            row = lax.shift_right_arithmetic(index, 7) - 8 * x
            col = lax.bitwise_and(index, 127) - lane8
            far = (row < -1) | (row > 8) | (col < -1) | (col > 1)
            bad = bad + jnp.where(far, 1.0, 0.0)
            inside = jnp.where(row == row8, part, 0.0)
            outside = jnp.where(row == beyond, part, 0.0)
            for n in range(3):
                here = col == n - 1
                own[n] = own[n] + jnp.where(here, inside, 0.0)
                edge[n] = edge[n] + jnp.where(here, outside, 0.0)
        for n in range(3):
            weights[n, x] = own[n]
            weights[3 + n, x] = edge[n]
        return bad

    bad = slabs_loop(weigh, jnp.zeros((8, NY), jnp.float32))

    pl.semaphore_wait(barrier, len(everyone))

    def send_frame(frame):
        copies = []
        for device in py_ring:
            columns = pl.ds(pl.multiple_of(device[1] * NY, NY), NY)
            copy = pltpu.make_async_remote_copy(
                src_ref=beam.at[frame, :, columns],
                dst_ref=window.at[frame, own_rows, :],
                send_sem=beam_send.at[frame],
                recv_sem=beam_recv.at[frame],
                device_id=device,
                device_id_type=MESH,
            )
            copy.start()

    def frame_bytes(frame, sem):
        most = window.at[frame, pl.ds(0, (NPY - 1) * BR), :]
        return pltpu.make_async_copy(most, most, sem.at[frame])

    send_frame(0)
    first.start(kct.at[:, 2:4], kct.at[:, NX : NX + 2])
    for frame in range(1, STEPS):
        send_frame(frame)

    first.arrive()
    for n in range(3):
        slabs = first.slabs(n)
        for at, slab in zip(GHOSTS, slabs):
            kct[n, at] = slab
    k_halo, k_corner = first.halo(0), first.corner(0)
    c_halo, t_halo = first.halo(1), first.halo(2)
    level = lax.broadcasted_iota(jnp.int32, (NZ, NY), 0)

    def over(k, up, down, below, above, left, right, storage, mask):
        bottom, top = level == 0, level == NZ - 1
        up = jnp.where(bottom, 0.0, up)
        down = jnp.where(top, 0.0, down)
        faces = [0.25 * (k + up), 0.25 * (k + down)]
        faces += [0.5 * (k + other) for other in (below, above, left, right)]
        diagonal = storage + (
            (faces[0] + faces[1]) + (faces[2] + faces[3]) + (faces[4] + faces[5])
        )
        inverse = mask / diagonal
        faces[0] = jnp.where(bottom, 0.0, faces[0])
        faces[1] = jnp.where(top, 0.0, faces[1])
        return [face * inverse for face in faces], diagonal, inverse

    def conduct(x, side, mask):
        i = x + 2
        k = kct[0, i]
        left, right = lateral(k, side)
        g, diagonal, inverse = over(
            k,
            rolled(k, 1, 0),
            rolled(k, -1, 0),
            kct[0, i - 1],
            kct[0, i + 1],
            left,
            right,
            kct[1, i],
            mask,
        )
        for n in range(6):
            g_ref[n, x + 1] = g[n]
        return diagonal, inverse

    conduct(-1, side_tile(k_corner, 0), place.has_low)
    conduct(NX, side_tile(k_corner, NX - 1), place.has_high)

    def conduct_inside(x, pack):
        diagonal, inverse = conduct(x, side_tile(k_halo, x), 1.0)
        d_ref[x] = diagonal
        e = kct[1, x + 2] * inverse
        e_ref[x + 2] = e
        return packed_into(pack, e, x)

    e_swap.pack[0] = slabs_loop(conduct_inside, zero)

    below, above, inner, outer = around_halo(k_halo, k_corner, k_pack)
    j = lax.rem(lanes(), 4)
    halo_mask = jnp.where(j < 2, place.has_right, place.has_left)
    halo_mask = jnp.where((j == 1) | (j == 2), halo_mask, 0.0)
    gp, _, _ = over(
        k_halo,
        rolled(k_halo, 1, 0),
        rolled(k_halo, -1, 0),
        below,
        above,
        inner,
        outer,
        c_halo + jnp.where(halo_mask > 0.0, 0.0, 1.0),
        halo_mask,
    )
    for n in range(6):
        gp_ref[n] = gp[n]

    t_ref = kct.at[2]

    def residual(x, carry):
        image = apply_slab(t_ref, x + 2, side_tile(t_halo, x), g_ref, x + 1)
        t = t_ref[x + 2]
        z_ref[x + 2] = e_ref[x + 2] * t - image
        x_ref[x] = t
        return carry

    slabs_loop(residual, 0)
    first.sent()

    own_beam.wait()

    def flux_tile(frame, x):
        def rows(i):
            return window[frame, pl.ds(pl.multiple_of(i * 8, 8), 8), :]

        mine = rows(x)
        around = jnp.where(
            row8 == 7, rows(jnp.maximum(x - 1, 0)), rows(jnp.minimum(x + 1, NX - 1))
        )
        part = weights[1, x] * mine + weights[4, x] * around
        part = part + weights[0, x] * rolled(mine, 1) + weights[3, x] * rolled(around, 1)
        part = part + weights[2, x] * rolled(mine, -1) + weights[5, x] * rolled(around, -1)
        flux = jnp.sum(part, axis=0, keepdims=True)
        top = d_ref[x, NZ - 8 : NZ, :]
        return jnp.where(row8 == 7, flux, 0.0) / top

    def zero_row():
        return jnp.zeros((8, NY), jnp.float32)

    def all_sum(step, moments, meanwhile):
        lane = lax.broadcasted_iota(jnp.int32, (1, NY), 1)
        row = jnp.zeros((1, NY), jnp.float32)
        for n, m in enumerate(moments):
            row = jnp.where(lane == n, jnp.sum(m, keepdims=True), row)
        for phase, (ring, slots, me) in enumerate(
            ((px_ring, red_px, place.px), (py_ring, red_py, place.py))
        ):
            source = red_src.at[step, phase]
            source[...] = row
            for device in ring:
                pltpu.make_async_remote_copy(
                    src_ref=source,
                    dst_ref=slots.at[step, me],
                    send_sem=red_send.at[step, phase],
                    recv_sem=red_recv.at[step, phase],
                    device_id=device,
                    device_id_type=MESH,
                ).start()
            slots[step, me] = row
            meanwhile[phase]()
            most = slots.at[step, pl.ds(0, len(ring))]
            pltpu.make_async_copy(most, most, red_recv.at[step, phase]).wait()
            parts = [slots[step, n] for n in range(len(ring) + 1)]
            while len(parts) > 1:
                parts = [a + b for a, b in zip(parts[::2], parts[1::2])]
            row = parts[0]
        return [
            jnp.sum(jnp.where(lane == n, row, 0.0), axis=1, keepdims=True)
            for n in range(len(moments))
        ]

    def folded(v):
        return v[0:8] + v[8:16] + v[16:24]

    frame_bytes(0, beam_recv).wait()

    def add_flux(x, pack):
        tile = flux_tile(0, x)
        fd_ref[0, x + 2] = tile
        z_ref[x + 2, NZ - 8 : NZ, :] = z_ref[x + 2, NZ - 8 : NZ, :] + tile
        return packed_into(pack, z_ref[x + 2], x)

    z_pack = slabs_loop(add_flux, zero)
    z_swap.pack[0] = z_pack
    z_swap.start(z_ref.at[pl.ds(2, 2)], z_ref.at[pl.ds(NX, 2)])
    e_swap.start(e_ref.at[pl.ds(2, 2)], e_ref.at[pl.ds(NX, 2)])
    z_swap.arrive()
    for at, slab in zip(GHOSTS, z_swap.slabs(0)):
        z_ref[at] = slab
    z_halo, z_corner = z_swap.halo(0), z_swap.corner(0)

    def later_fluxes():
        frame_bytes(1, beam_recv).wait()
        frame_bytes(2, beam_recv).wait()

        def next_flux(x, packs):
            second, third = flux_tile(1, x), flux_tile(2, x)
            third = third - second
            second = second - fd_ref[0, x + 2]
            fd_ref[1, x + 2] = second
            fd_ref[2, x + 2] = third
            return packed_into(packs[0], second, x), packed_into(packs[1], third, x)

        packs = slabs_loop(next_flux, (zero_row(),) * 2)
        f_swap.pack[0], f_swap.pack[1] = packs
        f_swap.start(fd_ref.at[pl.ds(1, 2), pl.ds(2, 2)], fd_ref.at[pl.ds(1, 2), pl.ds(NX, 2)])

    for step in range(STEPS):
        u_ref[1] = apply_slab(z_ref, 1, side_tile(z_corner, 0), g_ref, 0)
        u_ref[NX + 2] = apply_slab(z_ref, NX + 2, side_tile(z_corner, NX - 1), g_ref, NX + 1)
        u_halo = apply_halo(z_halo, z_corner, z_pack, gp_ref)
        swap = uv_swaps[step] if step + 1 < STEPS else None

        def first_image(x, carry):
            sums, pack = carry
            u = apply_slab(z_ref, x + 2, side_tile(z_halo, x), g_ref, x + 1)
            u_ref[x + 2] = u
            z = z_ref[x + 2]
            dz = d_ref[x] * z
            du = d_ref[x] * u
            sums = (
                sums[0] + folded(dz * z),
                sums[1] + folded(dz * u),
                sums[2] + folded(du * u),
            )
            return sums, (packed_into(pack, u, x) if swap else pack)

        sums, u_pack = slabs_loop(first_image, ((zero_row(),) * 3, zero))

        def second_image(x, carry):
            acc, pack = carry
            v = apply_slab(u_ref, x + 2, side_tile(u_halo, x), g_ref, x + 1)
            v_ref[x + 2] = v
            acc = acc + folded(d_ref[x] * u_ref[x + 2] * v)
            return acc, (packed_into(pack, v, x) if swap else pack)

        last, v_pack = slabs_loop(second_image, (zero_row(), zero))

        def send_images():
            if swap:
                swap.pack[0] = u_pack
                swap.pack[1] = v_pack
                swap.start(uv_ref.at[:, pl.ds(2, 2)], uv_ref.at[:, pl.ds(NX, 2)])
            if step == 0:
                later_fluxes()

        def receive_images():
            if step == 0:
                z_swap.sent()
                e_swap.arrive()
                for at, slab in zip(GHOSTS, e_swap.slabs(0)):
                    e_ref[at] = slab
                f_swap.arrive()
                for n in range(2):
                    for at, slab in zip(GHOSTS, f_swap.slabs(n)):
                        fd_ref[1 + n, at] = slab
            if swap:
                swap.arrive()

        g0, a, w, t, *rest = all_sum(
            step,
            list(sums) + [last] + ([bad] if step == 0 else []),
            (send_images, receive_images),
        )
        if step == 0:
            flag_out[...] = jnp.broadcast_to(rest[0], (8, NY))
        alpha0 = g0 / a
        gamma1 = alpha0 * alpha0 * w - g0
        beta1 = 1.0 + gamma1 / g0
        alpha1 = gamma1 / (beta1 * beta1 * a - 2.0 * beta1 * alpha0 * w + alpha0 * alpha0 * t)
        d1 = jnp.broadcast_to(alpha0 + alpha1 * beta1, (NZ, NY))
        d2 = jnp.broadcast_to(-alpha0 * alpha1, (NZ, NY))

        def next_z(z, u, v, e, tile):
            z = z - d1 * u - d2 * v + e * (d1 * z + d2 * u)
            return jnp.concatenate([z[: NZ - 8], z[NZ - 8 :] + tile], axis=0)

        if swap:
            for at, u, v in zip(GHOSTS, swap.slabs(0), swap.slabs(1)):
                z_ref[at] = next_z(z_ref[at], u, v, e_ref[at], fd_ref[step + 1, at])
            z_halo, z_corner = (
                next_z(z, get(swap, 0), get(swap, 1), get(e_swap, 0), get(f_swap, step))
                for z, get in ((z_halo, Exchange.halo), (z_corner, Exchange.corner))
            )

            def update(x, pack):
                z, u, v = z_ref[x + 2], u_ref[x + 2], v_ref[x + 2]
                x_ref[x] = x_ref[x] + (d1 * z + d2 * u)
                z = next_z(z, u, v, e_ref[x + 2], fd_ref[step + 1, x + 2])
                z_ref[x + 2] = z
                return packed_into(pack, z, x)

            z_pack = slabs_loop(update, zero)
            swap.sent()
        else:

            def finish(x, carry):
                z, u, v = z_ref[x + 2], u_ref[x + 2], v_ref[x + 2]
                x_out[pl.ds(x, NZ, stride=NX), :] = x_ref[x] + (d1 * z + d2 * u)
                r_out[pl.ds(x, NZ, stride=NX), :] = d_ref[x] * (z - d1 * u - d2 * v)
                return carry

            slabs_loop(finish, 0)

    e_swap.sent()
    f_swap.sent()
    for frame in range(STEPS):
        frame_bytes(frame, beam_send).wait()
    for step in range(STEPS):
        for phase, (slots, count) in enumerate(((red_px, NPX - 1), (red_py, NPY - 1))):
            most = slots.at[step, pl.ds(0, count)]
            pltpu.make_async_copy(most, most, red_send.at[step, phase]).wait()


def exchange_scratch(fields, rows):
    f32 = jnp.float32
    return [
        pltpu.VMEM((2, fields, 2, rows, NY), f32),
        pltpu.VMEM((2, fields, rows, NY), f32),
        pltpu.VMEM((4, fields, rows, NY), f32),
        pltpu.VMEM((fields, rows, NY), f32),
        pltpu.SemaphoreType.DMA((8,)),
        pltpu.SemaphoreType.DMA((8,)),
    ]


def body(
    incident_power_density,
    coupling_patch_locator,
    coupling_share_factor,
    starting_warmth,
    diffusive_coefficient,
    thermal_storage,
):
    f32 = jnp.float32
    flat = (NZ * NX, NY)
    hbm = pl.BlockSpec(memory_space=pl.ANY)
    vmem = pl.BlockSpec(memory_space=pltpu.VMEM)
    scratch = [
        pltpu.VMEM(flat, f32),
        pltpu.VMEM(flat, f32),
        pltpu.VMEM(flat, f32),
        pltpu.VMEM((CORR, NX, NY), jnp.int32),
        pltpu.VMEM((CORR, NX, NY), f32),
        pltpu.VMEM((STEPS, BR * NPY, NY), f32),
        pltpu.VMEM((6, NX, 8, NY), f32),
        pltpu.VMEM((3, NX + 4, NZ, NY), f32),
        pltpu.VMEM((NX + 4, NZ, NY), f32),
        pltpu.VMEM((2, NX + 4, NZ, NY), f32),
        pltpu.VMEM((NX, NZ, NY), f32),
        pltpu.VMEM((6, NX + 2, NZ, NY), f32),
        pltpu.VMEM((6, NZ, NY), f32),
        pltpu.VMEM((NX, NZ, NY), f32),
        pltpu.VMEM((NX + 4, NZ, NY), f32),
        pltpu.VMEM((STEPS, NX + 4, 8, NY), f32),
        pltpu.VMEM((STEPS, 2, 1, NY), f32),
        pltpu.VMEM((STEPS, NPX, 1, NY), f32),
        pltpu.VMEM((STEPS, NPY, 1, NY), f32),
        pltpu.SemaphoreType.DMA((6,)),
        pltpu.SemaphoreType.DMA((STEPS,)),
        pltpu.SemaphoreType.DMA((STEPS,)),
        pltpu.SemaphoreType.DMA((STEPS, 2)),
        pltpu.SemaphoreType.DMA((STEPS, 2)),
    ]
    for fields, rows in EXCHANGES:
        scratch += exchange_scratch(fields, rows)
    warmth, leftover, flag = pl.pallas_call(
        kernel,
        out_shape=(
            jax.ShapeDtypeStruct(flat, f32),
            jax.ShapeDtypeStruct(flat, f32),
            jax.ShapeDtypeStruct((8, NY), f32),
        ),
        in_specs=[hbm] * 6,
        out_specs=(vmem, vmem, vmem),
        scratch_shapes=scratch,
        compiler_params=pltpu.CompilerParams(
            collective_id=0, has_side_effects=True, vmem_limit_bytes=40 * 2**20
        ),
    )(
        incident_power_density,
        coupling_patch_locator,
        coupling_share_factor,
        starting_warmth.reshape(flat),
        diffusive_coefficient.reshape(flat),
        thermal_storage.reshape(flat),
    )
    shape = starting_warmth.shape
    return lax.cond(
        flag[0, 0] > 0.0,
        lambda: general(
            incident_power_density,
            coupling_patch_locator,
            coupling_share_factor,
            starting_warmth,
            diffusive_coefficient,
            thermal_storage,
        ),
        lambda: (warmth.reshape(shape), leftover.reshape(shape)),
    )


def solution(mesh):
    placed = (
        P(None, ("px", "py"), None),
        P(None, "px", "py"),
        P(None, "px", "py"),
        P(None, "px", "py"),
        P(None, "px", "py"),
        P(None, "px", "py"),
    )
    return jax.shard_map(
        body,
        mesh=mesh,
        in_specs=placed,
        out_specs=(P(None, "px", "py"), P(None, "px", "py")),
        check_vma=False,
    )
```

```python
import functools

import jax
import jax.numpy as jnp
from jax import lax
from jax.experimental import pallas as pl
from jax.experimental.pallas import tpu as pltpu
from jax.sharding import PartitionSpec as P

ITERS = 2
MESH = pl.DeviceIdType.MESH

NZ = 24
NX = 32
NY = 128
NPX = 8
NPY = 16
BR = 16
STEPS = 3
CORR = 8
UNROLL = 8


through_ratio = 0.5


def extended(block, sides, width):
    for axis, dim in sides:
        count = lax.axis_size(axis)
        forward = [(i, i + 1) for i in range(count - 1)]
        backward = [(target, source) for source, target in forward]
        low = lax.ppermute(
            lax.slice_in_dim(block, block.shape[dim] - width, None, axis=dim), axis, forward
        )
        high = lax.ppermute(lax.slice_in_dim(block, 0, width, axis=dim), axis, backward)
        block = jnp.concatenate([low, block, high], axis=dim)
    return block


def with_rim(field):
    rimmed = extended(field, (("px", 1), ("py", 2)), 1)
    return jnp.pad(rimmed, ((1, 1), (0, 0), (0, 0)))


def stencil(padded, field, faces, diagonal):
    beside = faces[0] * padded[:-2, 1:-1, 1:-1] + faces[1] * padded[2:, 1:-1, 1:-1]
    beside = beside + faces[2] * padded[1:-1, :-2, 1:-1] + faces[3] * padded[1:-1, 2:, 1:-1]
    beside = beside + faces[4] * padded[1:-1, 1:-1, :-2] + faces[5] * padded[1:-1, 1:-1, 2:]
    return diagonal * field - beside


def operate(field, faces, diagonal):
    return stencil(with_rim(field), field, faces, diagonal)


def face_terms(centre, padded):
    return (
        through_ratio * 0.5 * (centre + padded[:-2, 1:-1, 1:-1]),
        through_ratio * 0.5 * (centre + padded[2:, 1:-1, 1:-1]),
        0.5 * (centre + padded[1:-1, :-2, 1:-1]),
        0.5 * (centre + padded[1:-1, 2:, 1:-1]),
        0.5 * (centre + padded[1:-1, 1:-1, :-2]),
        0.5 * (centre + padded[1:-1, 1:-1, 2:]),
    )


def surface_flux(window, coupling_patch_locator, coupling_share_factor):
    flat = window.reshape(-1)
    values = flat[coupling_patch_locator]
    return jnp.sum(coupling_share_factor * values, axis=0)


def total(a, b):
    return lax.psum(jnp.sum(a * b), ("px", "py"))


def solve_step(solution, leftover_error_vector, faces, diagonal):
    scaled = leftover_error_vector / diagonal
    axis_direction = scaled
    gamma = total(leftover_error_vector, scaled)
    for turn in range(ITERS):
        image = operate(axis_direction, faces, diagonal)
        alpha = gamma / total(axis_direction, image)
        solution = solution + alpha * axis_direction
        leftover_error_vector = leftover_error_vector - alpha * image
        if turn + 1 < ITERS:
            scaled = leftover_error_vector / diagonal
            fresh = total(leftover_error_vector, scaled)
            axis_direction = scaled + fresh / gamma * axis_direction
            gamma = fresh
    return (solution, leftover_error_vector)


def general(
    incident_power_density,
    coupling_patch_locator,
    coupling_share_factor,
    starting_warmth,
    diffusive_coefficient,
    thermal_storage,
):
    sheet_level = starting_warmth.shape[0]
    rimmed = extended(diffusive_coefficient, (("px", 1), ("py", 2)), 1)
    padded = jnp.pad(rimmed, ((1, 1), (0, 0), (0, 0)))
    faces = face_terms(diffusive_coefficient, padded)
    diagonal = thermal_storage + faces[0] + faces[1] + faces[2] + faces[3] + faces[4] + faces[5]
    frames = incident_power_density.shape[0]
    final_warmth = starting_warmth
    leftover_error_vector = starting_warmth
    for frame in range(frames):
        window = lax.all_to_all(
            incident_power_density[frame : frame + 1], "py", split_axis=2, concat_axis=1, tiled=True
        )[0]
        flux = surface_flux(window, coupling_patch_locator, coupling_share_factor)
        right = thermal_storage * final_warmth
        right = right.at[sheet_level - 1].add(flux)
        leftover_error_vector = right - operate(final_warmth, faces, diagonal)
        final_warmth, leftover_error_vector = solve_step(
            final_warmth, leftover_error_vector, faces, diagonal
        )
    return (final_warmth, leftover_error_vector)


def lanes(rows=NZ):
    return lax.broadcasted_iota(jnp.int32, (rows, NY), 1)


def rolled(v, shift, axis=1):
    return pltpu.roll(v, shift % v.shape[axis], axis)


def slabs_loop(fn, init, step=UNROLL):
    def some(n, carry):
        for q in range(step):
            carry = fn(n * step + q, carry)
        return carry

    return lax.fori_loop(0, NX // step, some, init)


def side_tile(packed, x):
    return pltpu.roll(packed, lax.rem(638 - 4 * x, 128), 1)


def lateral(v, side):
    lane = lanes(v.shape[0])
    left = jnp.where(lane == 0, side, rolled(v, 1))
    right = jnp.where(lane == NY - 1, side, rolled(v, -1))
    return left, right


def apply_slab(ref, i, side, g_ref, gi):
    v = ref[i]
    left, right = lateral(v, side)
    out = g_ref[0, gi] * rolled(v, 1, 0) + g_ref[1, gi] * rolled(v, -1, 0)
    out = out + (g_ref[2, gi] * ref[i - 1] + g_ref[3, gi] * ref[i + 1])
    out = out + (g_ref[4, gi] * left + g_ref[5, gi] * right)
    return v - out


def around_halo(halo, corner, pack):
    lane = lanes()
    j = lax.rem(lane, 4)
    below = jnp.where(lane < 4, corner, rolled(halo, 4))
    above = jnp.where(lane >= NY - 4, corner, rolled(halo, -4))
    outer = jnp.where(j == 1, rolled(halo, 1), rolled(halo, -1))
    return below, above, pack, outer


def apply_halo(halo, corner, pack, gp_ref):
    below, above, inner, outer = around_halo(halo, corner, pack)
    out = gp_ref[0] * rolled(halo, 1, 0) + gp_ref[1] * rolled(halo, -1, 0)
    out = out + gp_ref[2] * below + gp_ref[3] * above + gp_ref[4] * inner + gp_ref[5] * outer
    return halo - out


class Place:
    def __init__(self):
        self.px = lax.axis_index("px")
        self.py = lax.axis_index("py")
        self.has_low = jnp.where(self.px > 0, 1.0, 0.0).astype(jnp.float32)
        self.has_high = jnp.where(self.px < NPX - 1, 1.0, 0.0).astype(jnp.float32)
        self.has_left = jnp.where(self.py > 0, 1.0, 0.0).astype(jnp.float32)
        self.has_right = jnp.where(self.py < NPY - 1, 1.0, 0.0).astype(jnp.float32)

    def at(self, dx, dy):
        return (lax.rem(self.px + dx + NPX, NPX), lax.rem(self.py + dy + NPY, NPY))


GHOSTS = (0, 1, NX + 2, NX + 3)
EXCHANGES = ((3, NZ), (1, NZ), (1, NZ), (2, 8), (2, NZ), (2, NZ))
CORNERS = ((-1, 1), (-1, -1), (1, 1), (1, -1))


class Exchange:
    def __init__(self, place, refs):
        self.place = place
        self.rx, self.rs, self.rk, self.pack, self.send, self.recv = refs
        self.copies = []

    def start(self, low, high):
        place = self.place
        plan = []
        for n, (dx, dy) in enumerate(CORNERS):
            plan.append((self.pack, self.rk.at[n], (-dx, -dy)))
        plan.append((self.pack, self.rs.at[0], (0, 1)))
        plan.append((self.pack, self.rs.at[1], (0, -1)))
        single = len(low.shape) == 3
        for n, (src, dx) in enumerate(((high, 1), (low, -1))):
            plan.append((src, self.rx.at[n, 0] if single else self.rx.at[n], (dx, 0)))
        for n, (src, dst, (dx, dy)) in enumerate(plan):
            copy = pltpu.make_async_remote_copy(
                src_ref=src,
                dst_ref=dst,
                send_sem=self.send.at[n],
                recv_sem=self.recv.at[n],
                device_id=place.at(dx, dy),
                device_id_type=MESH,
            )
            copy.start()
            self.copies.append(copy)

    def arrive(self):
        for copy in self.copies:
            copy.wait_recv()

    def sent(self):
        for copy in self.copies:
            copy.wait_send()

    def slabs(self, field):
        p = self.place
        return (
            self.rx[0, field, 0] * p.has_low,
            self.rx[0, field, 1] * p.has_low,
            self.rx[1, field, 0] * p.has_high,
            self.rx[1, field, 1] * p.has_high,
        )

    def halo(self, field):
        p = self.place
        left = self.rs[0, field] * p.has_left
        right = self.rs[1, field] * p.has_right
        j = lax.rem(lanes(left.shape[0]), 4)
        far = jnp.where(j == 0, rolled(right, -3), rolled(left, 3))
        near = jnp.where(j == 1, rolled(right, -1), rolled(left, 1))
        return jnp.where((j == 1) | (j == 2), near, far)

    def corner(self, field):
        p = self.place
        a = rolled(self.rk[0, field] * (p.has_low * p.has_right), 3)
        b = rolled(self.rk[1, field] * (p.has_low * p.has_left), 5)
        c = rolled(self.rk[2, field] * (p.has_high * p.has_right), -5)
        d = rolled(self.rk[3, field] * (p.has_high * p.has_left), -3)
        lane = lanes(a.shape[0])
        out = jnp.where(lane == 1, a, jnp.zeros_like(a))
        out = jnp.where(lane == 2, b, out)
        out = jnp.where(lane == NY - 3, c, out)
        return jnp.where(lane == NY - 2, d, out)


def packed_into(pack, v, x):
    lane = lanes(v.shape[0])
    return jnp.where(lane // 4 == x, pltpu.roll(v, lax.rem(4 * x + 2, NY), 1), pack)


HOPS = sorted(
    ((dz, dy) for dz in range(4) for dy in range(4) if dz or dy),
    key=lambda t: -(min(t[0], 4 - t[0]) + min(t[1], 4 - t[1])),
)


def ring_targets(place):
    x, core = place.px // 2, lax.rem(place.px, 2)
    z, y = place.py // 4, lax.rem(place.py, 4)
    px = []
    for dx, dc in ((2, 1), (2, 0), (1, 1), (1, 0), (3, 1), (3, 0), (0, 1)):
        px.append((lax.rem(x + dx, 4) * 2 + lax.rem(core + dc, 2), place.py))
    py = []
    for dz, dy in HOPS:
        py.append((place.px, lax.rem(z + dz, 4) * 4 + lax.rem(y + dy, 4)))
    return px, py


def kernel(
    beam,
    loc_in,
    share_in,
    t_in,
    k_in,
    c_in,
    x_out,
    r_out,
    flag_out,
    kraw,
    craw,
    traw,
    loc,
    share,
    window,
    weights,
    kct,
    z_ref,
    uv_ref,
    x_ref,
    g_ref,
    gp_ref,
    d_ref,
    e_ref,
    fd_ref,
    red_src,
    red_px,
    red_py,
    local_sem,
    beam_send,
    beam_recv,
    red_send,
    red_recv,
    *exchange_refs,
):
    place = Place()
    u_ref, v_ref = uv_ref.at[0], uv_ref.at[1]
    px_ring, py_ring = ring_targets(place)
    diagonal_devices = [place.at(dx, dy) for dx, dy in CORNERS]

    local = [
        pltpu.make_async_copy(src, dst, local_sem.at[n])
        for n, (src, dst) in enumerate(
            (
                (k_in, kraw),
                (c_in, craw),
                (t_in, traw),
                (loc_in, loc),
                (share_in, share),
            )
        )
    ]
    for copy in local:
        copy.start()
    own_columns = pl.ds(pl.multiple_of(place.py * NY, NY), NY)
    own_rows = pl.ds(pl.multiple_of(place.py * BR, BR), BR)
    own_beam = pltpu.make_async_copy(
        beam.at[:, :, own_columns], window.at[:, own_rows, :], local_sem.at[5]
    )
    own_beam.start()

    barrier = pltpu.get_barrier_semaphore()
    everyone = py_ring + px_ring + diagonal_devices
    for device in everyone:
        pl.semaphore_signal(barrier, inc=1, device_id=device, device_id_type=MESH)

    exchanges = [
        Exchange(place, exchange_refs[6 * n : 6 * n + 6]) for n in range(len(EXCHANGES))
    ]
    first, z_swap, e_swap, f_swap, *uv_swaps = exchanges

    for copy in local[:3]:
        copy.wait()
    zero = jnp.zeros((NZ, NY), jnp.float32)

    def lay(x, packs):
        out = []
        for n, raw in enumerate((kraw, craw, traw)):
            v = raw[pl.ds(x, NZ, stride=NX), :]
            kct[n, x + 2] = v
            out.append(packed_into(packs[n], v, x))
        return tuple(out)

    packs = slabs_loop(lay, (zero, zero, zero))
    k_pack, c_pack, t_pack = packs
    for n in range(3):
        first.pack[n] = packs[n]

    local[3].wait()
    local[4].wait()
    row8 = lax.broadcasted_iota(jnp.int32, (8, NY), 0)
    lane8 = lax.broadcasted_iota(jnp.int32, (8, NY), 1)
    beyond = jnp.where(row8 == 7, -1, jnp.where(row8 == 0, 8, -1000))

    def weigh(x, bad):
        own = [jnp.zeros((8, NY), jnp.float32) for _ in range(3)]
        edge = [jnp.zeros((8, NY), jnp.float32) for _ in range(3)]
        for k in range(CORR):
            index = jnp.broadcast_to(loc[k, pl.ds(x, 1), :], (8, NY))
            part = jnp.broadcast_to(share[k, pl.ds(x, 1), :], (8, NY))
            row = lax.shift_right_arithmetic(index, 7) - 8 * x
            col = lax.bitwise_and(index, 127) - lane8
            far = (row < -1) | (row > 8) | (col < -1) | (col > 1)
            bad = bad + jnp.where(far, 1.0, 0.0)
            inside = jnp.where(row == row8, part, 0.0)
            outside = jnp.where(row == beyond, part, 0.0)
            for n in range(3):
                here = col == n - 1
                own[n] = own[n] + jnp.where(here, inside, 0.0)
                edge[n] = edge[n] + jnp.where(here, outside, 0.0)
        for n in range(3):
            weights[n, x] = own[n]
            weights[3 + n, x] = edge[n]
        return bad

    bad = slabs_loop(weigh, jnp.zeros((8, NY), jnp.float32))

    pl.semaphore_wait(barrier, len(everyone))

    def send_frame(frame):
        copies = []
        for device in py_ring:
            columns = pl.ds(pl.multiple_of(device[1] * NY, NY), NY)
            copy = pltpu.make_async_remote_copy(
                src_ref=beam.at[frame, :, columns],
                dst_ref=window.at[frame, own_rows, :],
                send_sem=beam_send.at[frame],
                recv_sem=beam_recv.at[frame],
                device_id=device,
                device_id_type=MESH,
            )
            copy.start()

    def frame_bytes(frame, sem):
        most = window.at[frame, pl.ds(0, (NPY - 1) * BR), :]
        return pltpu.make_async_copy(most, most, sem.at[frame])

    first.start(kct.at[:, 2:4], kct.at[:, NX : NX + 2])
    send_frame(0)
    for frame in range(1, STEPS):
        send_frame(frame)

    first.arrive()
    for n in range(3):
        slabs = first.slabs(n)
        for at, slab in zip(GHOSTS, slabs):
            kct[n, at] = slab
    k_halo, k_corner = first.halo(0), first.corner(0)
    c_halo, t_halo = first.halo(1), first.halo(2)
    level = lax.broadcasted_iota(jnp.int32, (NZ, NY), 0)

    def over(k, up, down, below, above, left, right, storage, mask):
        bottom, top = level == 0, level == NZ - 1
        up = jnp.where(bottom, 0.0, up)
        down = jnp.where(top, 0.0, down)
        faces = [0.25 * (k + up), 0.25 * (k + down)]
        faces += [0.5 * (k + other) for other in (below, above, left, right)]
        diagonal = storage + (
            (faces[0] + faces[1]) + (faces[2] + faces[3]) + (faces[4] + faces[5])
        )
        inverse = mask / diagonal
        faces[0] = jnp.where(bottom, 0.0, faces[0])
        faces[1] = jnp.where(top, 0.0, faces[1])
        return [face * inverse for face in faces], diagonal, inverse

    def conduct(x, side, mask):
        i = x + 2
        k = kct[0, i]
        left, right = lateral(k, side)
        g, diagonal, inverse = over(
            k,
            rolled(k, 1, 0),
            rolled(k, -1, 0),
            kct[0, i - 1],
            kct[0, i + 1],
            left,
            right,
            kct[1, i],
            mask,
        )
        for n in range(6):
            g_ref[n, x + 1] = g[n]
        return diagonal, inverse

    conduct(-1, side_tile(k_corner, 0), place.has_low)
    conduct(NX, side_tile(k_corner, NX - 1), place.has_high)

    def conduct_inside(x, pack):
        diagonal, inverse = conduct(x, side_tile(k_halo, x), 1.0)
        d_ref[x] = diagonal
        e = kct[1, x + 2] * inverse
        e_ref[x + 2] = e
        return packed_into(pack, e, x)

    e_swap.pack[0] = slabs_loop(conduct_inside, zero)

    below, above, inner, outer = around_halo(k_halo, k_corner, k_pack)
    j = lax.rem(lanes(), 4)
    halo_mask = jnp.where(j < 2, place.has_right, place.has_left)
    halo_mask = jnp.where((j == 1) | (j == 2), halo_mask, 0.0)
    gp, _, _ = over(
        k_halo,
        rolled(k_halo, 1, 0),
        rolled(k_halo, -1, 0),
        below,
        above,
        inner,
        outer,
        c_halo + jnp.where(halo_mask > 0.0, 0.0, 1.0),
        halo_mask,
    )
    for n in range(6):
        gp_ref[n] = gp[n]

    t_ref = kct.at[2]

    def residual(x, carry):
        image = apply_slab(t_ref, x + 2, side_tile(t_halo, x), g_ref, x + 1)
        t = t_ref[x + 2]
        z_ref[x + 2] = e_ref[x + 2] * t - image
        x_ref[x] = t
        return carry

    slabs_loop(residual, 0)
    first.sent()

    own_beam.wait()

    def flux_tile(frame, x):
        def rows(i):
            return window[frame, pl.ds(pl.multiple_of(i * 8, 8), 8), :]

        mine = rows(x)
        around = jnp.where(
            row8 == 7, rows(jnp.maximum(x - 1, 0)), rows(jnp.minimum(x + 1, NX - 1))
        )
        part = weights[1, x] * mine + weights[4, x] * around
        part = part + weights[0, x] * rolled(mine, 1) + weights[3, x] * rolled(around, 1)
        part = part + weights[2, x] * rolled(mine, -1) + weights[5, x] * rolled(around, -1)
        flux = jnp.sum(part, axis=0, keepdims=True)
        top = d_ref[x, NZ - 8 : NZ, :]
        return jnp.where(row8 == 7, flux, 0.0) / top

    def zero_row():
        return jnp.zeros((8, NY), jnp.float32)

    def all_sum(step, moments, meanwhile):
        lane = lax.broadcasted_iota(jnp.int32, (1, NY), 1)
        row = jnp.zeros((1, NY), jnp.float32)
        for n, m in enumerate(moments):
            row = jnp.where(lane == n, jnp.sum(m, keepdims=True), row)
        for phase, (ring, slots, me) in enumerate(
            ((px_ring, red_px, place.px), (py_ring, red_py, place.py))
        ):
            source = red_src.at[step, phase]
            source[...] = row
            for device in ring:
                pltpu.make_async_remote_copy(
                    src_ref=source,
                    dst_ref=slots.at[step, me],
                    send_sem=red_send.at[step, phase],
                    recv_sem=red_recv.at[step, phase],
                    device_id=device,
                    device_id_type=MESH,
                ).start()
            slots[step, me] = row
            meanwhile[phase]()
            most = slots.at[step, pl.ds(0, len(ring))]
            pltpu.make_async_copy(most, most, red_recv.at[step, phase]).wait()
            parts = [slots[step, n] for n in range(len(ring) + 1)]
            while len(parts) > 1:
                parts = [a + b for a, b in zip(parts[::2], parts[1::2])]
            row = parts[0]
        return [
            jnp.sum(jnp.where(lane == n, row, 0.0), axis=1, keepdims=True)
            for n in range(len(moments))
        ]

    def folded(v):
        return v[0:8] + v[8:16] + v[16:24]

    frame_bytes(0, beam_recv).wait()

    def add_flux(x, pack):
        tile = flux_tile(0, x)
        fd_ref[0, x + 2] = tile
        z_ref[x + 2, NZ - 8 : NZ, :] = z_ref[x + 2, NZ - 8 : NZ, :] + tile
        return packed_into(pack, z_ref[x + 2], x)

    z_pack = slabs_loop(add_flux, zero)
    z_swap.pack[0] = z_pack
    z_swap.start(z_ref.at[pl.ds(2, 2)], z_ref.at[pl.ds(NX, 2)])
    e_swap.start(e_ref.at[pl.ds(2, 2)], e_ref.at[pl.ds(NX, 2)])
    z_swap.arrive()
    for at, slab in zip(GHOSTS, z_swap.slabs(0)):
        z_ref[at] = slab
    z_halo, z_corner = z_swap.halo(0), z_swap.corner(0)

    def later_fluxes():
        frame_bytes(1, beam_recv).wait()
        frame_bytes(2, beam_recv).wait()

        def next_flux(x, packs):
            second, third = flux_tile(1, x), flux_tile(2, x)
            third = third - second
            second = second - fd_ref[0, x + 2]
            fd_ref[1, x + 2] = second
            fd_ref[2, x + 2] = third
            return packed_into(packs[0], second, x), packed_into(packs[1], third, x)

        packs = slabs_loop(next_flux, (zero_row(),) * 2)
        f_swap.pack[0], f_swap.pack[1] = packs
        f_swap.start(fd_ref.at[pl.ds(1, 2), pl.ds(2, 2)], fd_ref.at[pl.ds(1, 2), pl.ds(NX, 2)])

    for step in range(STEPS):
        u_ref[1] = apply_slab(z_ref, 1, side_tile(z_corner, 0), g_ref, 0)
        u_ref[NX + 2] = apply_slab(z_ref, NX + 2, side_tile(z_corner, NX - 1), g_ref, NX + 1)
        u_halo = apply_halo(z_halo, z_corner, z_pack, gp_ref)
        swap = uv_swaps[step] if step + 1 < STEPS else None

        def first_image(x, carry):
            sums, pack = carry
            u = apply_slab(z_ref, x + 2, side_tile(z_halo, x), g_ref, x + 1)
            u_ref[x + 2] = u
            z = z_ref[x + 2]
            dz = d_ref[x] * z
            du = d_ref[x] * u
            sums = (
                sums[0] + folded(dz * z),
                sums[1] + folded(dz * u),
                sums[2] + folded(du * u),
            )
            return sums, (packed_into(pack, u, x) if swap else pack)

        sums, u_pack = slabs_loop(first_image, ((zero_row(),) * 3, zero))

        def second_image(x, carry):
            acc, pack = carry
            v = apply_slab(u_ref, x + 2, side_tile(u_halo, x), g_ref, x + 1)
            v_ref[x + 2] = v
            acc = acc + folded(d_ref[x] * u_ref[x + 2] * v)
            return acc, (packed_into(pack, v, x) if swap else pack)

        last, v_pack = slabs_loop(second_image, (zero_row(), zero))

        def send_images():
            if swap:
                swap.pack[0] = u_pack
                swap.pack[1] = v_pack
                swap.start(uv_ref.at[:, pl.ds(2, 2)], uv_ref.at[:, pl.ds(NX, 2)])
            if step == 0:
                later_fluxes()

        def receive_images():
            if step == 0:
                z_swap.sent()
                e_swap.arrive()
                for at, slab in zip(GHOSTS, e_swap.slabs(0)):
                    e_ref[at] = slab
                f_swap.arrive()
                for n in range(2):
                    for at, slab in zip(GHOSTS, f_swap.slabs(n)):
                        fd_ref[1 + n, at] = slab
            if swap:
                swap.arrive()

        g0, a, w, t, *rest = all_sum(
            step,
            list(sums) + [last] + ([bad] if step == 0 else []),
            (send_images, receive_images),
        )
        if step == 0:
            flag_out[0] = jnp.where(jnp.sum(rest[0]) > 0.0, 1, 0).astype(jnp.int32)
        alpha0 = g0 / a
        gamma1 = alpha0 * alpha0 * w - g0
        beta1 = 1.0 + gamma1 / g0
        alpha1 = gamma1 / (beta1 * beta1 * a - 2.0 * beta1 * alpha0 * w + alpha0 * alpha0 * t)
        d1 = jnp.broadcast_to(alpha0 + alpha1 * beta1, (NZ, NY))
        d2 = jnp.broadcast_to(-alpha0 * alpha1, (NZ, NY))

        def next_z(z, u, v, e, tile):
            z = z - d1 * u - d2 * v + e * (d1 * z + d2 * u)
            return jnp.concatenate([z[: NZ - 8], z[NZ - 8 :] + tile], axis=0)

        if swap:
            for at, u, v in zip(GHOSTS, swap.slabs(0), swap.slabs(1)):
                z_ref[at] = next_z(z_ref[at], u, v, e_ref[at], fd_ref[step + 1, at])
            z_halo, z_corner = (
                next_z(z, get(swap, 0), get(swap, 1), get(e_swap, 0), get(f_swap, step))
                for z, get in ((z_halo, Exchange.halo), (z_corner, Exchange.corner))
            )

            def update(x, pack):
                z, u, v = z_ref[x + 2], u_ref[x + 2], v_ref[x + 2]
                x_ref[x] = x_ref[x] + (d1 * z + d2 * u)
                z = next_z(z, u, v, e_ref[x + 2], fd_ref[step + 1, x + 2])
                z_ref[x + 2] = z
                return packed_into(pack, z, x)

            z_pack = slabs_loop(update, zero)
            swap.sent()
        else:

            def finish(x, carry):
                z, u, v = z_ref[x + 2], u_ref[x + 2], v_ref[x + 2]
                x_out[pl.ds(x, NZ, stride=NX), :] = x_ref[x] + (d1 * z + d2 * u)
                r_out[pl.ds(x, NZ, stride=NX), :] = d_ref[x] * (z - d1 * u - d2 * v)
                return carry

            slabs_loop(finish, 0)

    e_swap.sent()
    f_swap.sent()
    for frame in range(STEPS):
        frame_bytes(frame, beam_send).wait()
    for step in range(STEPS):
        for phase, (slots, count) in enumerate(((red_px, NPX - 1), (red_py, NPY - 1))):
            most = slots.at[step, pl.ds(0, count)]
            pltpu.make_async_copy(most, most, red_send.at[step, phase]).wait()


def exchange_scratch(fields, rows):
    f32 = jnp.float32
    return [
        pltpu.VMEM((2, fields, 2, rows, NY), f32),
        pltpu.VMEM((2, fields, rows, NY), f32),
        pltpu.VMEM((4, fields, rows, NY), f32),
        pltpu.VMEM((fields, rows, NY), f32),
        pltpu.SemaphoreType.DMA((8,)),
        pltpu.SemaphoreType.DMA((8,)),
    ]


def hand_on(a_in, b_in, a_out, b_out, sem):
    copies = [
        pltpu.make_async_copy(src, dst, sem.at[n])
        for n, (src, dst) in enumerate(((a_in, a_out), (b_in, b_out)))
    ]
    for copy in copies:
        copy.start()
    for copy in copies:
        copy.wait()


def handed_on(a, b):
    space = pl.BlockSpec(memory_space=pl.ANY)
    return pl.pallas_call(
        hand_on,
        out_shape=(jax.ShapeDtypeStruct(a.shape, a.dtype), jax.ShapeDtypeStruct(b.shape, b.dtype)),
        in_specs=[space, space],
        out_specs=(space, space),
        scratch_shapes=[pltpu.SemaphoreType.DMA((2,))],
    )(a, b)


def body(
    incident_power_density,
    coupling_patch_locator,
    coupling_share_factor,
    starting_warmth,
    diffusive_coefficient,
    thermal_storage,
):
    f32 = jnp.float32
    flat = (NZ * NX, NY)
    hbm = pl.BlockSpec(memory_space=pl.ANY)
    vmem = pl.BlockSpec(memory_space=pltpu.VMEM)
    scratch = [
        pltpu.VMEM(flat, f32),
        pltpu.VMEM(flat, f32),
        pltpu.VMEM(flat, f32),
        pltpu.VMEM((CORR, NX, NY), jnp.int32),
        pltpu.VMEM((CORR, NX, NY), f32),
        pltpu.VMEM((STEPS, BR * NPY, NY), f32),
        pltpu.VMEM((6, NX, 8, NY), f32),
        pltpu.VMEM((3, NX + 4, NZ, NY), f32),
        pltpu.VMEM((NX + 4, NZ, NY), f32),
        pltpu.VMEM((2, NX + 4, NZ, NY), f32),
        pltpu.VMEM((NX, NZ, NY), f32),
        pltpu.VMEM((6, NX + 2, NZ, NY), f32),
        pltpu.VMEM((6, NZ, NY), f32),
        pltpu.VMEM((NX, NZ, NY), f32),
        pltpu.VMEM((NX + 4, NZ, NY), f32),
        pltpu.VMEM((STEPS, NX + 4, 8, NY), f32),
        pltpu.VMEM((STEPS, 2, 1, NY), f32),
        pltpu.VMEM((STEPS, NPX, 1, NY), f32),
        pltpu.VMEM((STEPS, NPY, 1, NY), f32),
        pltpu.SemaphoreType.DMA((6,)),
        pltpu.SemaphoreType.DMA((STEPS,)),
        pltpu.SemaphoreType.DMA((STEPS,)),
        pltpu.SemaphoreType.DMA((STEPS, 2)),
        pltpu.SemaphoreType.DMA((STEPS, 2)),
    ]
    for fields, rows in EXCHANGES:
        scratch += exchange_scratch(fields, rows)
    warmth, leftover, flag = pl.pallas_call(
        kernel,
        out_shape=(
            jax.ShapeDtypeStruct(flat, f32),
            jax.ShapeDtypeStruct(flat, f32),
            jax.ShapeDtypeStruct((1,), jnp.int32),
        ),
        in_specs=[hbm] * 6,
        out_specs=(vmem, vmem, pl.BlockSpec(memory_space=pltpu.SMEM)),
        scratch_shapes=scratch,
        compiler_params=pltpu.CompilerParams(
            collective_id=0, has_side_effects=True, vmem_limit_bytes=40 * 2**20
        ),
    )(
        incident_power_density,
        coupling_patch_locator,
        coupling_share_factor,
        starting_warmth.reshape(flat),
        diffusive_coefficient.reshape(flat),
        thermal_storage.reshape(flat),
    )
    shape = starting_warmth.shape
    out = lax.cond(
        flag[0] > 0,
        lambda: list(
            general(
                incident_power_density,
                coupling_patch_locator,
                coupling_share_factor,
                starting_warmth,
                diffusive_coefficient,
                thermal_storage,
            )
        ),
        lambda: [out.reshape(shape) for out in handed_on(warmth, leftover)],
    )
    return tuple(out)


def solution(mesh):
    placed = (
        P(None, ("px", "py"), None),
        P(None, "px", "py"),
        P(None, "px", "py"),
        P(None, "px", "py"),
        P(None, "px", "py"),
        P(None, "px", "py"),
    )
    return jax.shard_map(
        body,
        mesh=mesh,
        in_specs=placed,
        out_specs=(P(None, "px", "py"), P(None, "px", "py")),
        check_vma=False,
    )
```

```python
import functools

import jax
import jax.numpy as jnp
from jax import lax
from jax.experimental import pallas as pl
from jax.experimental.pallas import tpu as pltpu
from jax.sharding import PartitionSpec as P

ITERS = 2
MESH = pl.DeviceIdType.MESH

NZ = 24
NX = 32
NY = 128
NPX = 8
NPY = 16
BR = 16
STEPS = 3
CORR = 8
UNROLL = 8


through_ratio = 0.5


def extended(block, sides, width):
    for axis, dim in sides:
        count = lax.axis_size(axis)
        forward = [(i, i + 1) for i in range(count - 1)]
        backward = [(target, source) for source, target in forward]
        low = lax.ppermute(
            lax.slice_in_dim(block, block.shape[dim] - width, None, axis=dim), axis, forward
        )
        high = lax.ppermute(lax.slice_in_dim(block, 0, width, axis=dim), axis, backward)
        block = jnp.concatenate([low, block, high], axis=dim)
    return block


def with_rim(field):
    rimmed = extended(field, (("px", 1), ("py", 2)), 1)
    return jnp.pad(rimmed, ((1, 1), (0, 0), (0, 0)))


def stencil(padded, field, faces, diagonal):
    beside = faces[0] * padded[:-2, 1:-1, 1:-1] + faces[1] * padded[2:, 1:-1, 1:-1]
    beside = beside + faces[2] * padded[1:-1, :-2, 1:-1] + faces[3] * padded[1:-1, 2:, 1:-1]
    beside = beside + faces[4] * padded[1:-1, 1:-1, :-2] + faces[5] * padded[1:-1, 1:-1, 2:]
    return diagonal * field - beside


def operate(field, faces, diagonal):
    return stencil(with_rim(field), field, faces, diagonal)


def face_terms(centre, padded):
    return (
        through_ratio * 0.5 * (centre + padded[:-2, 1:-1, 1:-1]),
        through_ratio * 0.5 * (centre + padded[2:, 1:-1, 1:-1]),
        0.5 * (centre + padded[1:-1, :-2, 1:-1]),
        0.5 * (centre + padded[1:-1, 2:, 1:-1]),
        0.5 * (centre + padded[1:-1, 1:-1, :-2]),
        0.5 * (centre + padded[1:-1, 1:-1, 2:]),
    )


def surface_flux(window, coupling_patch_locator, coupling_share_factor):
    flat = window.reshape(-1)
    values = flat[coupling_patch_locator]
    return jnp.sum(coupling_share_factor * values, axis=0)


def total(a, b):
    return lax.psum(jnp.sum(a * b), ("px", "py"))


def solve_step(solution, leftover_error_vector, faces, diagonal):
    scaled = leftover_error_vector / diagonal
    axis_direction = scaled
    gamma = total(leftover_error_vector, scaled)
    for turn in range(ITERS):
        image = operate(axis_direction, faces, diagonal)
        alpha = gamma / total(axis_direction, image)
        solution = solution + alpha * axis_direction
        leftover_error_vector = leftover_error_vector - alpha * image
        if turn + 1 < ITERS:
            scaled = leftover_error_vector / diagonal
            fresh = total(leftover_error_vector, scaled)
            axis_direction = scaled + fresh / gamma * axis_direction
            gamma = fresh
    return (solution, leftover_error_vector)


def general(
    incident_power_density,
    coupling_patch_locator,
    coupling_share_factor,
    starting_warmth,
    diffusive_coefficient,
    thermal_storage,
):
    sheet_level = starting_warmth.shape[0]
    rimmed = extended(diffusive_coefficient, (("px", 1), ("py", 2)), 1)
    padded = jnp.pad(rimmed, ((1, 1), (0, 0), (0, 0)))
    faces = face_terms(diffusive_coefficient, padded)
    diagonal = thermal_storage + faces[0] + faces[1] + faces[2] + faces[3] + faces[4] + faces[5]
    frames = incident_power_density.shape[0]
    final_warmth = starting_warmth
    leftover_error_vector = starting_warmth
    for frame in range(frames):
        window = lax.all_to_all(
            incident_power_density[frame : frame + 1], "py", split_axis=2, concat_axis=1, tiled=True
        )[0]
        flux = surface_flux(window, coupling_patch_locator, coupling_share_factor)
        right = thermal_storage * final_warmth
        right = right.at[sheet_level - 1].add(flux)
        leftover_error_vector = right - operate(final_warmth, faces, diagonal)
        final_warmth, leftover_error_vector = solve_step(
            final_warmth, leftover_error_vector, faces, diagonal
        )
    return (final_warmth, leftover_error_vector)


def lanes(rows=NZ):
    return lax.broadcasted_iota(jnp.int32, (rows, NY), 1)


def rolled(v, shift, axis=1):
    return pltpu.roll(v, shift % v.shape[axis], axis)


def slabs_loop(fn, init, step=UNROLL):
    def some(n, carry):
        for q in range(step):
            carry = fn(n * step + q, carry)
        return carry

    return lax.fori_loop(0, NX // step, some, init)


def side_tile(packed, x):
    return pltpu.roll(packed, lax.rem(638 - 4 * x, 128), 1)


def lateral(v, side):
    lane = lanes(v.shape[0])
    left = jnp.where(lane == 0, side, rolled(v, 1))
    right = jnp.where(lane == NY - 1, side, rolled(v, -1))
    return left, right


def apply_slab(ref, i, side, g_ref, gi):
    v = ref[i]
    left, right = lateral(v, side)
    out = g_ref[0, gi] * rolled(v, 1, 0) + g_ref[1, gi] * rolled(v, -1, 0)
    out = out + (g_ref[2, gi] * ref[i - 1] + g_ref[3, gi] * ref[i + 1])
    out = out + (g_ref[4, gi] * left + g_ref[5, gi] * right)
    return v - out


def around_halo(halo, corner, pack):
    lane = lanes()
    j = lax.rem(lane, 4)
    below = jnp.where(lane < 4, corner, rolled(halo, 4))
    above = jnp.where(lane >= NY - 4, corner, rolled(halo, -4))
    outer = jnp.where(j == 1, rolled(halo, 1), rolled(halo, -1))
    return below, above, pack, outer


def apply_halo(halo, corner, pack, gp_ref):
    below, above, inner, outer = around_halo(halo, corner, pack)
    out = gp_ref[0] * rolled(halo, 1, 0) + gp_ref[1] * rolled(halo, -1, 0)
    out = out + gp_ref[2] * below + gp_ref[3] * above + gp_ref[4] * inner + gp_ref[5] * outer
    return halo - out


class Place:
    def __init__(self):
        self.px = lax.axis_index("px")
        self.py = lax.axis_index("py")
        self.has_low = jnp.where(self.px > 0, 1.0, 0.0).astype(jnp.float32)
        self.has_high = jnp.where(self.px < NPX - 1, 1.0, 0.0).astype(jnp.float32)
        self.has_left = jnp.where(self.py > 0, 1.0, 0.0).astype(jnp.float32)
        self.has_right = jnp.where(self.py < NPY - 1, 1.0, 0.0).astype(jnp.float32)

    def at(self, dx, dy):
        return (lax.rem(self.px + dx + NPX, NPX), lax.rem(self.py + dy + NPY, NPY))


GHOSTS = (0, 1, NX + 2, NX + 3)
EXCHANGES = ((1, NZ), (1, NZ), (2, 8))
CORNERS = ((-1, 1), (-1, -1), (1, 1), (1, -1))


class Exchange:
    def __init__(self, place, refs):
        self.place = place
        self.rx, self.rs, self.rk, self.pack, self.send, self.recv = refs

    def plan(self, low, high):
        to_right, to_left = self.packs()
        plan = []
        for n, (dx, dy) in enumerate(CORNERS):
            plan.append((to_left if dy > 0 else to_right, self.rk.at[n], (-dx, -dy)))
        plan.append((to_right, self.rs.at[0], (0, 1)))
        plan.append((to_left, self.rs.at[1], (0, -1)))
        single = len(low.shape) + 2 == len(self.rx.shape)
        for n, (src, dx) in enumerate(((high, 1), (low, -1))):
            plan.append((src, self.rx.at[n, 0] if single else self.rx.at[n], (dx, 0)))
        return [
            pltpu.make_async_remote_copy(
                src_ref=src,
                dst_ref=dst,
                send_sem=self.send.at[n],
                recv_sem=self.recv.at[n],
                device_id=self.place.at(dx, dy),
                device_id_type=MESH,
            )
            for n, (src, dst, (dx, dy)) in enumerate(plan)
        ]

    def packs(self):
        return self.pack, self.pack

    def start(self, *edges):
        for copy in self.plan(*edges):
            copy.start()

    def arrive(self, *edges):
        for copy in self.plan(*edges):
            copy.wait_recv()

    def sent(self, *edges):
        for copy in self.plan(*edges):
            copy.wait_send()

    def slabs(self, field):
        p = self.place
        return (
            self.rx[0, field, 0] * p.has_low,
            self.rx[0, field, 1] * p.has_low,
            self.rx[1, field, 0] * p.has_high,
            self.rx[1, field, 1] * p.has_high,
        )

    def sides(self, field):
        return self.rs[0, field], self.rs[1, field], (-3, -1, 1, 3)

    def corners(self, field):
        return [self.rk[n, field] for n in range(4)], (3, 5, -5, -3)

    def halo(self, field):
        p = self.place
        left, right, shifts = self.sides(field)
        left, right = left * p.has_left, right * p.has_right
        j = lax.rem(lanes(left.shape[0]), 4)
        far = jnp.where(j == 0, rolled(right, shifts[0]), rolled(left, shifts[3]))
        near = jnp.where(j == 1, rolled(right, shifts[1]), rolled(left, shifts[2]))
        return jnp.where((j == 1) | (j == 2), near, far)

    def corner(self, field):
        p = self.place
        tiles, shifts = self.corners(field)
        masks = (
            p.has_low * p.has_right,
            p.has_low * p.has_left,
            p.has_high * p.has_right,
            p.has_high * p.has_left,
        )
        lane = lanes(tiles[0].shape[0])
        out = jnp.zeros_like(tiles[0])
        for at, tile, mask, shift in zip((1, 2, NY - 3, NY - 2), tiles, masks, shifts):
            out = jnp.where(lane == at, rolled(tile * mask, shift), out)
        return out


class PairExchange(Exchange):
    def packs(self):
        return self.pack.at[0], self.pack.at[1]

    def fill(self, first, second):
        j = lax.rem(lanes(), 4)
        self.pack[0] = jnp.where(j < 2, first, rolled(second, 2))
        self.pack[1] = jnp.where(j < 2, rolled(first, -2), second)

    def sides(self, field):
        return self.rs[0], self.rs[1], ((-3, -1, -1, 1) if field else (-1, 1, 1, 3))

    def corners(self, field):
        return [self.rk[n] for n in range(4)], ((3, 3, -5, -5) if field else (5, 5, -3, -3))


class FirstExchange(PairExchange):
    def fill(self, k, c, t):
        j = lax.rem(lanes(), 4)
        right = jnp.where(j == 2, rolled(c, 1), rolled(t, 2))
        left = jnp.where(j == 2, c, rolled(t, 1))
        self.pack[0] = jnp.where(j < 2, k, right)
        self.pack[1] = jnp.where(j < 2, rolled(k, -2), left)

    def sides(self, field):
        return self.rs[0], self.rs[1], ((-1, 1, 1, 3), (0, -1, 0, 0), (0, -2, -1, 0))[field]


def packed_into(pack, v, x):
    lane = lanes(v.shape[0])
    return jnp.where(lane // 4 == x, pltpu.roll(v, lax.rem(4 * x + 2, NY), 1), pack)


HOPS = sorted(
    ((dz, dy) for dz in range(4) for dy in range(4) if dz or dy),
    key=lambda t: -(min(t[0], 4 - t[0]) + min(t[1], 4 - t[1])),
)


def ring_targets(place):
    x, core = place.px // 2, lax.rem(place.px, 2)
    z, y = place.py // 4, lax.rem(place.py, 4)
    px = []
    for dx, dc in ((2, 1), (2, 0), (1, 1), (1, 0), (3, 1), (3, 0), (0, 1)):
        px.append((lax.rem(x + dx, 4) * 2 + lax.rem(core + dc, 2), place.py))
    py = []
    for dz, dy in HOPS:
        py.append((place.px, lax.rem(z + dz, 4) * 4 + lax.rem(y + dy, 4)))
    return px, py


def kernel(
    beam,
    loc_in,
    share_in,
    t_in,
    k_in,
    c_in,
    x_out,
    r_out,
    flag_out,
    kraw,
    craw,
    traw,
    loc,
    share,
    window,
    weights,
    kct,
    z_ref,
    uv_ref,
    x_ref,
    g_ref,
    gp_ref,
    d_ref,
    e_ref,
    fd_ref,
    z_near,
    e_near,
    f_near,
    uv_near,
    red_src,
    red_px,
    red_py,
    local_sem,
    beam_send,
    beam_recv,
    red_send,
    red_recv,
    *exchange_refs,
):
    place = Place()
    u_ref, v_ref = uv_ref.at[0], uv_ref.at[1]
    px_ring, py_ring = ring_targets(place)
    diagonal_devices = [place.at(dx, dy) for dx, dy in CORNERS]

    local = [
        pltpu.make_async_copy(src, dst, local_sem.at[n])
        for n, (src, dst) in enumerate(
            (
                (k_in, kraw),
                (c_in, craw),
                (t_in, traw),
                (loc_in, loc),
                (share_in, share),
            )
        )
    ]
    for copy in local:
        copy.start()
    own_columns = pl.ds(pl.multiple_of(place.py * NY, NY), NY)
    own_rows = pl.ds(pl.multiple_of(place.py * BR, BR), BR)
    own_beam = pltpu.make_async_copy(
        beam.at[:, :, own_columns], window.at[:, own_rows, :], local_sem.at[5]
    )
    own_beam.start()

    barrier = pltpu.get_barrier_semaphore()
    everyone = py_ring + px_ring + diagonal_devices
    for device in everyone:
        pl.semaphore_signal(barrier, inc=1, device_id=device, device_id_type=MESH)

    exchanges = [
        Exchange(place, exchange_refs[6 * n : 6 * n + 6]) for n in range(len(EXCHANGES))
    ]
    z_swap, e_swap, f_swap = exchanges
    first = FirstExchange(place, exchange_refs[-13:-7])
    k_edge = exchange_refs[-7]
    uv_refs = exchange_refs[-6:]
    k_edges = k_edge.at[0], k_edge.at[1]
    z_edges = z_ref.at[pl.ds(2, 2)], z_ref.at[pl.ds(NX, 2)]
    e_edges = e_ref.at[pl.ds(2, 2)], e_ref.at[pl.ds(NX, 2)]
    f_edges = fd_ref.at[pl.ds(1, 2), pl.ds(2, 2)], fd_ref.at[pl.ds(1, 2), pl.ds(NX, 2)]
    uv_edges = uv_ref.at[:, pl.ds(2, 2)], uv_ref.at[:, pl.ds(NX, 2)]

    for copy in local[:3]:
        copy.wait()
    zero = jnp.zeros((NZ, NY), jnp.float32)

    def zero_row():
        return jnp.zeros((8, NY), jnp.float32)

    def lay(x, packs):
        out = []
        for n, raw in enumerate((kraw, craw, traw)):
            v = raw[pl.ds(x, NZ, stride=NX), :]
            kct[n, x + 2] = v
            out.append(packed_into(packs[n], v, x))
        return tuple(out)

    packs = slabs_loop(lay, (zero, zero, zero))
    k_pack, c_pack, t_pack = packs
    first.fill(*packs)
    edges = ((0, 0, NX - 2), (0, 1, NX - 1), (1, 0, NX - 1), (2, 0, NX - 1))
    for n, (field, low, high) in enumerate(edges):
        k_edge[0, n] = kct[field, low + 2]
        k_edge[1, n] = kct[field, high + 2]

    local[3].wait()
    local[4].wait()
    row8 = lax.broadcasted_iota(jnp.int32, (8, NY), 0)
    lane8 = lax.broadcasted_iota(jnp.int32, (8, NY), 1)
    beyond = jnp.where(row8 == 7, -1, jnp.where(row8 == 0, 8, -1000))

    def weigh(x, bad):
        own = [jnp.zeros((8, NY), jnp.float32) for _ in range(3)]
        edge = [jnp.zeros((8, NY), jnp.float32) for _ in range(3)]
        for k in range(CORR):
            index = jnp.broadcast_to(loc[k, pl.ds(x, 1), :], (8, NY))
            part = jnp.broadcast_to(share[k, pl.ds(x, 1), :], (8, NY))
            row = lax.shift_right_arithmetic(index, 7) - 8 * x
            col = lax.bitwise_and(index, 127) - lane8
            far = (row < -1) | (row > 8) | (col < -1) | (col > 1)
            bad = bad + jnp.where(far, 1.0, 0.0)
            inside = jnp.where(row == row8, part, 0.0)
            outside = jnp.where(row == beyond, part, 0.0)
            for n in range(3):
                here = col == n - 1
                own[n] = own[n] + jnp.where(here, inside, 0.0)
                edge[n] = edge[n] + jnp.where(here, outside, 0.0)
        for n in range(3):
            weights[n, x] = own[n]
            weights[3 + n, x] = edge[n]
        return bad

    bad = slabs_loop(weigh, jnp.zeros((8, NY), jnp.float32))

    pl.semaphore_wait(barrier, len(everyone))

    def send_frame(frame):
        def send_block(n, nothing):
            n = jnp.where(n < 10, n, n + 1)
            device = (
                place.px,
                lax.rem(place.py // 4 + 2 + n // 4, 4) * 4 + lax.rem(lax.rem(place.py, 4) + 2 + lax.rem(n, 4), 4),
            )
            columns = pl.ds(pl.multiple_of(device[1] * NY, NY), NY)
            copy = pltpu.make_async_remote_copy(
                src_ref=beam.at[frame, :, columns],
                dst_ref=window.at[frame, own_rows, :],
                send_sem=beam_send.at[frame],
                recv_sem=beam_recv.at[frame],
                device_id=device,
                device_id_type=MESH,
            )
            copy.start()
            return nothing

        lax.fori_loop(0, NPY - 1, send_block, 0)

    def frame_bytes(frame, sem):
        most = window.at[frame, pl.ds(0, (NPY - 1) * BR), :]
        return pltpu.make_async_copy(most, most, sem.at[frame])

    first.start(*k_edges)
    send_frame(0)
    for frame in range(1, STEPS):
        send_frame(frame)

    first.arrive(*k_edges)
    for n, (field, low, high) in enumerate(edges):
        kct[field, high + 2 - NX] = first.rx[0, n] * place.has_low
        kct[field, low + 2 + NX] = first.rx[1, n] * place.has_high
    k_halo, k_corner = first.halo(0), first.corner(0)
    c_halo, t_halo = first.halo(1), first.halo(2)
    c_halo = jnp.where((lax.rem(lanes(), 4) + 1) // 2 == 1, c_halo, 0.0)
    level = lax.broadcasted_iota(jnp.int32, (NZ, NY), 0)

    def over(k, up, down, below, above, left, right, storage, mask):
        bottom, top = level == 0, level == NZ - 1
        up = jnp.where(bottom, 0.0, up)
        down = jnp.where(top, 0.0, down)
        faces = [0.25 * (k + up), 0.25 * (k + down)]
        faces += [0.5 * (k + other) for other in (below, above, left, right)]
        diagonal = storage + (
            (faces[0] + faces[1]) + (faces[2] + faces[3]) + (faces[4] + faces[5])
        )
        inverse = mask / diagonal
        faces[0] = jnp.where(bottom, 0.0, faces[0])
        faces[1] = jnp.where(top, 0.0, faces[1])
        return [face * inverse for face in faces], diagonal, inverse

    def conduct(x, side, mask):
        i = x + 2
        k = kct[0, i]
        left, right = lateral(k, side)
        g, diagonal, inverse = over(
            k,
            rolled(k, 1, 0),
            rolled(k, -1, 0),
            kct[0, i - 1],
            kct[0, i + 1],
            left,
            right,
            kct[1, i],
            mask,
        )
        for n in range(6):
            g_ref[n, x + 1] = g[n]
        return diagonal, inverse

    conduct(-1, side_tile(k_corner, 0), place.has_low)
    conduct(NX, side_tile(k_corner, NX - 1), place.has_high)

    def conduct_inside(x, pack):
        diagonal, inverse = conduct(x, side_tile(k_halo, x), 1.0)
        d_ref[x] = diagonal
        e = kct[1, x + 2] * inverse
        e_ref[x + 2] = e
        return packed_into(pack, e, x)

    e_swap.pack[0] = slabs_loop(conduct_inside, zero)

    below, above, inner, outer = around_halo(k_halo, k_corner, k_pack)
    j = lax.rem(lanes(), 4)
    halo_mask = jnp.where(j < 2, place.has_right, place.has_left)
    halo_mask = jnp.where((j == 1) | (j == 2), halo_mask, 0.0)
    gp, _, _ = over(
        k_halo,
        rolled(k_halo, 1, 0),
        rolled(k_halo, -1, 0),
        below,
        above,
        inner,
        outer,
        c_halo + jnp.where(halo_mask > 0.0, 0.0, 1.0),
        halo_mask,
    )
    for n in range(6):
        gp_ref[n] = gp[n]

    t_ref = kct.at[2]

    def residual(x, carry):
        image = apply_slab(t_ref, x + 2, side_tile(t_halo, x), g_ref, x + 1)
        t = t_ref[x + 2]
        z = e_ref[x + 2] * t - image
        z_ref[x + 2] = z
        x_ref[x] = t
        return packed_into(carry, z, x)

    z_near[2] = slabs_loop(residual, zero)
    first.sent(*k_edges)

    own_beam.wait()

    def flux_tile(frame, x):
        def rows(i):
            return window[frame, pl.ds(pl.multiple_of(i * 8, 8), 8), :]

        mine = rows(x)
        around = jnp.where(
            row8 == 7, rows(jnp.maximum(x - 1, 0)), rows(jnp.minimum(x + 1, NX - 1))
        )
        part = weights[1, x] * mine + weights[4, x] * around
        part = part + weights[0, x] * rolled(mine, 1) + weights[3, x] * rolled(around, 1)
        part = part + weights[2, x] * rolled(mine, -1) + weights[5, x] * rolled(around, -1)
        flux = jnp.sum(part, axis=0, keepdims=True)
        top = d_ref[x, NZ - 8 : NZ, :]
        return jnp.where(row8 == 7, flux, 0.0) / top

    def all_sum(step, moments, meanwhile):
        lane = lax.broadcasted_iota(jnp.int32, (1, NY), 1)
        row = jnp.zeros((1, NY), jnp.float32)
        for n, m in enumerate(moments):
            row = jnp.where(lane == n, jnp.sum(m, keepdims=True), row)
        for phase, (ring, slots, me) in enumerate(
            ((px_ring, red_px, place.px), (py_ring, red_py, place.py))
        ):
            source = red_src.at[step, phase]
            source[...] = row
            for device in ring:
                pltpu.make_async_remote_copy(
                    src_ref=source,
                    dst_ref=slots.at[step, me],
                    send_sem=red_send.at[step, phase],
                    recv_sem=red_recv.at[step, phase],
                    device_id=device,
                    device_id_type=MESH,
                ).start()
            slots[step, me] = row
            meanwhile[phase]()
            most = slots.at[step, pl.ds(0, len(ring))]
            pltpu.make_async_copy(most, most, red_recv.at[step, phase]).wait()
            parts = [slots[step, n] for n in range(len(ring) + 1)]
            while len(parts) > 1:
                parts = [a + b for a, b in zip(parts[::2], parts[1::2])]
            row = parts[0]
        return [
            jnp.sum(jnp.where(lane == n, row, 0.0), axis=1, keepdims=True)
            for n in range(len(moments))
        ]

    def folded(v):
        return v[0:8] + v[8:16] + v[16:24]

    frame_bytes(0, beam_recv).wait()

    def add_flux(x, pack):
        tile = flux_tile(0, x)
        fd_ref[0, x + 2] = tile
        z_ref[x + 2, NZ - 8 : NZ, :] = z_ref[x + 2, NZ - 8 : NZ, :] + tile
        return packed_into(pack, tile, x)

    z_near[2, NZ - 8 : NZ] = z_near[2, NZ - 8 : NZ] + slabs_loop(add_flux, zero_row())
    z_swap.pack[0] = z_near[2]
    z_swap.start(*z_edges)
    e_swap.start(*e_edges)
    z_swap.arrive(*z_edges)
    for at, slab in zip(GHOSTS, z_swap.slabs(0)):
        z_ref[at] = slab
    z_near[0], z_near[1] = z_swap.halo(0), z_swap.corner(0)

    def later_fluxes():
        frame_bytes(1, beam_recv).wait()
        frame_bytes(2, beam_recv).wait()

        def next_flux(x, packs):
            second, third = flux_tile(1, x), flux_tile(2, x)
            third = third - second
            second = second - fd_ref[0, x + 2]
            fd_ref[1, x + 2] = second
            fd_ref[2, x + 2] = third
            return packed_into(packs[0], second, x), packed_into(packs[1], third, x)

        packs = slabs_loop(next_flux, (zero_row(),) * 2)
        f_swap.pack[0], f_swap.pack[1] = packs
        f_swap.start(*f_edges)

    def one_step(step, nothing):
        swap = PairExchange(place, [ref.at[step] for ref in uv_refs])
        more = step + 1 < STEPS
        z_halo, z_corner = z_near[0], z_near[1]
        u_ref[1] = apply_slab(z_ref, 1, side_tile(z_corner, 0), g_ref, 0)
        u_ref[NX + 2] = apply_slab(z_ref, NX + 2, side_tile(z_corner, NX - 1), g_ref, NX + 1)
        u_halo = apply_halo(z_halo, z_corner, z_near[2], gp_ref)

        def first_image(x, carry):
            sums, pack = carry
            u = apply_slab(z_ref, x + 2, side_tile(z_halo, x), g_ref, x + 1)
            u_ref[x + 2] = u
            z = z_ref[x + 2]
            dz = d_ref[x] * z
            du = d_ref[x] * u
            sums = (
                sums[0] + folded(dz * z),
                sums[1] + folded(dz * u),
                sums[2] + folded(du * u),
            )
            return sums, packed_into(pack, u, x)

        sums, u_pack = slabs_loop(first_image, ((zero_row(),) * 3, zero))

        def second_image(x, carry):
            acc, pack = carry
            v = apply_slab(u_ref, x + 2, side_tile(u_halo, x), g_ref, x + 1)
            v_ref[x + 2] = v
            acc = acc + folded(d_ref[x] * u_ref[x + 2] * v)
            return acc, packed_into(pack, v, x)

        last, v_pack = slabs_loop(second_image, (zero_row(), zero))

        def send_images():
            @pl.when(more)
            def _():
                swap.fill(u_pack, v_pack)
                swap.start(*uv_edges)

            @pl.when(step == 0)
            def _():
                later_fluxes()

        def receive_images():
            @pl.when(step == 0)
            def _():
                z_swap.sent(*z_edges)
                e_swap.arrive(*e_edges)
                for at, slab in zip(GHOSTS, e_swap.slabs(0)):
                    e_ref[at] = slab
                f_swap.arrive(*f_edges)
                for n in range(2):
                    for at, slab in zip(GHOSTS, f_swap.slabs(n)):
                        fd_ref[1 + n, at] = slab
                e_near[0], e_near[1] = e_swap.halo(0), e_swap.corner(0)
                for n in range(2):
                    f_near[n, 0], f_near[n, 1] = f_swap.halo(n), f_swap.corner(n)

            @pl.when(more)
            def _():
                swap.arrive(*uv_edges)
                for n in range(2):
                    uv_near[n, 0], uv_near[n, 1] = swap.halo(n), swap.corner(n)

        g0, a, w, t, far = all_sum(
            step, list(sums) + [last, bad], (send_images, receive_images)
        )
        flag_out[0] = jnp.where(jnp.sum(far) > 0.0, 1, 0).astype(jnp.int32)
        inverse = 1.0 / (a * t - w * w)
        d1 = jnp.broadcast_to((g0 * t - a * w) * inverse, (NZ, NY))
        d2 = jnp.broadcast_to((a * a - g0 * w) * inverse, (NZ, NY))

        def next_z(z, u, v, e, tile):
            z = z - d1 * u - d2 * v + e * (d1 * z + d2 * u)
            return jnp.concatenate([z[: NZ - 8], z[NZ - 8 :] + tile], axis=0)

        @pl.when(more)
        def _():
            for at, u, v in zip(GHOSTS, swap.slabs(0), swap.slabs(1)):
                z_ref[at] = next_z(z_ref[at], u, v, e_ref[at], fd_ref[step + 1, at])
            for n in range(2):
                z_near[n] = next_z(z_near[n], uv_near[0, n], uv_near[1, n], e_near[n], f_near[step, n])

            def update(x, pack):
                z, u, v = z_ref[x + 2], u_ref[x + 2], v_ref[x + 2]
                x_ref[x] = x_ref[x] + (d1 * z + d2 * u)
                z = next_z(z, u, v, e_ref[x + 2], fd_ref[step + 1, x + 2])
                z_ref[x + 2] = z
                return packed_into(pack, z, x)

            z_near[2] = slabs_loop(update, zero)
            swap.sent(*uv_edges)

        @pl.when(not more)
        def _():
            def finish(x, carry):
                z, u, v = z_ref[x + 2], u_ref[x + 2], v_ref[x + 2]
                x_out[pl.ds(x, NZ, stride=NX), :] = x_ref[x] + (d1 * z + d2 * u)
                r_out[pl.ds(x, NZ, stride=NX), :] = d_ref[x] * (z - d1 * u - d2 * v)
                return carry

            slabs_loop(finish, 0)

        return nothing

    for step in range(STEPS):
        one_step(step, 0)
    e_swap.sent(*e_edges)
    f_swap.sent(*f_edges)
    for frame in range(STEPS):
        frame_bytes(frame, beam_send).wait()
    for step in range(STEPS):
        for phase, (slots, count) in enumerate(((red_px, NPX - 1), (red_py, NPY - 1))):
            most = slots.at[step, pl.ds(0, count)]
            pltpu.make_async_copy(most, most, red_send.at[step, phase]).wait()


def exchange_scratch(fields, rows):
    f32 = jnp.float32
    return [
        pltpu.VMEM((2, fields, 2, rows, NY), f32),
        pltpu.VMEM((2, fields, rows, NY), f32),
        pltpu.VMEM((4, fields, rows, NY), f32),
        pltpu.VMEM((fields, rows, NY), f32),
        pltpu.SemaphoreType.DMA((8,)),
        pltpu.SemaphoreType.DMA((8,)),
    ]


def hand_on(a_in, b_in, a_out, b_out, sem):
    copies = [
        pltpu.make_async_copy(src, dst, sem.at[n])
        for n, (src, dst) in enumerate(((a_in, a_out), (b_in, b_out)))
    ]
    for copy in copies:
        copy.start()
    for copy in copies:
        copy.wait()


def handed_on(a, b):
    space = pl.BlockSpec(memory_space=pl.ANY)
    return pl.pallas_call(
        hand_on,
        out_shape=(jax.ShapeDtypeStruct(a.shape, a.dtype), jax.ShapeDtypeStruct(b.shape, b.dtype)),
        in_specs=[space, space],
        out_specs=(space, space),
        scratch_shapes=[pltpu.SemaphoreType.DMA((2,))],
    )(a, b)


def body(
    incident_power_density,
    coupling_patch_locator,
    coupling_share_factor,
    starting_warmth,
    diffusive_coefficient,
    thermal_storage,
):
    f32 = jnp.float32
    flat = (NZ * NX, NY)
    hbm = pl.BlockSpec(memory_space=pl.ANY)
    vmem = pl.BlockSpec(memory_space=pltpu.VMEM)
    scratch = [
        pltpu.VMEM(flat, f32),
        pltpu.VMEM(flat, f32),
        pltpu.VMEM(flat, f32),
        pltpu.VMEM((CORR, NX, NY), jnp.int32),
        pltpu.VMEM((CORR, NX, NY), f32),
        pltpu.VMEM((STEPS, BR * NPY, NY), f32),
        pltpu.VMEM((6, NX, 8, NY), f32),
        pltpu.VMEM((3, NX + 4, NZ, NY), f32),
        pltpu.VMEM((NX + 4, NZ, NY), f32),
        pltpu.VMEM((2, NX + 4, NZ, NY), f32),
        pltpu.VMEM((NX, NZ, NY), f32),
        pltpu.VMEM((6, NX + 2, NZ, NY), f32),
        pltpu.VMEM((6, NZ, NY), f32),
        pltpu.VMEM((NX, NZ, NY), f32),
        pltpu.VMEM((NX + 4, NZ, NY), f32),
        pltpu.VMEM((STEPS, NX + 4, 8, NY), f32),
        pltpu.VMEM((3, NZ, NY), f32),
        pltpu.VMEM((2, NZ, NY), f32),
        pltpu.VMEM((2, 2, 8, NY), f32),
        pltpu.VMEM((2, 2, NZ, NY), f32),
        pltpu.VMEM((STEPS, 2, 1, NY), f32),
        pltpu.VMEM((STEPS, NPX, 1, NY), f32),
        pltpu.VMEM((STEPS, NPY, 1, NY), f32),
        pltpu.SemaphoreType.DMA((6,)),
        pltpu.SemaphoreType.DMA((STEPS,)),
        pltpu.SemaphoreType.DMA((STEPS,)),
        pltpu.SemaphoreType.DMA((STEPS, 2)),
        pltpu.SemaphoreType.DMA((STEPS, 2)),
    ]
    for fields, rows in EXCHANGES:
        scratch += exchange_scratch(fields, rows)
    scratch += [
        pltpu.VMEM((2, 4, NZ, NY), f32),
        pltpu.VMEM((2, NZ, NY), f32),
        pltpu.VMEM((4, NZ, NY), f32),
        pltpu.VMEM((2, NZ, NY), f32),
        pltpu.SemaphoreType.DMA((8,)),
        pltpu.SemaphoreType.DMA((8,)),
        pltpu.VMEM((2, 4, NZ, NY), f32),
        pltpu.VMEM((STEPS - 1, 2, 2, 2, NZ, NY), f32),
        pltpu.VMEM((STEPS - 1, 2, NZ, NY), f32),
        pltpu.VMEM((STEPS - 1, 4, NZ, NY), f32),
        pltpu.VMEM((STEPS - 1, 2, NZ, NY), f32),
        pltpu.SemaphoreType.DMA((STEPS - 1, 8)),
        pltpu.SemaphoreType.DMA((STEPS - 1, 8)),
    ]
    warmth, leftover, flag = pl.pallas_call(
        kernel,
        out_shape=(
            jax.ShapeDtypeStruct(flat, f32),
            jax.ShapeDtypeStruct(flat, f32),
            jax.ShapeDtypeStruct((1,), jnp.int32),
        ),
        in_specs=[hbm] * 6,
        out_specs=(vmem, vmem, pl.BlockSpec(memory_space=pltpu.SMEM)),
        scratch_shapes=scratch,
        compiler_params=pltpu.CompilerParams(
            collective_id=0, has_side_effects=True, vmem_limit_bytes=40 * 2**20
        ),
    )(
        incident_power_density,
        coupling_patch_locator,
        coupling_share_factor,
        starting_warmth.reshape(flat),
        diffusive_coefficient.reshape(flat),
        thermal_storage.reshape(flat),
    )
    shape = starting_warmth.shape
    out = lax.cond(
        flag[0] > 0,
        lambda: list(
            general(
                incident_power_density,
                coupling_patch_locator,
                coupling_share_factor,
                starting_warmth,
                diffusive_coefficient,
                thermal_storage,
            )
        ),
        lambda: [out.reshape(shape) for out in handed_on(warmth, leftover)],
    )
    return tuple(out)


def solution(mesh):
    placed = (
        P(None, ("px", "py"), None),
        P(None, "px", "py"),
        P(None, "px", "py"),
        P(None, "px", "py"),
        P(None, "px", "py"),
        P(None, "px", "py"),
    )
    return jax.shard_map(
        body,
        mesh=mesh,
        in_specs=placed,
        out_specs=(P(None, "px", "py"), P(None, "px", "py")),
        check_vma=False,
    )
```

```python
import functools

import jax
import jax.numpy as jnp
from jax import lax
from jax.experimental import pallas as pl
from jax.experimental.pallas import tpu as pltpu
from jax.sharding import PartitionSpec as P

ITERS = 2
MESH = pl.DeviceIdType.MESH

NZ = 24
NX = 32
NY = 128
NPX = 8
NPY = 16
BR = 16
STEPS = 3
CORR = 8
UNROLL = 8


through_ratio = 0.5


def extended(block, sides, width):
    for axis, dim in sides:
        count = lax.axis_size(axis)
        forward = [(i, i + 1) for i in range(count - 1)]
        backward = [(target, source) for source, target in forward]
        low = lax.ppermute(
            lax.slice_in_dim(block, block.shape[dim] - width, None, axis=dim), axis, forward
        )
        high = lax.ppermute(lax.slice_in_dim(block, 0, width, axis=dim), axis, backward)
        block = jnp.concatenate([low, block, high], axis=dim)
    return block


def with_rim(field):
    rimmed = extended(field, (("px", 1), ("py", 2)), 1)
    return jnp.pad(rimmed, ((1, 1), (0, 0), (0, 0)))


def stencil(padded, field, faces, diagonal):
    beside = faces[0] * padded[:-2, 1:-1, 1:-1] + faces[1] * padded[2:, 1:-1, 1:-1]
    beside = beside + faces[2] * padded[1:-1, :-2, 1:-1] + faces[3] * padded[1:-1, 2:, 1:-1]
    beside = beside + faces[4] * padded[1:-1, 1:-1, :-2] + faces[5] * padded[1:-1, 1:-1, 2:]
    return diagonal * field - beside


def operate(field, faces, diagonal):
    return stencil(with_rim(field), field, faces, diagonal)


def face_terms(centre, padded):
    return (
        through_ratio * 0.5 * (centre + padded[:-2, 1:-1, 1:-1]),
        through_ratio * 0.5 * (centre + padded[2:, 1:-1, 1:-1]),
        0.5 * (centre + padded[1:-1, :-2, 1:-1]),
        0.5 * (centre + padded[1:-1, 2:, 1:-1]),
        0.5 * (centre + padded[1:-1, 1:-1, :-2]),
        0.5 * (centre + padded[1:-1, 1:-1, 2:]),
    )


def surface_flux(window, coupling_patch_locator, coupling_share_factor):
    flat = window.reshape(-1)
    values = flat[coupling_patch_locator]
    return jnp.sum(coupling_share_factor * values, axis=0)


def total(a, b):
    return lax.psum(jnp.sum(a * b), ("px", "py"))


def solve_step(solution, leftover_error_vector, faces, diagonal):
    scaled = leftover_error_vector / diagonal
    axis_direction = scaled
    gamma = total(leftover_error_vector, scaled)
    for turn in range(ITERS):
        image = operate(axis_direction, faces, diagonal)
        alpha = gamma / total(axis_direction, image)
        solution = solution + alpha * axis_direction
        leftover_error_vector = leftover_error_vector - alpha * image
        if turn + 1 < ITERS:
            scaled = leftover_error_vector / diagonal
            fresh = total(leftover_error_vector, scaled)
            axis_direction = scaled + fresh / gamma * axis_direction
            gamma = fresh
    return (solution, leftover_error_vector)


def general(
    incident_power_density,
    coupling_patch_locator,
    coupling_share_factor,
    starting_warmth,
    diffusive_coefficient,
    thermal_storage,
):
    sheet_level = starting_warmth.shape[0]
    rimmed = extended(diffusive_coefficient, (("px", 1), ("py", 2)), 1)
    padded = jnp.pad(rimmed, ((1, 1), (0, 0), (0, 0)))
    faces = face_terms(diffusive_coefficient, padded)
    diagonal = thermal_storage + faces[0] + faces[1] + faces[2] + faces[3] + faces[4] + faces[5]
    frames = incident_power_density.shape[0]
    final_warmth = starting_warmth
    leftover_error_vector = starting_warmth
    for frame in range(frames):
        window = lax.all_to_all(
            incident_power_density[frame : frame + 1], "py", split_axis=2, concat_axis=1, tiled=True
        )[0]
        flux = surface_flux(window, coupling_patch_locator, coupling_share_factor)
        right = thermal_storage * final_warmth
        right = right.at[sheet_level - 1].add(flux)
        leftover_error_vector = right - operate(final_warmth, faces, diagonal)
        final_warmth, leftover_error_vector = solve_step(
            final_warmth, leftover_error_vector, faces, diagonal
        )
    return (final_warmth, leftover_error_vector)


def lanes(rows=NZ):
    return lax.broadcasted_iota(jnp.int32, (rows, NY), 1)


def rolled(v, shift, axis=1):
    return pltpu.roll(v, shift % v.shape[axis], axis)


def slabs_loop(fn, init, step=UNROLL):
    def some(n, carry):
        for q in range(step):
            carry = fn(n * step + q, carry)
        return carry

    return lax.fori_loop(0, NX // step, some, init)


def side_tile(packed, x):
    return pltpu.roll(packed, lax.rem(638 - 4 * x, 128), 1)


def lateral(v, side):
    lane = lanes(v.shape[0])
    left = jnp.where(lane == 0, side, rolled(v, 1))
    right = jnp.where(lane == NY - 1, side, rolled(v, -1))
    return left, right


def apply_slab(ref, i, side, g_ref, gi):
    v = ref[i]
    left, right = lateral(v, side)
    out = g_ref[0, gi] * rolled(v, 1, 0) + g_ref[1, gi] * rolled(v, -1, 0)
    out = out + (g_ref[2, gi] * ref[i - 1] + g_ref[3, gi] * ref[i + 1])
    out = out + (g_ref[4, gi] * left + g_ref[5, gi] * right)
    return v - out


def around_halo(halo, corner, pack):
    lane = lanes()
    j = lax.rem(lane, 4)
    below = jnp.where(lane < 4, corner, rolled(halo, 4))
    above = jnp.where(lane >= NY - 4, corner, rolled(halo, -4))
    outer = jnp.where(j == 1, rolled(halo, 1), rolled(halo, -1))
    return below, above, pack, outer


def apply_halo(halo, corner, pack, gp_ref):
    below, above, inner, outer = around_halo(halo, corner, pack)
    out = gp_ref[0] * rolled(halo, 1, 0) + gp_ref[1] * rolled(halo, -1, 0)
    out = out + gp_ref[2] * below + gp_ref[3] * above + gp_ref[4] * inner + gp_ref[5] * outer
    return halo - out


class Place:
    def __init__(self):
        self.px = lax.axis_index("px")
        self.py = lax.axis_index("py")
        self.has_low = jnp.where(self.px > 0, 1.0, 0.0).astype(jnp.float32)
        self.has_high = jnp.where(self.px < NPX - 1, 1.0, 0.0).astype(jnp.float32)
        self.has_left = jnp.where(self.py > 0, 1.0, 0.0).astype(jnp.float32)
        self.has_right = jnp.where(self.py < NPY - 1, 1.0, 0.0).astype(jnp.float32)

    def at(self, dx, dy):
        return (lax.rem(self.px + dx + NPX, NPX), lax.rem(self.py + dy + NPY, NPY))


GHOSTS = (0, 1, NX + 2, NX + 3)
EXCHANGES = ((1, 8), (2, 8))
CORNERS = ((-1, 1), (-1, -1), (1, 1), (1, -1))


class Exchange:
    def __init__(self, place, refs):
        self.place = place
        self.rx, self.rs, self.rk, self.pack, self.send, self.recv = refs

    def plan(self, low, high):
        to_right, to_left = self.packs()
        plan = []
        for n, (dx, dy) in enumerate(CORNERS):
            plan.append((to_left if dy > 0 else to_right, self.rk.at[n], (-dx, -dy)))
        plan.append((to_right, self.rs.at[0], (0, 1)))
        plan.append((to_left, self.rs.at[1], (0, -1)))
        single = len(low.shape) + 2 == len(self.rx.shape)
        for n, (src, dx) in enumerate(((high, 1), (low, -1))):
            plan.append((src, self.rx.at[n, 0] if single else self.rx.at[n], (dx, 0)))
        return [
            pltpu.make_async_remote_copy(
                src_ref=src,
                dst_ref=dst,
                send_sem=self.send.at[n],
                recv_sem=self.recv.at[n],
                device_id=self.place.at(dx, dy),
                device_id_type=MESH,
            )
            for n, (src, dst, (dx, dy)) in enumerate(plan)
        ]

    def packs(self):
        return self.pack, self.pack

    def start(self, *edges):
        for copy in self.plan(*edges):
            copy.start()

    def arrive(self, *edges):
        for copy in self.plan(*edges):
            copy.wait_recv()

    def sent(self, *edges):
        for copy in self.plan(*edges):
            copy.wait_send()

    def slabs(self, field):
        p = self.place
        return (
            self.rx[0, field, 0] * p.has_low,
            self.rx[0, field, 1] * p.has_low,
            self.rx[1, field, 0] * p.has_high,
            self.rx[1, field, 1] * p.has_high,
        )

    def sides(self, field):
        return self.rs[0, field], self.rs[1, field], (-3, -1, 1, 3)

    def corners(self, field):
        return [self.rk[n, field] for n in range(4)], (3, 5, -5, -3)

    def halo(self, field):
        p = self.place
        left, right, shifts = self.sides(field)
        left, right = left * p.has_left, right * p.has_right
        j = lax.rem(lanes(left.shape[0]), 4)
        far = jnp.where(j == 0, rolled(right, shifts[0]), rolled(left, shifts[3]))
        near = jnp.where(j == 1, rolled(right, shifts[1]), rolled(left, shifts[2]))
        return jnp.where((j == 1) | (j == 2), near, far)

    def corner(self, field):
        p = self.place
        tiles, shifts = self.corners(field)
        masks = (
            p.has_low * p.has_right,
            p.has_low * p.has_left,
            p.has_high * p.has_right,
            p.has_high * p.has_left,
        )
        lane = lanes(tiles[0].shape[0])
        out = jnp.zeros_like(tiles[0])
        for at, tile, mask, shift in zip((1, 2, NY - 3, NY - 2), tiles, masks, shifts):
            out = jnp.where(lane == at, rolled(tile * mask, shift), out)
        return out


class PairExchange(Exchange):
    def packs(self):
        return self.pack.at[0], self.pack.at[1]

    def fill(self, first, second):
        j = lax.rem(lanes(), 4)
        self.pack[0] = jnp.where(j < 2, first, rolled(second, 2))
        self.pack[1] = jnp.where(j < 2, rolled(first, -2), second)

    def sides(self, field):
        return self.rs[0], self.rs[1], ((-3, -1, -1, 1) if field else (-1, 1, 1, 3))

    def corners(self, field):
        return [self.rk[n] for n in range(4)], ((3, 3, -5, -5) if field else (5, 5, -3, -3))


class FirstExchange(PairExchange):
    def fill(self, k, c, t):
        j = lax.rem(lanes(), 4)
        right = jnp.where(j == 2, rolled(c, 1), rolled(t, 2))
        left = jnp.where(j == 2, c, rolled(t, 1))
        self.pack[0] = jnp.where(j < 2, k, right)
        self.pack[1] = jnp.where(j < 2, rolled(k, -2), left)

    def sides(self, field):
        return self.rs[0], self.rs[1], ((-1, 1, 1, 3), (0, -1, 0, 0), (0, -2, -1, 0))[field]


def packed_into(pack, v, x):
    lane = lanes(v.shape[0])
    return jnp.where(lane // 4 == x, pltpu.roll(v, lax.rem(4 * x + 2, NY), 1), pack)


HOPS = sorted(
    ((dz, dy) for dz in range(4) for dy in range(4) if dz or dy),
    key=lambda t: -(min(t[0], 4 - t[0]) + min(t[1], 4 - t[1])),
)


def ring_targets(place):
    x, core = place.px // 2, lax.rem(place.px, 2)
    z, y = place.py // 4, lax.rem(place.py, 4)
    px = []
    for dx, dc in ((2, 1), (2, 0), (1, 1), (1, 0), (3, 1), (3, 0), (0, 1)):
        px.append((lax.rem(x + dx, 4) * 2 + lax.rem(core + dc, 2), place.py))
    py = []
    for dz, dy in HOPS:
        py.append((place.px, lax.rem(z + dz, 4) * 4 + lax.rem(y + dy, 4)))
    return px, py


def kernel(
    beam,
    loc_in,
    share_in,
    t_in,
    k_in,
    c_in,
    x_out,
    r_out,
    flag_out,
    kraw,
    craw,
    traw,
    loc,
    share,
    window,
    weights,
    kct,
    z_ref,
    uv_ref,
    x_ref,
    g_ref,
    gp_ref,
    d_ref,
    e_ref,
    fd_ref,
    z_near,
    e_near,
    f_near,
    uv_near,
    red_src,
    red_px,
    red_py,
    local_sem,
    beam_send,
    beam_recv,
    red_send,
    red_recv,
    *exchange_refs,
):
    place = Place()
    u_ref, v_ref = uv_ref.at[0], uv_ref.at[1]
    px_ring, py_ring = ring_targets(place)
    diagonal_devices = [place.at(dx, dy) for dx, dy in CORNERS]

    local = [
        pltpu.make_async_copy(src, dst, local_sem.at[n])
        for n, (src, dst) in enumerate(
            (
                (k_in, kraw),
                (c_in, craw),
                (t_in, traw),
                (loc_in, loc),
                (share_in, share),
            )
        )
    ]
    for copy in local:
        copy.start()
    own_columns = pl.ds(pl.multiple_of(place.py * NY, NY), NY)
    own_rows = pl.ds(pl.multiple_of(place.py * BR, BR), BR)
    own_beam = pltpu.make_async_copy(
        beam.at[:, :, own_columns], window.at[:, own_rows, :], local_sem.at[5]
    )
    own_beam.start()

    barrier = pltpu.get_barrier_semaphore()
    everyone = py_ring + px_ring + diagonal_devices
    for device in everyone:
        pl.semaphore_signal(barrier, inc=1, device_id=device, device_id_type=MESH)

    exchanges = [
        Exchange(place, exchange_refs[6 * n : 6 * n + 6]) for n in range(len(EXCHANGES))
    ]
    tile_swap, f_swap = exchanges
    ze_swap = PairExchange(place, exchange_refs[-20:-14])
    ze_edge = exchange_refs[-14]
    first = FirstExchange(place, exchange_refs[-13:-7])
    k_edge = exchange_refs[-7]
    uv_refs = exchange_refs[-6:]
    k_edges = k_edge.at[0], k_edge.at[1]
    tile_edges = fd_ref.at[0, pl.ds(2, 2)], fd_ref.at[0, pl.ds(NX, 2)]
    ze_edges = ze_edge.at[0], ze_edge.at[1]
    f_edges = fd_ref.at[pl.ds(1, 2), pl.ds(2, 2)], fd_ref.at[pl.ds(1, 2), pl.ds(NX, 2)]
    uv_edges = uv_ref.at[:, pl.ds(2, 2)], uv_ref.at[:, pl.ds(NX, 2)]

    for copy in local[:3]:
        copy.wait()
    zero = jnp.zeros((NZ, NY), jnp.float32)

    def folded(v):
        return v[0:8] + v[8:16] + v[16:24]

    def zero_row():
        return jnp.zeros((8, NY), jnp.float32)

    def lay(x, packs):
        out = []
        for n, raw in enumerate((kraw, craw, traw)):
            v = raw[pl.ds(x, NZ, stride=NX), :]
            kct[n, x + 2] = v
            out.append(packed_into(packs[n], v, x))
        return tuple(out)

    packs = slabs_loop(lay, (zero, zero, zero))
    k_pack, c_pack, t_pack = packs
    first.fill(*packs)
    edges = ((0, 0, NX - 2), (0, 1, NX - 1), (1, 0, NX - 1), (2, 0, NX - 1))
    for n, (field, low, high) in enumerate(edges):
        k_edge[0, n] = kct[field, low + 2]
        k_edge[1, n] = kct[field, high + 2]

    local[3].wait()
    local[4].wait()
    row8 = lax.broadcasted_iota(jnp.int32, (8, NY), 0)
    lane8 = lax.broadcasted_iota(jnp.int32, (8, NY), 1)
    beyond = jnp.where(row8 == 7, -1, jnp.where(row8 == 0, 8, -1000))

    def weigh(x, bad):
        own = [jnp.zeros((8, NY), jnp.float32) for _ in range(3)]
        edge = [jnp.zeros((8, NY), jnp.float32) for _ in range(3)]
        for k in range(CORR):
            index = jnp.broadcast_to(loc[k, pl.ds(x, 1), :], (8, NY))
            part = jnp.broadcast_to(share[k, pl.ds(x, 1), :], (8, NY))
            row = lax.shift_right_arithmetic(index, 7) - 8 * x
            col = lax.bitwise_and(index, 127) - lane8
            far = (row < -1) | (row > 8) | (col < -1) | (col > 1)
            bad = bad + jnp.where(far, 1.0, 0.0)
            inside = jnp.where(row == row8, part, 0.0)
            outside = jnp.where(row == beyond, part, 0.0)
            for n in range(3):
                here = col == n - 1
                own[n] = own[n] + jnp.where(here, inside, 0.0)
                edge[n] = edge[n] + jnp.where(here, outside, 0.0)
        for n in range(3):
            weights[n, x] = own[n]
            weights[3 + n, x] = edge[n]
        return bad

    bad = slabs_loop(weigh, jnp.zeros((8, NY), jnp.float32))

    pl.semaphore_wait(barrier, len(everyone))

    def send_frame(frame):
        def send_block(n, nothing):
            n = jnp.where(n < 10, n, n + 1)
            device = (
                place.px,
                lax.rem(place.py // 4 + 2 + n // 4, 4) * 4 + lax.rem(lax.rem(place.py, 4) + 2 + lax.rem(n, 4), 4),
            )
            columns = pl.ds(pl.multiple_of(device[1] * NY, NY), NY)
            copy = pltpu.make_async_remote_copy(
                src_ref=beam.at[frame, :, columns],
                dst_ref=window.at[frame, own_rows, :],
                send_sem=beam_send.at[frame],
                recv_sem=beam_recv.at[frame],
                device_id=device,
                device_id_type=MESH,
            )
            copy.start()
            return nothing

        lax.fori_loop(0, NPY - 1, send_block, 0)

    def frame_bytes(frame, sem):
        most = window.at[frame, pl.ds(0, (NPY - 1) * BR), :]
        return pltpu.make_async_copy(most, most, sem.at[frame])

    first.start(*k_edges)
    send_frame(0)
    for frame in range(1, STEPS):
        send_frame(frame)

    first.arrive(*k_edges)
    for n, (field, low, high) in enumerate(edges):
        kct[field, high + 2 - NX] = first.rx[0, n] * place.has_low
        kct[field, low + 2 + NX] = first.rx[1, n] * place.has_high
    k_halo, k_corner = first.halo(0), first.corner(0)
    c_halo, t_halo = first.halo(1), first.halo(2)
    c_halo = jnp.where((lax.rem(lanes(), 4) + 1) // 2 == 1, c_halo, 0.0)
    level = lax.broadcasted_iota(jnp.int32, (NZ, NY), 0)

    def over(k, up, down, below, above, left, right, storage, mask):
        bottom, top = level == 0, level == NZ - 1
        up = jnp.where(bottom, 0.0, up)
        down = jnp.where(top, 0.0, down)
        faces = [0.25 * (k + up), 0.25 * (k + down)]
        faces += [0.5 * (k + other) for other in (below, above, left, right)]
        diagonal = storage + (
            (faces[0] + faces[1]) + (faces[2] + faces[3]) + (faces[4] + faces[5])
        )
        inverse = mask / diagonal
        faces[0] = jnp.where(bottom, 0.0, faces[0])
        faces[1] = jnp.where(top, 0.0, faces[1])
        return [face * inverse for face in faces], diagonal, inverse

    def conduct(x, side, mask):
        i = x + 2
        k = kct[0, i]
        left, right = lateral(k, side)
        g, diagonal, inverse = over(
            k,
            rolled(k, 1, 0),
            rolled(k, -1, 0),
            kct[0, i - 1],
            kct[0, i + 1],
            left,
            right,
            kct[1, i],
            mask,
        )
        for n in range(6):
            g_ref[n, x + 1] = g[n]
        return diagonal, inverse

    conduct(-1, side_tile(k_corner, 0), place.has_low)
    conduct(NX, side_tile(k_corner, NX - 1), place.has_high)

    def conduct_inside(x, pack):
        diagonal, inverse = conduct(x, side_tile(k_halo, x), 1.0)
        d_ref[x] = diagonal
        e = kct[1, x + 2] * inverse
        e_ref[x + 2] = e
        return packed_into(pack, e, x)

    e_pack = slabs_loop(conduct_inside, zero)

    below, above, inner, outer = around_halo(k_halo, k_corner, k_pack)
    j = lax.rem(lanes(), 4)
    halo_mask = jnp.where(j < 2, place.has_right, place.has_left)
    halo_mask = jnp.where((j == 1) | (j == 2), halo_mask, 0.0)
    gp, _, _ = over(
        k_halo,
        rolled(k_halo, 1, 0),
        rolled(k_halo, -1, 0),
        below,
        above,
        inner,
        outer,
        c_halo + jnp.where(halo_mask > 0.0, 0.0, 1.0),
        halo_mask,
    )
    for n in range(6):
        gp_ref[n] = gp[n]

    t_ref = kct.at[2]

    def residual(x, carry):
        image = apply_slab(t_ref, x + 2, side_tile(t_halo, x), g_ref, x + 1)
        t = t_ref[x + 2]
        z = e_ref[x + 2] * t - image
        z_ref[x + 2] = z
        x_ref[x] = t
        return packed_into(carry, z, x)

    z_pack = slabs_loop(residual, zero)
    z_near[2] = z_pack
    ze_swap.fill(z_pack, e_pack)
    for n in range(2):
        for m, ref in enumerate((z_ref, e_ref)):
            ze_edge[0, m, n] = ref[2 + n]
            ze_edge[1, m, n] = ref[NX + n]
    ze_swap.start(*ze_edges)
    first.sent(*k_edges)

    own_beam.wait()

    def flux_tile(frame, x):
        def rows(i):
            return window[frame, pl.ds(pl.multiple_of(i * 8, 8), 8), :]

        mine = rows(x)
        around = jnp.where(
            row8 == 7, rows(jnp.maximum(x - 1, 0)), rows(jnp.minimum(x + 1, NX - 1))
        )
        part = weights[1, x] * mine + weights[4, x] * around
        part = part + weights[0, x] * rolled(mine, 1) + weights[3, x] * rolled(around, 1)
        part = part + weights[2, x] * rolled(mine, -1) + weights[5, x] * rolled(around, -1)
        flux = jnp.sum(part, axis=0, keepdims=True)
        top = d_ref[x, NZ - 8 : NZ, :]
        return jnp.where(row8 == 7, flux, 0.0) / top

    def all_sum(step, moments, meanwhile):
        lane = lax.broadcasted_iota(jnp.int32, (1, NY), 1)
        row = jnp.zeros((1, NY), jnp.float32)
        for n, m in enumerate(moments):
            row = jnp.where(lane == n, jnp.sum(m, keepdims=True), row)
        for phase, (ring, slots, me) in enumerate(
            ((px_ring, red_px, place.px), (py_ring, red_py, place.py))
        ):
            source = red_src.at[step, phase]
            source[...] = row
            for device in ring:
                pltpu.make_async_remote_copy(
                    src_ref=source,
                    dst_ref=slots.at[step, me],
                    send_sem=red_send.at[step, phase],
                    recv_sem=red_recv.at[step, phase],
                    device_id=device,
                    device_id_type=MESH,
                ).start()
            slots[step, me] = row
            meanwhile[phase]()
            most = slots.at[step, pl.ds(0, len(ring))]
            pltpu.make_async_copy(most, most, red_recv.at[step, phase]).wait()
            parts = [slots[step, n] for n in range(len(ring) + 1)]
            while len(parts) > 1:
                parts = [a + b for a, b in zip(parts[::2], parts[1::2])]
            row = parts[0]
        return [
            jnp.sum(jnp.where(lane == n, row, 0.0), axis=1, keepdims=True)
            for n in range(len(moments))
        ]

    frame_bytes(0, beam_recv).wait()

    def add_flux(x, pack):
        tile = flux_tile(0, x)
        fd_ref[0, x + 2] = tile
        z_ref[x + 2, NZ - 8 : NZ, :] = z_ref[x + 2, NZ - 8 : NZ, :] + tile
        return packed_into(pack, tile, x)

    top = pl.ds(NZ - 8, 8)
    tile_pack = slabs_loop(add_flux, zero_row())
    tile_swap.pack[0] = tile_pack
    tile_swap.start(*tile_edges)
    z_near[2, top] = z_near[2, top] + tile_pack
    ze_swap.arrive(*ze_edges)
    for at, z, e in zip(GHOSTS, ze_swap.slabs(0), ze_swap.slabs(1)):
        z_ref[at] = z
        e_ref[at] = e
    for near, n in ((z_near, 0), (e_near, 1)):
        near[0], near[1] = ze_swap.halo(n), ze_swap.corner(n)

    dry_halo = z_near[0]

    def early_image(x, carry):
        sums, pack = carry
        u = apply_slab(z_ref, x + 2, side_tile(dry_halo, x), g_ref, x + 1)
        u_ref[x + 2] = u
        z = z_ref[x + 2]
        dz = d_ref[x] * z
        zu, uu = dz * u, d_ref[x] * u * u
        sums = (
            sums[0] + folded(dz * z),
            sums[1] + (zu[0:8] + zu[8:16]),
            sums[2] + (uu[0:8] + uu[8:16]),
        )
        return sums, packed_into(pack, u, x)

    early_sums, early_pack = slabs_loop(early_image, ((zero_row(),) * 3, zero))
    tile_swap.arrive(*tile_edges)
    tiles = tile_swap.slabs(0)
    for at, tile in zip(GHOSTS, tiles):
        z_ref[at, top] = z_ref[at, top] + tile
    tile_halo = tile_swap.halo(0)
    for n, tile in enumerate((tile_halo, tile_swap.corner(0))):
        z_near[n, top] = z_near[n, top] + tile
    u_ref[2, top] = u_ref[2, top] - g_ref[2, 1, top] * tiles[1]
    u_ref[NX + 1, top] = u_ref[NX + 1, top] - g_ref[3, NX, top] * tiles[2]

    def late_image(x, carry):
        sums, pack = carry
        side = side_tile(tile_halo, x)
        near = jnp.where(lane8 == 0, g_ref[4, x + 1, top] * side, 0.0)
        near = jnp.where(lane8 == NY - 1, g_ref[5, x + 1, top] * side, near)
        u = u_ref[x + 2, top] - near
        u_ref[x + 2, top] = u
        du = d_ref[x, top] * u
        sums = (sums[0] + du * z_ref[x + 2, top], sums[1] + du * u)
        return sums, packed_into(pack, u, x)

    late_sums, late_pack = slabs_loop(late_image, (early_sums[1:], zero_row()))
    early_sums = (early_sums[0], *late_sums)
    early_pack = jnp.concatenate([early_pack[: NZ - 8], late_pack], axis=0)

    def later_fluxes():
        frame_bytes(1, beam_recv).wait()
        frame_bytes(2, beam_recv).wait()

        def next_flux(x, packs):
            second, third = flux_tile(1, x), flux_tile(2, x)
            third = third - second
            second = second - fd_ref[0, x + 2]
            fd_ref[1, x + 2] = second
            fd_ref[2, x + 2] = third
            return packed_into(packs[0], second, x), packed_into(packs[1], third, x)

        packs = slabs_loop(next_flux, (zero_row(),) * 2)
        f_swap.pack[0], f_swap.pack[1] = packs
        f_swap.start(*f_edges)

    def one_step(step, nothing):
        swap = PairExchange(place, [ref.at[step] for ref in uv_refs])
        more = step + 1 < STEPS
        z_halo, z_corner = z_near[0], z_near[1]
        u_ref[1] = apply_slab(z_ref, 1, side_tile(z_corner, 0), g_ref, 0)
        u_ref[NX + 2] = apply_slab(z_ref, NX + 2, side_tile(z_corner, NX - 1), g_ref, NX + 1)
        u_halo = apply_halo(z_halo, z_corner, z_near[2], gp_ref)

        def first_image(x, carry):
            sums, pack = carry
            u = apply_slab(z_ref, x + 2, side_tile(z_halo, x), g_ref, x + 1)
            u_ref[x + 2] = u
            z = z_ref[x + 2]
            dz = d_ref[x] * z
            du = d_ref[x] * u
            sums = (
                sums[0] + folded(dz * z),
                sums[1] + folded(dz * u),
                sums[2] + folded(du * u),
            )
            return sums, (packed_into(pack, u, x) if more else pack)

        if step == 0:
            sums, u_pack = early_sums, early_pack
        else:
            sums, u_pack = slabs_loop(first_image, ((zero_row(),) * 3, zero))

        def second_image(x, carry):
            acc, pack = carry
            v = apply_slab(u_ref, x + 2, side_tile(u_halo, x), g_ref, x + 1)
            v_ref[x + 2] = v
            acc = acc + folded(d_ref[x] * u_ref[x + 2] * v)
            return acc, (packed_into(pack, v, x) if more else pack)

        last, v_pack = slabs_loop(second_image, (zero_row(), zero))

        def send_images():
            @pl.when(more)
            def _():
                swap.fill(u_pack, v_pack)
                swap.start(*uv_edges)

            @pl.when(step == 0)
            def _():
                later_fluxes()

        def receive_images():
            @pl.when(step == 0)
            def _():
                ze_swap.sent(*ze_edges)
                tile_swap.sent(*tile_edges)
                f_swap.arrive(*f_edges)
                for n in range(2):
                    for at, slab in zip(GHOSTS, f_swap.slabs(n)):
                        fd_ref[1 + n, at] = slab
                for n in range(2):
                    f_near[n, 0], f_near[n, 1] = f_swap.halo(n), f_swap.corner(n)

            @pl.when(more)
            def _():
                swap.arrive(*uv_edges)
                for n in range(2):
                    uv_near[n, 0], uv_near[n, 1] = swap.halo(n), swap.corner(n)

        moments = list(sums) + [last] + ([bad] if step == 0 else [])
        g0, a, w, t, *far = all_sum(step, moments, (send_images, receive_images))
        if step == 0:
            flag_out[0] = jnp.where(jnp.sum(far[0]) > 0.0, 1, 0).astype(jnp.int32)
        inverse = 1.0 / (a * t - w * w)
        d1 = jnp.broadcast_to((g0 * t - a * w) * inverse, (NZ, NY))
        d2 = jnp.broadcast_to((a * a - g0 * w) * inverse, (NZ, NY))

        def next_z(z, u, v, e, tile):
            z = z - d1 * u - d2 * v + e * (d1 * z + d2 * u)
            return jnp.concatenate([z[: NZ - 8], z[NZ - 8 :] + tile], axis=0)

        @pl.when(more)
        def _():
            for at, u, v in zip(GHOSTS, swap.slabs(0), swap.slabs(1)):
                z_ref[at] = next_z(z_ref[at], u, v, e_ref[at], fd_ref[step + 1, at])
            for n in range(2):
                z_near[n] = next_z(z_near[n], uv_near[0, n], uv_near[1, n], e_near[n], f_near[step, n])

            def update(x, pack):
                z, u, v = z_ref[x + 2], u_ref[x + 2], v_ref[x + 2]
                x_ref[x] = x_ref[x] + (d1 * z + d2 * u)
                z = next_z(z, u, v, e_ref[x + 2], fd_ref[step + 1, x + 2])
                z_ref[x + 2] = z
                return packed_into(pack, z, x)

            z_near[2] = slabs_loop(update, zero)
            swap.sent(*uv_edges)

        @pl.when(not more)
        def _():
            def finish(x, carry):
                z, u, v = z_ref[x + 2], u_ref[x + 2], v_ref[x + 2]
                x_out[pl.ds(x, NZ, stride=NX), :] = x_ref[x] + (d1 * z + d2 * u)
                r_out[pl.ds(x, NZ, stride=NX), :] = d_ref[x] * (z - d1 * u - d2 * v)
                return carry

            slabs_loop(finish, 0)

        return nothing

    for step in range(STEPS):
        one_step(step, 0)
    f_swap.sent(*f_edges)
    for frame in range(STEPS):
        frame_bytes(frame, beam_send).wait()
    for step in range(STEPS):
        for phase, (slots, count) in enumerate(((red_px, NPX - 1), (red_py, NPY - 1))):
            most = slots.at[step, pl.ds(0, count)]
            pltpu.make_async_copy(most, most, red_send.at[step, phase]).wait()


def exchange_scratch(fields, rows):
    f32 = jnp.float32
    return [
        pltpu.VMEM((2, fields, 2, rows, NY), f32),
        pltpu.VMEM((2, fields, rows, NY), f32),
        pltpu.VMEM((4, fields, rows, NY), f32),
        pltpu.VMEM((fields, rows, NY), f32),
        pltpu.SemaphoreType.DMA((8,)),
        pltpu.SemaphoreType.DMA((8,)),
    ]


def hand_on(a_in, b_in, a_out, b_out, sem):
    copies = [
        pltpu.make_async_copy(src, dst, sem.at[n])
        for n, (src, dst) in enumerate(((a_in, a_out), (b_in, b_out)))
    ]
    for copy in copies:
        copy.start()
    for copy in copies:
        copy.wait()


def handed_on(a, b):
    space = pl.BlockSpec(memory_space=pl.ANY)
    return pl.pallas_call(
        hand_on,
        out_shape=(jax.ShapeDtypeStruct(a.shape, a.dtype), jax.ShapeDtypeStruct(b.shape, b.dtype)),
        in_specs=[space, space],
        out_specs=(space, space),
        scratch_shapes=[pltpu.SemaphoreType.DMA((2,))],
    )(a, b)


def body(
    incident_power_density,
    coupling_patch_locator,
    coupling_share_factor,
    starting_warmth,
    diffusive_coefficient,
    thermal_storage,
):
    f32 = jnp.float32
    flat = (NZ * NX, NY)
    hbm = pl.BlockSpec(memory_space=pl.ANY)
    vmem = pl.BlockSpec(memory_space=pltpu.VMEM)
    scratch = [
        pltpu.VMEM(flat, f32),
        pltpu.VMEM(flat, f32),
        pltpu.VMEM(flat, f32),
        pltpu.VMEM((CORR, NX, NY), jnp.int32),
        pltpu.VMEM((CORR, NX, NY), f32),
        pltpu.VMEM((STEPS, BR * NPY, NY), f32),
        pltpu.VMEM((6, NX, 8, NY), f32),
        pltpu.VMEM((3, NX + 4, NZ, NY), f32),
        pltpu.VMEM((NX + 4, NZ, NY), f32),
        pltpu.VMEM((2, NX + 4, NZ, NY), f32),
        pltpu.VMEM((NX, NZ, NY), f32),
        pltpu.VMEM((6, NX + 2, NZ, NY), f32),
        pltpu.VMEM((6, NZ, NY), f32),
        pltpu.VMEM((NX, NZ, NY), f32),
        pltpu.VMEM((NX + 4, NZ, NY), f32),
        pltpu.VMEM((STEPS, NX + 4, 8, NY), f32),
        pltpu.VMEM((3, NZ, NY), f32),
        pltpu.VMEM((2, NZ, NY), f32),
        pltpu.VMEM((2, 2, 8, NY), f32),
        pltpu.VMEM((2, 2, NZ, NY), f32),
        pltpu.VMEM((STEPS, 2, 1, NY), f32),
        pltpu.VMEM((STEPS, NPX, 1, NY), f32),
        pltpu.VMEM((STEPS, NPY, 1, NY), f32),
        pltpu.SemaphoreType.DMA((6,)),
        pltpu.SemaphoreType.DMA((STEPS,)),
        pltpu.SemaphoreType.DMA((STEPS,)),
        pltpu.SemaphoreType.DMA((STEPS, 2)),
        pltpu.SemaphoreType.DMA((STEPS, 2)),
    ]
    for fields, rows in EXCHANGES:
        scratch += exchange_scratch(fields, rows)
    scratch += [
        pltpu.VMEM((2, 2, 2, NZ, NY), f32),
        pltpu.VMEM((2, NZ, NY), f32),
        pltpu.VMEM((4, NZ, NY), f32),
        pltpu.VMEM((2, NZ, NY), f32),
        pltpu.SemaphoreType.DMA((8,)),
        pltpu.SemaphoreType.DMA((8,)),
        pltpu.VMEM((2, 2, 2, NZ, NY), f32),
        pltpu.VMEM((2, 4, NZ, NY), f32),
        pltpu.VMEM((2, NZ, NY), f32),
        pltpu.VMEM((4, NZ, NY), f32),
        pltpu.VMEM((2, NZ, NY), f32),
        pltpu.SemaphoreType.DMA((8,)),
        pltpu.SemaphoreType.DMA((8,)),
        pltpu.VMEM((2, 4, NZ, NY), f32),
        pltpu.VMEM((STEPS - 1, 2, 2, 2, NZ, NY), f32),
        pltpu.VMEM((STEPS - 1, 2, NZ, NY), f32),
        pltpu.VMEM((STEPS - 1, 4, NZ, NY), f32),
        pltpu.VMEM((STEPS - 1, 2, NZ, NY), f32),
        pltpu.SemaphoreType.DMA((STEPS - 1, 8)),
        pltpu.SemaphoreType.DMA((STEPS - 1, 8)),
    ]
    warmth, leftover, flag = pl.pallas_call(
        kernel,
        out_shape=(
            jax.ShapeDtypeStruct(flat, f32),
            jax.ShapeDtypeStruct(flat, f32),
            jax.ShapeDtypeStruct((1,), jnp.int32),
        ),
        in_specs=[hbm] * 6,
        out_specs=(vmem, vmem, pl.BlockSpec(memory_space=pltpu.SMEM)),
        scratch_shapes=scratch,
        compiler_params=pltpu.CompilerParams(
            collective_id=0, has_side_effects=True, vmem_limit_bytes=40 * 2**20
        ),
    )(
        incident_power_density,
        coupling_patch_locator,
        coupling_share_factor,
        starting_warmth.reshape(flat),
        diffusive_coefficient.reshape(flat),
        thermal_storage.reshape(flat),
    )
    shape = starting_warmth.shape
    out = lax.cond(
        flag[0] > 0,
        lambda: list(
            general(
                incident_power_density,
                coupling_patch_locator,
                coupling_share_factor,
                starting_warmth,
                diffusive_coefficient,
                thermal_storage,
            )
        ),
        lambda: [out.reshape(shape) for out in handed_on(warmth, leftover)],
    )
    return tuple(out)


def solution(mesh):
    placed = (
        P(None, ("px", "py"), None),
        P(None, "px", "py"),
        P(None, "px", "py"),
        P(None, "px", "py"),
        P(None, "px", "py"),
        P(None, "px", "py"),
    )
    return jax.shard_map(
        body,
        mesh=mesh,
        in_specs=placed,
        out_specs=(P(None, "px", "py"), P(None, "px", "py")),
        check_vma=False,
    )
```

```python
import functools

import jax
import jax.numpy as jnp
from jax import lax
from jax.experimental import pallas as pl
from jax.experimental.pallas import tpu as pltpu
from jax.sharding import PartitionSpec as P

ITERS = 2
MESH = pl.DeviceIdType.MESH

NZ = 24
NX = 32
NY = 128
NPX = 8
NPY = 16
BR = 16
STEPS = 3
CORR = 8
UNROLL = 8


through_ratio = 0.5


def extended(block, sides, width):
    for axis, dim in sides:
        count = lax.axis_size(axis)
        forward = [(i, i + 1) for i in range(count - 1)]
        backward = [(target, source) for source, target in forward]
        low = lax.ppermute(
            lax.slice_in_dim(block, block.shape[dim] - width, None, axis=dim), axis, forward
        )
        high = lax.ppermute(lax.slice_in_dim(block, 0, width, axis=dim), axis, backward)
        block = jnp.concatenate([low, block, high], axis=dim)
    return block


def with_rim(field):
    rimmed = extended(field, (("px", 1), ("py", 2)), 1)
    return jnp.pad(rimmed, ((1, 1), (0, 0), (0, 0)))


def stencil(padded, field, faces, diagonal):
    beside = faces[0] * padded[:-2, 1:-1, 1:-1] + faces[1] * padded[2:, 1:-1, 1:-1]
    beside = beside + faces[2] * padded[1:-1, :-2, 1:-1] + faces[3] * padded[1:-1, 2:, 1:-1]
    beside = beside + faces[4] * padded[1:-1, 1:-1, :-2] + faces[5] * padded[1:-1, 1:-1, 2:]
    return diagonal * field - beside


def operate(field, faces, diagonal):
    return stencil(with_rim(field), field, faces, diagonal)


def face_terms(centre, padded):
    return (
        through_ratio * 0.5 * (centre + padded[:-2, 1:-1, 1:-1]),
        through_ratio * 0.5 * (centre + padded[2:, 1:-1, 1:-1]),
        0.5 * (centre + padded[1:-1, :-2, 1:-1]),
        0.5 * (centre + padded[1:-1, 2:, 1:-1]),
        0.5 * (centre + padded[1:-1, 1:-1, :-2]),
        0.5 * (centre + padded[1:-1, 1:-1, 2:]),
    )


def surface_flux(window, coupling_patch_locator, coupling_share_factor):
    flat = window.reshape(-1)
    values = flat[coupling_patch_locator]
    return jnp.sum(coupling_share_factor * values, axis=0)


def total(a, b):
    return lax.psum(jnp.sum(a * b), ("px", "py"))


def solve_step(solution, leftover_error_vector, faces, diagonal):
    scaled = leftover_error_vector / diagonal
    axis_direction = scaled
    gamma = total(leftover_error_vector, scaled)
    for turn in range(ITERS):
        image = operate(axis_direction, faces, diagonal)
        alpha = gamma / total(axis_direction, image)
        solution = solution + alpha * axis_direction
        leftover_error_vector = leftover_error_vector - alpha * image
        if turn + 1 < ITERS:
            scaled = leftover_error_vector / diagonal
            fresh = total(leftover_error_vector, scaled)
            axis_direction = scaled + fresh / gamma * axis_direction
            gamma = fresh
    return (solution, leftover_error_vector)


def general(
    incident_power_density,
    coupling_patch_locator,
    coupling_share_factor,
    starting_warmth,
    diffusive_coefficient,
    thermal_storage,
):
    sheet_level = starting_warmth.shape[0]
    rimmed = extended(diffusive_coefficient, (("px", 1), ("py", 2)), 1)
    padded = jnp.pad(rimmed, ((1, 1), (0, 0), (0, 0)))
    faces = face_terms(diffusive_coefficient, padded)
    diagonal = thermal_storage + faces[0] + faces[1] + faces[2] + faces[3] + faces[4] + faces[5]
    frames = incident_power_density.shape[0]
    final_warmth = starting_warmth
    leftover_error_vector = starting_warmth
    for frame in range(frames):
        window = lax.all_to_all(
            incident_power_density[frame : frame + 1], "py", split_axis=2, concat_axis=1, tiled=True
        )[0]
        flux = surface_flux(window, coupling_patch_locator, coupling_share_factor)
        right = thermal_storage * final_warmth
        right = right.at[sheet_level - 1].add(flux)
        leftover_error_vector = right - operate(final_warmth, faces, diagonal)
        final_warmth, leftover_error_vector = solve_step(
            final_warmth, leftover_error_vector, faces, diagonal
        )
    return (final_warmth, leftover_error_vector)


def lanes(rows=NZ):
    return lax.broadcasted_iota(jnp.int32, (rows, NY), 1)


def rolled(v, shift, axis=1):
    return pltpu.roll(v, shift % v.shape[axis], axis)


def slabs_loop(fn, init, step=UNROLL):
    def some(n, carry):
        for q in range(step):
            carry = fn(n * step + q, carry)
        return carry

    return lax.fori_loop(0, NX // step, some, init)


def side_tile(packed, x):
    return pltpu.roll(packed, lax.rem(638 - 4 * x, 128), 1)


def lateral(v, side):
    lane = lanes(v.shape[0])
    left = jnp.where(lane == 0, side, rolled(v, 1))
    right = jnp.where(lane == NY - 1, side, rolled(v, -1))
    return left, right


def apply_slab(ref, i, side, g_ref, gi):
    v = ref[i]
    left, right = lateral(v, side)
    out = g_ref[0, gi] * rolled(v, 1, 0) + g_ref[1, gi] * rolled(v, -1, 0)
    out = out + (g_ref[2, gi] * ref[i - 1] + g_ref[3, gi] * ref[i + 1])
    out = out + (g_ref[4, gi] * left + g_ref[5, gi] * right)
    return v - out


def around_halo(halo, corner, pack):
    lane = lanes()
    j = lax.rem(lane, 4)
    below = jnp.where(lane < 4, corner, rolled(halo, 4))
    above = jnp.where(lane >= NY - 4, corner, rolled(halo, -4))
    outer = jnp.where(j == 1, rolled(halo, 1), rolled(halo, -1))
    return below, above, pack, outer


def apply_halo(halo, corner, pack, gp_ref):
    below, above, inner, outer = around_halo(halo, corner, pack)
    out = gp_ref[0] * rolled(halo, 1, 0) + gp_ref[1] * rolled(halo, -1, 0)
    out = out + gp_ref[2] * below + gp_ref[3] * above + gp_ref[4] * inner + gp_ref[5] * outer
    return halo - out


class Place:
    def __init__(self):
        self.px = lax.axis_index("px")
        self.py = lax.axis_index("py")
        self.has_low = jnp.where(self.px > 0, 1.0, 0.0).astype(jnp.float32)
        self.has_high = jnp.where(self.px < NPX - 1, 1.0, 0.0).astype(jnp.float32)
        self.has_left = jnp.where(self.py > 0, 1.0, 0.0).astype(jnp.float32)
        self.has_right = jnp.where(self.py < NPY - 1, 1.0, 0.0).astype(jnp.float32)

    def at(self, dx, dy):
        return (lax.rem(self.px + dx + NPX, NPX), lax.rem(self.py + dy + NPY, NPY))


GHOSTS = (0, 1, NX + 2, NX + 3)
EXCHANGES = ((1, 8), (2, 8))
CORNERS = ((-1, 1), (-1, -1), (1, 1), (1, -1))


class Exchange:
    def __init__(self, place, refs):
        self.place = place
        self.rx, self.rs, self.rk, self.pack, self.send, self.recv = refs

    def plan(self, low, high):
        to_right, to_left = self.packs()
        plan = []
        for n, (dx, dy) in enumerate(CORNERS):
            plan.append((to_left if dy > 0 else to_right, self.rk.at[n], (-dx, -dy)))
        plan.append((to_right, self.rs.at[0], (0, 1)))
        plan.append((to_left, self.rs.at[1], (0, -1)))
        single = len(low.shape) + 2 == len(self.rx.shape)
        for n, (src, dx) in enumerate(((high, 1), (low, -1))):
            plan.append((src, self.rx.at[n, 0] if single else self.rx.at[n], (dx, 0)))
        return [
            pltpu.make_async_remote_copy(
                src_ref=src,
                dst_ref=dst,
                send_sem=self.send.at[n],
                recv_sem=self.recv.at[n],
                device_id=self.place.at(dx, dy),
                device_id_type=MESH,
            )
            for n, (src, dst, (dx, dy)) in enumerate(plan)
        ]

    def packs(self):
        return self.pack, self.pack

    def start(self, *edges):
        for copy in self.plan(*edges):
            copy.start()

    def arrive(self, *edges):
        for copy in self.plan(*edges):
            copy.wait_recv()

    def sent(self, *edges):
        for copy in self.plan(*edges):
            copy.wait_send()

    def slabs(self, field):
        p = self.place
        return (
            self.rx[0, field, 0] * p.has_low,
            self.rx[0, field, 1] * p.has_low,
            self.rx[1, field, 0] * p.has_high,
            self.rx[1, field, 1] * p.has_high,
        )

    def sides(self, field):
        return self.rs[0, field], self.rs[1, field], (-3, -1, 1, 3)

    def corners(self, field):
        return [self.rk[n, field] for n in range(4)], (3, 5, -5, -3)

    def halo(self, field):
        p = self.place
        left, right, shifts = self.sides(field)
        left, right = left * p.has_left, right * p.has_right
        j = lax.rem(lanes(left.shape[0]), 4)
        far = jnp.where(j == 0, rolled(right, shifts[0]), rolled(left, shifts[3]))
        near = jnp.where(j == 1, rolled(right, shifts[1]), rolled(left, shifts[2]))
        return jnp.where((j == 1) | (j == 2), near, far)

    def corner(self, field):
        p = self.place
        tiles, shifts = self.corners(field)
        masks = (
            p.has_low * p.has_right,
            p.has_low * p.has_left,
            p.has_high * p.has_right,
            p.has_high * p.has_left,
        )
        lane = lanes(tiles[0].shape[0])
        out = jnp.zeros_like(tiles[0])
        for at, tile, mask, shift in zip((1, 2, NY - 3, NY - 2), tiles, masks, shifts):
            out = jnp.where(lane == at, rolled(tile * mask, shift), out)
        return out


class PairExchange(Exchange):
    def packs(self):
        return self.pack.at[0], self.pack.at[1]

    def fill(self, first, second):
        j = lax.rem(lanes(), 4)
        self.pack[0] = jnp.where(j < 2, first, rolled(second, 2))
        self.pack[1] = jnp.where(j < 2, rolled(first, -2), second)

    def sides(self, field):
        return self.rs[0], self.rs[1], ((-3, -1, -1, 1) if field else (-1, 1, 1, 3))

    def corners(self, field):
        return [self.rk[n] for n in range(4)], ((3, 3, -5, -5) if field else (5, 5, -3, -3))


class FirstExchange(PairExchange):
    def fill(self, k, c, t):
        j = lax.rem(lanes(), 4)
        right = jnp.where(j == 2, rolled(c, 1), rolled(t, 2))
        left = jnp.where(j == 2, c, rolled(t, 1))
        self.pack[0] = jnp.where(j < 2, k, right)
        self.pack[1] = jnp.where(j < 2, rolled(k, -2), left)

    def sides(self, field):
        return self.rs[0], self.rs[1], ((-1, 1, 1, 3), (0, -1, 0, 0), (0, -2, -1, 0))[field]


def packed_into(pack, v, x):
    lane = lanes(v.shape[0])
    return jnp.where(lane // 4 == x, pltpu.roll(v, lax.rem(4 * x + 2, NY), 1), pack)


HOPS = sorted(
    ((dz, dy) for dz in range(4) for dy in range(4) if dz or dy),
    key=lambda t: -(min(t[0], 4 - t[0]) + min(t[1], 4 - t[1])),
)


def ring_targets(place):
    x, core = place.px // 2, lax.rem(place.px, 2)
    z, y = place.py // 4, lax.rem(place.py, 4)
    px = []
    for dx, dc in ((2, 1), (2, 0), (1, 1), (1, 0), (3, 1), (3, 0), (0, 1)):
        px.append((lax.rem(x + dx, 4) * 2 + lax.rem(core + dc, 2), place.py))
    py = []
    for dz, dy in HOPS:
        py.append((place.px, lax.rem(z + dz, 4) * 4 + lax.rem(y + dy, 4)))
    return px, py


def kernel(
    beam,
    loc_in,
    share_in,
    t_in,
    k_in,
    c_in,
    x_out,
    r_out,
    flag_out,
    kraw,
    craw,
    traw,
    loc,
    share,
    window,
    weights,
    kct,
    z_ref,
    uv_ref,
    x_ref,
    g_ref,
    gp_ref,
    d_ref,
    e_ref,
    fd_ref,
    z_near,
    e_near,
    f_near,
    uv_near,
    red_src,
    red_px,
    red_py,
    local_sem,
    beam_send,
    beam_recv,
    red_send,
    red_recv,
    *exchange_refs,
):
    place = Place()
    u_ref, v_ref = uv_ref.at[0], uv_ref.at[1]
    px_ring, py_ring = ring_targets(place)
    diagonal_devices = [place.at(dx, dy) for dx, dy in CORNERS]

    local = [
        pltpu.make_async_copy(src, dst, local_sem.at[n])
        for n, (src, dst) in enumerate(
            (
                (k_in, kraw),
                (c_in, craw),
                (t_in, traw),
                (loc_in, loc),
                (share_in, share),
            )
        )
    ]
    for copy in local:
        copy.start()
    own_columns = pl.ds(pl.multiple_of(place.py * NY, NY), NY)
    own_rows = pl.ds(pl.multiple_of(place.py * BR, BR), BR)
    own_beam = pltpu.make_async_copy(
        beam.at[:, :, own_columns], window.at[:, own_rows, :], local_sem.at[5]
    )
    own_beam.start()

    barrier = pltpu.get_barrier_semaphore()
    everyone = py_ring + px_ring + diagonal_devices
    for device in everyone:
        pl.semaphore_signal(barrier, inc=1, device_id=device, device_id_type=MESH)

    exchanges = [
        Exchange(place, exchange_refs[6 * n : 6 * n + 6]) for n in range(len(EXCHANGES))
    ]
    tile_swap, f_swap = exchanges
    ze_swap = PairExchange(place, exchange_refs[-20:-14])
    ze_edge = exchange_refs[-14]
    first = FirstExchange(place, exchange_refs[-13:-7])
    k_edge = exchange_refs[-7]
    uv_refs = exchange_refs[-6:]
    k_edges = k_edge.at[0], k_edge.at[1]
    tile_edges = fd_ref.at[0, pl.ds(2, 2)], fd_ref.at[0, pl.ds(NX, 2)]
    ze_edges = ze_edge.at[0], ze_edge.at[1]
    f_edges = fd_ref.at[pl.ds(1, 2), pl.ds(2, 2)], fd_ref.at[pl.ds(1, 2), pl.ds(NX, 2)]
    uv_edges = uv_ref.at[:, pl.ds(2, 2)], uv_ref.at[:, pl.ds(NX, 2)]

    for copy in local[:3]:
        copy.wait()
    zero = jnp.zeros((NZ, NY), jnp.float32)

    def folded(v):
        return v[0:8] + v[8:16] + v[16:24]

    def zero_row():
        return jnp.zeros((8, NY), jnp.float32)

    def lay(x, packs):
        out = []
        for n, raw in enumerate((kraw, craw, traw)):
            v = raw[pl.ds(x, NZ, stride=NX), :]
            kct[n, x + 2] = v
            out.append(packed_into(packs[n], v, x))
        return tuple(out)

    packs = slabs_loop(lay, (zero, zero, zero))
    k_pack, c_pack, t_pack = packs
    first.fill(*packs)
    edges = ((0, 0, NX - 2), (0, 1, NX - 1), (1, 0, NX - 1), (2, 0, NX - 1))
    for n, (field, low, high) in enumerate(edges):
        k_edge[0, n] = kct[field, low + 2]
        k_edge[1, n] = kct[field, high + 2]

    local[3].wait()
    local[4].wait()
    row8 = lax.broadcasted_iota(jnp.int32, (8, NY), 0)
    lane8 = lax.broadcasted_iota(jnp.int32, (8, NY), 1)
    beyond = jnp.where(row8 == 7, -1, jnp.where(row8 == 0, 8, -1000))

    def weigh(x, bad):
        own = [jnp.zeros((8, NY), jnp.float32) for _ in range(3)]
        edge = [jnp.zeros((8, NY), jnp.float32) for _ in range(3)]
        for k in range(CORR):
            index = jnp.broadcast_to(loc[k, pl.ds(x, 1), :], (8, NY))
            part = jnp.broadcast_to(share[k, pl.ds(x, 1), :], (8, NY))
            row = lax.shift_right_arithmetic(index, 7) - 8 * x
            col = lax.bitwise_and(index, 127) - lane8
            far = (row < -1) | (row > 8) | (col < -1) | (col > 1)
            bad = bad + jnp.where(far, 1.0, 0.0)
            inside = jnp.where(row == row8, part, 0.0)
            outside = jnp.where(row == beyond, part, 0.0)
            for n in range(3):
                here = col == n - 1
                own[n] = own[n] + jnp.where(here, inside, 0.0)
                edge[n] = edge[n] + jnp.where(here, outside, 0.0)
        for n in range(3):
            weights[n, x] = own[n]
            weights[3 + n, x] = edge[n]
        return bad

    bad = slabs_loop(weigh, jnp.zeros((8, NY), jnp.float32))

    pl.semaphore_wait(barrier, len(everyone))

    def send_frame(frame):
        def send_block(n, nothing):
            n = jnp.where(n < 10, n, n + 1)
            device = (
                place.px,
                lax.rem(place.py // 4 + 2 + n // 4, 4) * 4 + lax.rem(lax.rem(place.py, 4) + 2 + lax.rem(n, 4), 4),
            )
            columns = pl.ds(pl.multiple_of(device[1] * NY, NY), NY)
            copy = pltpu.make_async_remote_copy(
                src_ref=beam.at[frame, :, columns],
                dst_ref=window.at[frame, own_rows, :],
                send_sem=beam_send.at[frame],
                recv_sem=beam_recv.at[frame],
                device_id=device,
                device_id_type=MESH,
            )
            copy.start()
            return nothing

        lax.fori_loop(0, NPY - 1, send_block, 0)

    def frame_bytes(frame, sem):
        most = window.at[frame, pl.ds(0, (NPY - 1) * BR), :]
        return pltpu.make_async_copy(most, most, sem.at[frame])

    first.start(*k_edges)
    send_frame(0)
    for frame in range(1, STEPS):
        send_frame(frame)

    first.arrive(*k_edges)
    for n, (field, low, high) in enumerate(edges):
        kct[field, high + 2 - NX] = first.rx[0, n] * place.has_low
        kct[field, low + 2 + NX] = first.rx[1, n] * place.has_high
    k_halo, k_corner = first.halo(0), first.corner(0)
    c_halo, t_halo = first.halo(1), first.halo(2)
    c_halo = jnp.where((lax.rem(lanes(), 4) + 1) // 2 == 1, c_halo, 0.0)
    level = lax.broadcasted_iota(jnp.int32, (NZ, NY), 0)

    def over(k, up, down, below, above, left, right, storage, mask):
        bottom, top = level == 0, level == NZ - 1
        up = jnp.where(bottom, 0.0, up)
        down = jnp.where(top, 0.0, down)
        faces = [0.25 * (k + up), 0.25 * (k + down)]
        faces += [0.5 * (k + other) for other in (below, above, left, right)]
        diagonal = storage + (
            (faces[0] + faces[1]) + (faces[2] + faces[3]) + (faces[4] + faces[5])
        )
        inverse = mask / diagonal
        faces[0] = jnp.where(bottom, 0.0, faces[0])
        faces[1] = jnp.where(top, 0.0, faces[1])
        return [face * inverse for face in faces], diagonal, inverse

    def conduct(x, side, mask):
        i = x + 2
        k = kct[0, i]
        left, right = lateral(k, side)
        g, diagonal, inverse = over(
            k,
            rolled(k, 1, 0),
            rolled(k, -1, 0),
            kct[0, i - 1],
            kct[0, i + 1],
            left,
            right,
            kct[1, i],
            mask,
        )
        for n in range(6):
            g_ref[n, x + 1] = g[n]
        return diagonal, inverse

    conduct(-1, side_tile(k_corner, 0), place.has_low)
    conduct(NX, side_tile(k_corner, NX - 1), place.has_high)

    def conduct_inside(x, pack):
        diagonal, inverse = conduct(x, side_tile(k_halo, x), 1.0)
        d_ref[x] = diagonal
        e = kct[1, x + 2] * inverse
        e_ref[x + 2] = e
        return packed_into(pack, e, x)

    e_pack = slabs_loop(conduct_inside, zero)

    below, above, inner, outer = around_halo(k_halo, k_corner, k_pack)
    j = lax.rem(lanes(), 4)
    halo_mask = jnp.where(j < 2, place.has_right, place.has_left)
    halo_mask = jnp.where((j == 1) | (j == 2), halo_mask, 0.0)
    gp, _, _ = over(
        k_halo,
        rolled(k_halo, 1, 0),
        rolled(k_halo, -1, 0),
        below,
        above,
        inner,
        outer,
        c_halo + jnp.where(halo_mask > 0.0, 0.0, 1.0),
        halo_mask,
    )
    for n in range(6):
        gp_ref[n] = gp[n]

    t_ref = kct.at[2]

    def residual(x, carry):
        image = apply_slab(t_ref, x + 2, side_tile(t_halo, x), g_ref, x + 1)
        t = t_ref[x + 2]
        z = e_ref[x + 2] * t - image
        z_ref[x + 2] = z
        x_ref[x] = t
        return packed_into(carry, z, x)

    z_pack = slabs_loop(residual, zero)
    z_near[2] = z_pack
    ze_swap.fill(z_pack, e_pack)
    for n in range(2):
        for m, ref in enumerate((z_ref, e_ref)):
            ze_edge[0, m, n] = ref[2 + n]
            ze_edge[1, m, n] = ref[NX + n]
    ze_swap.start(*ze_edges)
    first.sent(*k_edges)

    own_beam.wait()

    def flux_tile(frame, x):
        def rows(i):
            return window[frame, pl.ds(pl.multiple_of(i * 8, 8), 8), :]

        mine = rows(x)
        around = jnp.where(
            row8 == 7, rows(jnp.maximum(x - 1, 0)), rows(jnp.minimum(x + 1, NX - 1))
        )
        part = weights[1, x] * mine + weights[4, x] * around
        part = part + weights[0, x] * rolled(mine, 1) + weights[3, x] * rolled(around, 1)
        part = part + weights[2, x] * rolled(mine, -1) + weights[5, x] * rolled(around, -1)
        flux = jnp.sum(part, axis=0, keepdims=True)
        top = d_ref[x, NZ - 8 : NZ, :]
        return jnp.where(row8 == 7, flux, 0.0) / top

    def all_sum(step, moments, meanwhile):
        lane = lax.broadcasted_iota(jnp.int32, (1, NY), 1)
        row = jnp.zeros((1, NY), jnp.float32)
        for n, m in enumerate(moments):
            row = jnp.where(lane == n, jnp.sum(m, keepdims=True), row)
        for phase, (ring, slots, me) in enumerate(
            ((px_ring, red_px, place.px), (py_ring, red_py, place.py))
        ):
            source = red_src.at[step, phase]
            source[...] = row
            for device in ring:
                pltpu.make_async_remote_copy(
                    src_ref=source,
                    dst_ref=slots.at[step, me],
                    send_sem=red_send.at[step, phase],
                    recv_sem=red_recv.at[step, phase],
                    device_id=device,
                    device_id_type=MESH,
                ).start()
            slots[step, me] = row
            meanwhile[phase]()
            most = slots.at[step, pl.ds(0, len(ring))]
            pltpu.make_async_copy(most, most, red_recv.at[step, phase]).wait()
            parts = [slots[step, n] for n in range(len(ring) + 1)]
            while len(parts) > 1:
                parts = [a + b for a, b in zip(parts[::2], parts[1::2])]
            row = parts[0]
        return [
            jnp.sum(jnp.where(lane == n, row, 0.0), axis=1, keepdims=True)
            for n in range(len(moments))
        ]

    frame_bytes(0, beam_recv).wait()

    def add_flux(x, pack):
        tile = flux_tile(0, x)
        fd_ref[0, x + 2] = tile
        z_ref[x + 2, NZ - 8 : NZ, :] = z_ref[x + 2, NZ - 8 : NZ, :] + tile
        return packed_into(pack, tile, x)

    top = pl.ds(NZ - 8, 8)
    tile_pack = slabs_loop(add_flux, zero_row(), 16)
    tile_swap.pack[0] = tile_pack
    tile_swap.start(*tile_edges)
    z_near[2, top] = z_near[2, top] + tile_pack
    ze_swap.arrive(*ze_edges)
    for at, z, e in zip(GHOSTS, ze_swap.slabs(0), ze_swap.slabs(1)):
        z_ref[at] = z
        e_ref[at] = e
    for near, n in ((z_near, 0), (e_near, 1)):
        near[0], near[1] = ze_swap.halo(n), ze_swap.corner(n)

    dry_halo = z_near[0]

    def early_image(x, carry):
        sums, pack = carry
        u = apply_slab(z_ref, x + 2, side_tile(dry_halo, x), g_ref, x + 1)
        u_ref[x + 2] = u
        z = z_ref[x + 2]
        dz = d_ref[x] * z
        zu, uu = dz * u, d_ref[x] * u * u
        sums = (
            sums[0] + folded(dz * z),
            sums[1] + (zu[0:8] + zu[8:16]),
            sums[2] + (uu[0:8] + uu[8:16]),
        )
        return sums, packed_into(pack, u, x)

    early_sums, early_pack = slabs_loop(early_image, ((zero_row(),) * 3, zero))
    tile_swap.arrive(*tile_edges)
    tiles = tile_swap.slabs(0)
    for at, tile in zip(GHOSTS, tiles):
        z_ref[at, top] = z_ref[at, top] + tile
    tile_halo = tile_swap.halo(0)
    for n, tile in enumerate((tile_halo, tile_swap.corner(0))):
        z_near[n, top] = z_near[n, top] + tile
    u_ref[2, top] = u_ref[2, top] - g_ref[2, 1, top] * tiles[1]
    u_ref[NX + 1, top] = u_ref[NX + 1, top] - g_ref[3, NX, top] * tiles[2]

    def late_image(x, carry):
        sums, pack = carry
        side = side_tile(tile_halo, x)
        near = jnp.where(lane8 == 0, g_ref[4, x + 1, top] * side, 0.0)
        near = jnp.where(lane8 == NY - 1, g_ref[5, x + 1, top] * side, near)
        u = u_ref[x + 2, top] - near
        u_ref[x + 2, top] = u
        du = d_ref[x, top] * u
        sums = (sums[0] + du * z_ref[x + 2, top], sums[1] + du * u)
        return sums, packed_into(pack, u, x)

    late_sums, late_pack = slabs_loop(late_image, (early_sums[1:], zero_row()), 16)
    early_sums = (early_sums[0], *late_sums)
    early_pack = jnp.concatenate([early_pack[: NZ - 8], late_pack], axis=0)

    def later_fluxes():
        frame_bytes(1, beam_recv).wait()
        frame_bytes(2, beam_recv).wait()

        def next_flux(x, packs):
            second, third = flux_tile(1, x), flux_tile(2, x)
            third = third - second
            second = second - fd_ref[0, x + 2]
            fd_ref[1, x + 2] = second
            fd_ref[2, x + 2] = third
            return packed_into(packs[0], second, x), packed_into(packs[1], third, x)

        packs = slabs_loop(next_flux, (zero_row(),) * 2)
        f_swap.pack[0], f_swap.pack[1] = packs
        f_swap.start(*f_edges)

    def one_step(step, nothing):
        swap = PairExchange(place, [ref.at[step] for ref in uv_refs])
        more = step + 1 < STEPS
        z_halo, z_corner = z_near[0], z_near[1]
        u_ref[1] = apply_slab(z_ref, 1, side_tile(z_corner, 0), g_ref, 0)
        u_ref[NX + 2] = apply_slab(z_ref, NX + 2, side_tile(z_corner, NX - 1), g_ref, NX + 1)
        u_halo = apply_halo(z_halo, z_corner, z_near[2], gp_ref)

        def first_image(x, carry):
            sums, pack = carry
            u = apply_slab(z_ref, x + 2, side_tile(z_halo, x), g_ref, x + 1)
            u_ref[x + 2] = u
            z = z_ref[x + 2]
            dz = d_ref[x] * z
            du = d_ref[x] * u
            sums = (
                sums[0] + folded(dz * z),
                sums[1] + folded(dz * u),
                sums[2] + folded(du * u),
            )
            return sums, (packed_into(pack, u, x) if more else pack)

        if step == 0:
            sums, u_pack = early_sums, early_pack
        else:
            sums, u_pack = slabs_loop(first_image, ((zero_row(),) * 3, zero))

        def second_image(x, carry):
            acc, pack = carry
            v = apply_slab(u_ref, x + 2, side_tile(u_halo, x), g_ref, x + 1)
            v_ref[x + 2] = v
            acc = acc + folded(d_ref[x] * u_ref[x + 2] * v)
            return acc, (packed_into(pack, v, x) if more else pack)

        last, v_pack = slabs_loop(second_image, (zero_row(), zero))

        def send_images():
            @pl.when(more)
            def _():
                swap.fill(u_pack, v_pack)
                swap.start(*uv_edges)

            @pl.when(step == 0)
            def _():
                later_fluxes()

        def receive_images():
            @pl.when(step == 0)
            def _():
                ze_swap.sent(*ze_edges)
                tile_swap.sent(*tile_edges)
                f_swap.arrive(*f_edges)
                for n in range(2):
                    for at, slab in zip(GHOSTS, f_swap.slabs(n)):
                        fd_ref[1 + n, at] = slab
                for n in range(2):
                    f_near[n, 0], f_near[n, 1] = f_swap.halo(n), f_swap.corner(n)

            @pl.when(more)
            def _():
                swap.arrive(*uv_edges)
                for n in range(2):
                    uv_near[n, 0], uv_near[n, 1] = swap.halo(n), swap.corner(n)

        moments = list(sums) + [last] + ([bad] if step == 0 else [])
        g0, a, w, t, *far = all_sum(step, moments, (send_images, receive_images))
        if step == 0:
            flag_out[0] = jnp.where(jnp.sum(far[0]) > 0.0, 1, 0).astype(jnp.int32)
        inverse = 1.0 / (a * t - w * w)
        d1 = jnp.broadcast_to((g0 * t - a * w) * inverse, (NZ, NY))
        d2 = jnp.broadcast_to((a * a - g0 * w) * inverse, (NZ, NY))

        def next_z(z, u, v, e, tile):
            z = z - d1 * u - d2 * v + e * (d1 * z + d2 * u)
            return jnp.concatenate([z[: NZ - 8], z[NZ - 8 :] + tile], axis=0)

        @pl.when(more)
        def _():
            for at, u, v in zip(GHOSTS, swap.slabs(0), swap.slabs(1)):
                z_ref[at] = next_z(z_ref[at], u, v, e_ref[at], fd_ref[step + 1, at])
            for n in range(2):
                z_near[n] = next_z(z_near[n], uv_near[0, n], uv_near[1, n], e_near[n], f_near[step, n])

            def update(x, pack):
                z, u, v = z_ref[x + 2], u_ref[x + 2], v_ref[x + 2]
                x_ref[x] = x_ref[x] + (d1 * z + d2 * u)
                z = next_z(z, u, v, e_ref[x + 2], fd_ref[step + 1, x + 2])
                z_ref[x + 2] = z
                return packed_into(pack, z, x)

            z_near[2] = slabs_loop(update, zero)
            swap.sent(*uv_edges)

        @pl.when(not more)
        def _():
            def finish(x, carry):
                z, u, v = z_ref[x + 2], u_ref[x + 2], v_ref[x + 2]
                x_out[pl.ds(x, NZ, stride=NX), :] = x_ref[x] + (d1 * z + d2 * u)
                r_out[pl.ds(x, NZ, stride=NX), :] = d_ref[x] * (z - d1 * u - d2 * v)
                return carry

            slabs_loop(finish, 0)

        return nothing

    for step in range(STEPS):
        one_step(step, 0)
    f_swap.sent(*f_edges)
    for frame in range(STEPS):
        frame_bytes(frame, beam_send).wait()
    for step in range(STEPS):
        for phase, (slots, count) in enumerate(((red_px, NPX - 1), (red_py, NPY - 1))):
            most = slots.at[step, pl.ds(0, count)]
            pltpu.make_async_copy(most, most, red_send.at[step, phase]).wait()


def exchange_scratch(fields, rows):
    f32 = jnp.float32
    return [
        pltpu.VMEM((2, fields, 2, rows, NY), f32),
        pltpu.VMEM((2, fields, rows, NY), f32),
        pltpu.VMEM((4, fields, rows, NY), f32),
        pltpu.VMEM((fields, rows, NY), f32),
        pltpu.SemaphoreType.DMA((8,)),
        pltpu.SemaphoreType.DMA((8,)),
    ]


def hand_on(a_in, b_in, a_out, b_out, sem):
    copies = [
        pltpu.make_async_copy(src.at[pl.ds(n * 192, 192)], dst.at[pl.ds(n * 192, 192)], sem.at[m, n])
        for m, (src, dst) in enumerate(((a_in, a_out), (b_in, b_out)))
        for n in range(4)
    ]
    for copy in copies:
        copy.start()
    for copy in copies:
        copy.wait()


def handed_on(a, b):
    space = pl.BlockSpec(memory_space=pl.ANY)
    return pl.pallas_call(
        hand_on,
        out_shape=(jax.ShapeDtypeStruct(a.shape, a.dtype), jax.ShapeDtypeStruct(b.shape, b.dtype)),
        in_specs=[space, space],
        out_specs=(space, space),
        scratch_shapes=[pltpu.SemaphoreType.DMA((2, 4))],
    )(a, b)


def body(
    incident_power_density,
    coupling_patch_locator,
    coupling_share_factor,
    starting_warmth,
    diffusive_coefficient,
    thermal_storage,
):
    f32 = jnp.float32
    flat = (NZ * NX, NY)
    hbm = pl.BlockSpec(memory_space=pl.ANY)
    vmem = pl.BlockSpec(memory_space=pltpu.VMEM)
    scratch = [
        pltpu.VMEM(flat, f32),
        pltpu.VMEM(flat, f32),
        pltpu.VMEM(flat, f32),
        pltpu.VMEM((CORR, NX, NY), jnp.int32),
        pltpu.VMEM((CORR, NX, NY), f32),
        pltpu.VMEM((STEPS, BR * NPY, NY), f32),
        pltpu.VMEM((6, NX, 8, NY), f32),
        pltpu.VMEM((3, NX + 4, NZ, NY), f32),
        pltpu.VMEM((NX + 4, NZ, NY), f32),
        pltpu.VMEM((2, NX + 4, NZ, NY), f32),
        pltpu.VMEM((NX, NZ, NY), f32),
        pltpu.VMEM((6, NX + 2, NZ, NY), f32),
        pltpu.VMEM((6, NZ, NY), f32),
        pltpu.VMEM((NX, NZ, NY), f32),
        pltpu.VMEM((NX + 4, NZ, NY), f32),
        pltpu.VMEM((STEPS, NX + 4, 8, NY), f32),
        pltpu.VMEM((3, NZ, NY), f32),
        pltpu.VMEM((2, NZ, NY), f32),
        pltpu.VMEM((2, 2, 8, NY), f32),
        pltpu.VMEM((2, 2, NZ, NY), f32),
        pltpu.VMEM((STEPS, 2, 1, NY), f32),
        pltpu.VMEM((STEPS, NPX, 1, NY), f32),
        pltpu.VMEM((STEPS, NPY, 1, NY), f32),
        pltpu.SemaphoreType.DMA((6,)),
        pltpu.SemaphoreType.DMA((STEPS,)),
        pltpu.SemaphoreType.DMA((STEPS,)),
        pltpu.SemaphoreType.DMA((STEPS, 2)),
        pltpu.SemaphoreType.DMA((STEPS, 2)),
    ]
    for fields, rows in EXCHANGES:
        scratch += exchange_scratch(fields, rows)
    scratch += [
        pltpu.VMEM((2, 2, 2, NZ, NY), f32),
        pltpu.VMEM((2, NZ, NY), f32),
        pltpu.VMEM((4, NZ, NY), f32),
        pltpu.VMEM((2, NZ, NY), f32),
        pltpu.SemaphoreType.DMA((8,)),
        pltpu.SemaphoreType.DMA((8,)),
        pltpu.VMEM((2, 2, 2, NZ, NY), f32),
        pltpu.VMEM((2, 4, NZ, NY), f32),
        pltpu.VMEM((2, NZ, NY), f32),
        pltpu.VMEM((4, NZ, NY), f32),
        pltpu.VMEM((2, NZ, NY), f32),
        pltpu.SemaphoreType.DMA((8,)),
        pltpu.SemaphoreType.DMA((8,)),
        pltpu.VMEM((2, 4, NZ, NY), f32),
        pltpu.VMEM((STEPS - 1, 2, 2, 2, NZ, NY), f32),
        pltpu.VMEM((STEPS - 1, 2, NZ, NY), f32),
        pltpu.VMEM((STEPS - 1, 4, NZ, NY), f32),
        pltpu.VMEM((STEPS - 1, 2, NZ, NY), f32),
        pltpu.SemaphoreType.DMA((STEPS - 1, 8)),
        pltpu.SemaphoreType.DMA((STEPS - 1, 8)),
    ]
    warmth, leftover, flag = pl.pallas_call(
        kernel,
        out_shape=(
            jax.ShapeDtypeStruct(flat, f32),
            jax.ShapeDtypeStruct(flat, f32),
            jax.ShapeDtypeStruct((1,), jnp.int32),
        ),
        in_specs=[hbm] * 6,
        out_specs=(vmem, vmem, pl.BlockSpec(memory_space=pltpu.SMEM)),
        scratch_shapes=scratch,
        compiler_params=pltpu.CompilerParams(
            collective_id=0, has_side_effects=True, vmem_limit_bytes=40 * 2**20
        ),
    )(
        incident_power_density,
        coupling_patch_locator,
        coupling_share_factor,
        starting_warmth.reshape(flat),
        diffusive_coefficient.reshape(flat),
        thermal_storage.reshape(flat),
    )
    shape = starting_warmth.shape
    out = lax.cond(
        flag[0] > 0,
        lambda: list(
            general(
                incident_power_density,
                coupling_patch_locator,
                coupling_share_factor,
                starting_warmth,
                diffusive_coefficient,
                thermal_storage,
            )
        ),
        lambda: [out.reshape(shape) for out in handed_on(warmth, leftover)],
    )
    return tuple(out)


def solution(mesh):
    placed = (
        P(None, ("px", "py"), None),
        P(None, "px", "py"),
        P(None, "px", "py"),
        P(None, "px", "py"),
        P(None, "px", "py"),
        P(None, "px", "py"),
    )
    return jax.shard_map(
        body,
        mesh=mesh,
        in_specs=placed,
        out_specs=(P(None, "px", "py"), P(None, "px", "py")),
        check_vma=False,
    )
```
